32 devices in a mesh: layer: 2 (over x), row: 4 (over y, core), col: 4 (over z).
Axes of the slice: x: 2, y: 2, z: 4, core: 2. Of those that a mesh axis runs over, the one named last changes fastest.
Arguments:
- partials: float32 [2, 1, 4, 256, 1, 4, 256], P('layer', None, 'row', None, None, 'col'), as said below
- pattern: int32 [1, 4, 2, 1, 4, 2], P(None, 'row', None, None, 'col'), may hold values from 0 to 1, as said below
Outputs:
- schur: float32 [1, 4, 2, 128, 1, 4, 256], P(None, 'row', 'layer', None, None, 'col')
- factor_panels: float32 [2, 1, 4, 256, 256], P(None, None, 'row')
The draws below stay inside these ranges and needn't reach their ends.
Inputs may be any that keep to these rules, and one draw needn't show every extreme that they name: `partials`: each layer's partial is symmetric; in their sum the leading principal submatrix of order 2 * 256 is positive definite. `pattern`: symmetric in the global tile index.
All inputs are finite; a program needn't handle non-finite values.
Results may differ from the reference program's by a relative error of at most 0.0001.
Values sent between devices are 32-bit elements; how exact they have to be, the bound alone decides.
No kernel may reach another device: no remote copies, remote signals or barrier semaphores. Data moves between devices by JAX's collectives and lax.ppermute only.
A program may use at most 64 MiB of HBM per device.

```python
import jax
import jax.numpy as jnp
from jax import lax

W = 256
TILE = 128
NBLK = 4
LAYERS = 2
TPB = 2
N_ROW = 4
N_COL = 4


def draw_partials(key, part):
    key = jax.random.fold_in(key, 3)
    subkeys = jax.random.split(key, 2)
    front_order = NBLK * W
    noise = jnp.clip(jax.random.normal(subkeys[0], (LAYERS, front_order, front_order), jnp.float32), -4.0, 4.0)
    symmetric = (noise + jnp.transpose(noise, (0, 2, 1))) * 0.5 ** 0.5 / LAYERS ** 0.5
    diagonal = jax.random.uniform(subkeys[1], (LAYERS, front_order), jnp.float32, 4.0, 8.0) * W ** 0.5 / LAYERS
    identity = jnp.eye(front_order, dtype=jnp.float32)
    matrix = symmetric * (1.0 - identity) + identity * diagonal[:, :, None]
    return matrix.reshape(LAYERS, NBLK // N_ROW, N_ROW, W, NBLK // N_COL, N_COL, W)


def draw_pattern(key, part):
    key = jax.random.fold_in(key, 7)
    first_key, second_key = jax.random.split(key)
    tile_count = NBLK * TPB
    levels = jax.random.randint(first_key, (tile_count,), 0, 8)
    raw_draw = jax.random.randint(second_key, (tile_count, tile_count), 0, 16)
    tile_ids = jnp.arange(tile_count)
    upper_half = tile_ids[:, None] <= tile_ids[None, :]
    symmetric = jnp.where(upper_half, raw_draw, raw_draw.T)
    threshold = levels[:, None] + levels[None, :]
    tile_pattern = (symmetric < threshold).astype(jnp.int32)
    return tile_pattern.reshape(NBLK // N_ROW, N_ROW, TPB, NBLK // N_COL, N_COL, TPB)


def setup_inputs(seed: int = 0) -> dict:
    streams_of = jax.random.split(jax.random.key(seed), 3)
    return {
        "partials": draw_partials(jax.random.fold_in(streams_of[2], 71), 0),
        "pattern": draw_pattern(jax.random.fold_in(streams_of[2], 71), 0),
    }


def reference(partials, pattern):
    front_order = NBLK * W
    tile_count = NBLK * TPB
    matrix = jnp.sum(partials.astype(jnp.float32), axis=0).reshape(front_order, front_order)
    tile_pattern = pattern.reshape(tile_count, tile_count)
    tile_block = jnp.arange(tile_count) // TPB
    kept_tiles = (tile_pattern > 0) | (tile_block[:, None] < 2) | (tile_block[None, :] < 2)
    entry_keep = jnp.repeat(jnp.repeat(kept_tiles, TILE, axis=0), TILE, axis=1)
    block_ids = jnp.arange(front_order) // W
    panel_list = []
    for panel in range(2):
        start = panel * W
        diagonal = matrix[start:start + W, start:start + W]
        diag_factor = jnp.linalg.cholesky(diagonal)
        column_raw = matrix[:, start:start + W]
        lower_panel = jax.scipy.linalg.solve_triangular(diag_factor, column_raw.T, lower=True).T
        lower_panel = jnp.where(block_ids[:, None] > panel, lower_panel, 0.0)
        lower_panel = lower_panel.at[start:start + W].set(diag_factor)
        row_raw = matrix[start:start + W, :]
        upper_panel = jax.scipy.linalg.solve_triangular(diag_factor, row_raw, lower=True)
        upper_panel = jnp.where(block_ids[None, :] > panel, upper_panel, 0.0)
        product = jnp.dot(lower_panel.astype(jnp.float32), upper_panel.astype(jnp.float32), precision=lax.Precision.HIGHEST, preferred_element_type=jnp.float32)
        matrix = matrix - jnp.where(entry_keep, product, 0.0)
        panel_list.append(lower_panel)
    schur = matrix.reshape(NBLK // N_ROW, N_ROW, LAYERS, W // LAYERS, NBLK // N_COL, N_COL, W)
    factor_panels = jnp.stack(panel_list).reshape(2, NBLK // N_ROW, N_ROW, W, W)
    return (schur, factor_panels)
```

```python
import functools

import jax
import jax.numpy as jnp
from jax import lax
from jax.experimental import pallas as pl
from jax.experimental.pallas import tpu as pltpu
from jax.sharding import PartitionSpec as P

F32 = jnp.float32
SUB = 8
NT = (((1,), (1,)), ((), ()))
NN = (((1,), (0,)), ((), ()))


def dot(a, b, dims=NN):
    return lax.dot_general(
        a, b, dims, precision=lax.Precision.HIGHEST, preferred_element_type=F32
    )


def lane_splat(x, lane):
    return jnp.broadcast_to(x[:, lane : lane + 1], x.shape)


def row_splat(x, row):
    return jnp.broadcast_to(x[row : row + 1, :], x.shape)


def recip(x):
    return pl.reciprocal(x, approx=True)


def total(terms):
    while len(terms) > 1:
        terms = [terms[i] + terms[i + 1] for i in range(0, len(terms), 2)]
    return terms[0]


def factor_rows(rows):
    groups = len(rows)
    sub = lax.broadcasted_iota(jnp.int32, rows[0].shape, 0)
    lane = lax.broadcasted_iota(jnp.int32, rows[0].shape, 1)
    here = [sub == j for j in range(SUB)]
    held = list(rows)
    out = []
    cols = [lane_splat(held[0], k) for k in range(SUB)]
    for b in range(groups):
        y = held[b]
        near = range(b + 1, min(b + 3, groups))
        side = {g: [lane_splat(held[g], b * SUB + k) for k in range(SUB)] for g in near}
        below = {g: [lane_splat(held[g], b * SUB + k) for k in range(SUB)] for g in range(b + 3, groups)}
        if b + 1 < groups:
            ahead = [lane_splat(held[b + 1], (b + 1) * SUB + k) for k in range(SUB)]
        done = jnp.zeros_like(y)
        for j in range(0, SUB, 2):
            c0, c1 = cols[j], cols[j + 1]
            p, q, s = row_splat(c0, j), row_splat(c1, j), row_splat(c1, j + 1)
            r = recip(p * s - q * q)
            m0 = jnp.where(here[j], c0 - 1.0, c0)
            m1 = jnp.where(here[j + 1], c1 - 1.0, c1)
            for k in range(j + 2, SUB):
                a0, a1 = row_splat(cols[k], j), row_splat(cols[k], j + 1)
                n0, n1 = s * a0 - q * a1, p * a1 - q * a0
                cols[k] = cols[k] - (m0 * n0 + m1 * n1) * r
                for g in near:
                    side[g][k] = side[g][k] - (side[g][j] * n0 + side[g][j + 1] * n1) * r
            if b + 1 < groups:
                s0, s1 = side[b + 1][j], side[b + 1][j + 1]
                for k in range(SUB):
                    a0, a1 = row_splat(s0, k), row_splat(s1, k)
                    n0, n1 = s * a0 - q * a1, p * a1 - q * a0
                    ahead[k] = ahead[k] - (s0 * n0 + s1 * n1) * r
            y0, y1 = row_splat(y, j), row_splat(y, j + 1)
            w0, w1 = (s * y0 - q * y1) * r, (p * y1 - q * y0) * r
            for g in near:
                held[g] = held[g] - (side[g][j] * w0 + side[g][j + 1] * w1)
            y = y - (m0 * w0 + m1 * w1)
            root0 = lax.rsqrt(p)
            ratio = q * root0 * root0
            root1 = lax.rsqrt(s - q * ratio)
            done = jnp.where(here[j], y0 * root0, done)
            done = jnp.where(here[j + 1], (y1 - ratio * y0) * root1, done)
        out.append(jnp.where(lane >= sub + b * SUB, done, 0.0))
        if b + 1 == groups:
            break
        cols = ahead
        yk = [row_splat(y, k) for k in range(SUB)]
        for g, c in below.items():
            held[g] = held[g] - total([c[k] * yk[k] for k in range(SUB)])
    return out


def tile_rows(tile):
    return [tile[g * SUB : (g + 1) * SUB, :] for g in range(tile.shape[0] // SUB)]


def factor(tile, lower_ref, inverse_ref, work):
    order = tile.shape[0]
    half = order // 2
    at_row = lax.broadcasted_iota(jnp.int32, tile.shape, 0)
    at_col = lax.broadcasted_iota(jnp.int32, tile.shape, 1)
    diagonal = jnp.sum(jnp.where(at_row == at_col, tile, 0.0), axis=0, keepdims=True)
    scale = jnp.broadcast_to(lax.rsqrt(diagonal), tile.shape)
    down = scale.T
    a = tile * scale * down
    one = jnp.where(at_row[:half, :half] == at_col[:half, :half], 1.0, 0.0).astype(F32)
    beside = jnp.where(at_row[:half] + half == at_col[:half], 1.0, 0.0).astype(F32)
    work[half:, :half] = a[half:, half:]
    work[half:, half:] = one
    first = jnp.concatenate(factor_rows(tile_rows(jnp.where(at_col[:half] < half, a[:half], beside))), axis=0)
    inverse0 = first[:, half:]
    under = dot(a[half:, :half], inverse0, NT)
    work[half:, :half] -= dot(under, under, NT)
    second = jnp.concatenate(factor_rows(tile_rows(work[half:, :])), axis=0)
    inverse1 = second[:, half:]
    inverse_ref[:half, :half] = inverse0 * scale[:half, :half]
    inverse_ref[:half, half:] = jnp.zeros((half, half), F32)
    inverse_ref[half:, :half] = -dot(inverse1, dot(under, inverse0)) * scale[half:, :half]
    inverse_ref[half:, half:] = inverse1 * scale[half:, half:]
    work[:half, :] = jnp.where(at_col[:half] < half, first, 0.0)
    work[half:, :half] = jnp.zeros((half, half), F32)
    work[half:, half:] = second[:, :half]
    up = recip(down)
    lower_ref[...] = work[...].T * up
    lower_ref[half:, :half] = under * up[half:, :half]


def pack_kernel(index_ref, source_ref, mine_ref, *refs):
    *send_refs, linear_ref, arrived = refs
    layer = index_ref[0]
    first = (index_ref[1] == 0) & (index_ref[2] == 0)
    height, tile = mine_ref.shape
    piece = linear_ref.shape[0] // (len(send_refs) + 1)
    out_refs = (mine_ref, *send_refs)

    @pl.when(first)
    def _():
        load = pltpu.make_async_copy(source_ref, linear_ref, arrived.at[0])
        load.start()
        load.wait()
        at_row = lax.broadcasted_iota(jnp.int32, (tile, tile), 0)
        at_col = lax.broadcasted_iota(jnp.int32, (tile, tile), 1)
        corner = linear_ref[pl.ds(2 * tile + 1, tile, 2), :]
        mixed = jnp.where(at_row >= at_col, linear_ref[pl.ds(0, tile, 2), :], corner)
        below = linear_ref[pl.ds(2 * tile, tile, 2), :]
        diagonal = jnp.sum(jnp.where(at_row == at_col, corner, 0.0), axis=0, keepdims=True)
        for ref in out_refs:
            ref[:tile, :] = mixed
            ref[tile : 2 * tile, :] = below
            ref[2 * tile :, :] = jnp.broadcast_to(diagonal, (height - 2 * tile, tile))

    @pl.when(jnp.logical_not(first))
    def _():
        loads = []
        for k, ref in enumerate(out_refs):
            start = pl.multiple_of((layer ^ k) * piece, piece)
            from_ref = source_ref.at[pl.ds(start, piece), :]
            loads.append(pltpu.make_async_copy(from_ref, ref.at[pl.ds(0, piece), :], arrived.at[k]))
            loads[-1].start()
        for ref in out_refs:
            ref[piece:, :] = jnp.zeros((height - piece, tile), F32)
        for load in loads:
            load.wait()


def unpack(pieces, to_ref):
    tile = pieces[0].shape[1]
    slab = pieces[0].shape[0] // 2
    for t, piece in enumerate(pieces):
        to_ref[t * slab : (t + 1) * slab, :tile] = piece[pl.ds(0, slab, 2), :]
        to_ref[t * slab : (t + 1) * slab, tile:] = piece[pl.ds(1, slab, 2), :]


def symmetric(lower, keep):
    part = jnp.where(keep, lower, 0.0)
    at = lax.broadcasted_iota(jnp.int32, lower.shape, 0) == lax.broadcasted_iota(jnp.int32, lower.shape, 1)
    return part + jnp.where(at, 0.0, part).T


def first_kernel(packed_ref, block_ref, lower_ref, inverse_ref, left_ref, rest_ref, work):
    tile = packed_ref.shape[1]
    at_row = lax.broadcasted_iota(jnp.int32, (tile, tile), 0)
    at_col = lax.broadcasted_iota(jnp.int32, (tile, tile), 1)
    mixed = packed_ref[:tile, :]
    below = packed_ref[tile : 2 * tile, :]
    tile0 = symmetric(mixed, at_row >= at_col)
    upper1 = jnp.where(at_row < at_col, mixed, 0.0)
    diagonal = jnp.broadcast_to(packed_ref[2 * tile : 2 * tile + 1, :], (tile, tile))
    tile1 = upper1 + upper1.T + jnp.where(at_row == at_col, diagonal, 0.0)
    block_ref[:tile, :tile] = tile0
    block_ref[tile:, :tile] = below
    block_ref[:tile, tile:] = below.T
    block_ref[tile:, tile:] = tile1
    factor(tile0, lower_ref, inverse_ref, work)
    left = dot(below, inverse_ref[...], NT)
    left_ref[...] = left
    rest_ref[...] = tile1 - dot(left, left, NT)


def second_kernel(lower0_ref, inverse0_ref, left_ref, rest_ref, lower_ref, inverse_ref, work):
    tile = rest_ref.shape[0]
    zero = jnp.zeros((tile, tile), F32)
    first, second = slice(0, tile), slice(tile, 2 * tile)
    lower_ref[first, first] = lower0_ref[...]
    lower_ref[first, second] = zero
    lower_ref[second, first] = left_ref[...]
    inverse_ref[first, first] = inverse0_ref[...]
    inverse_ref[first, second] = zero
    factor(rest_ref[...], lower_ref.at[second, second], inverse_ref.at[second, second], work)
    inverse_ref[second, first] = -dot(inverse_ref[second, second], dot(left_ref[...], inverse0_ref[...]))


def third_kernel(
    lead_ref, inverse0_ref, left_ref, lower_ref, inverse_ref, under_ref, rest_ref,
    corner_ref, below_ref, work,
):
    tile = lower_ref.shape[0]
    unpack([lead_ref.at[t, 0] for t in range(lead_ref.shape[0])], below_ref)
    unpack([lead_ref.at[t, 1] for t in range(lead_ref.shape[0])], corner_ref)
    left_ref[...] = dot(below_ref[...], inverse0_ref[...], NT)
    top, bottom = left_ref[:tile, :], left_ref[tile:, :]
    factor(corner_ref[:tile, :tile] - dot(top, top, NT), lower_ref, inverse_ref, work)
    under = dot(corner_ref[tile:, :tile] - dot(bottom, top, NT), inverse_ref[...], NT)
    under_ref[...] = under
    rest_ref[...] = corner_ref[tile:, tile:] - dot(bottom, bottom, NT) - dot(under, under, NT)


def fourth_kernel(
    left_ref, inverse0_ref, lower0_ref, small_ref, under_ref, rest_ref, lower_ref, inverse_ref, cross_ref, work
):
    second_kernel(lower0_ref, small_ref, under_ref, rest_ref, lower_ref, inverse_ref, work)
    cross_ref[...] = -dot(inverse_ref[...], dot(left_ref[...], inverse0_ref[...]))


def final_kernel(
    index_ref, keep_ref, own_ref, block_ref, rows_ref, cols_ref,
    lower0_ref, inverse0_ref, lower1_ref, inverse1_ref, left_ref, cross_ref,
    schur_ref, panels_ref, upper_ref, row_ref,
):
    layer, row, col = index_ref[0], index_ref[1], index_ref[2]
    width = upper_ref.shape[1]
    tiles_per = keep_ref.shape[0]
    tile = width // tiles_per
    slabs = rows_ref.shape[0]
    slab_rows = width // slabs

    @pl.when(row == 0)
    def _():
        panels_ref[0] = lower0_ref[...]
        panels_ref[1] = jnp.zeros((width, width), F32)

    @pl.when(row == 1)
    def _():
        panels_ref[0] = left_ref[...]
        panels_ref[1] = lower1_ref[...]

    @pl.when(row > 1)
    def _():
        for k in range(2):
            unpack([rows_ref.at[t, k] for t in range(slabs)], row_ref.at[k])
        panels_ref[0] = dot(row_ref[0], inverse0_ref[...], NT)
        panels_ref[1] = dot(row_ref[0], cross_ref[...], NT) + dot(row_ref[1], inverse1_ref[...], NT)

    @pl.when(col == 0)
    def _():
        upper_ref[...] = jnp.zeros(upper_ref.shape, F32)

    @pl.when(col == 1)
    def _():
        upper_ref[:width, :] = left_ref[...].T
        upper_ref[width:, :] = jnp.zeros((width, width), F32)

    @pl.when(col > 1)
    def _():
        for k in range(2):
            unpack([cols_ref.at[t, k] for t in range(slabs)], row_ref.at[k])
        upper_ref[:width, :] = dot(inverse0_ref[...], row_ref[0])
        upper_ref[width:, :] = dot(cross_ref[...], row_ref[0]) + dot(inverse1_ref[...], row_ref[1])

    slab = pl.ds(pl.multiple_of(layer * slab_rows, slab_rows), slab_rows)
    product = dot(panels_ref[0, slab, :], upper_ref[:width, :]) + dot(panels_ref[1, slab, :], upper_ref[width:, :])
    at_row = (lax.broadcasted_iota(jnp.int32, (slab_rows, tile), 0) + layer * slab_rows) // tile
    for j in range(tiles_per):
        keep = jnp.zeros((slab_rows, tile), jnp.int32)
        for i in range(tiles_per):
            keep = jnp.where(at_row == i, keep_ref[i, j], keep)
        own = own_ref[pl.ds(j, slab_rows, tiles_per), :]
        at = slice(j * tile, (j + 1) * tile)
        own = jnp.where((row == 0) & (col == 0), block_ref[slab, at], own)
        schur_ref[pl.ds(j, slab_rows, tiles_per), :] = own - jnp.where(keep > 0, product[:, at], 0.0)


AXES = ("layer", "row", "col")


def trade(x, axis, k):
    return lax.ppermute(x, axis, [(i, i ^ k) for i in range(lax.axis_size(axis))])


def ask_layers(x, members=None):
    parts = [x]
    layers, rows, cols = (lax.axis_size(a) for a in AXES)
    for k in range(1, layers):
        if members is None:
            parts.append(trade(x, "layer", k))
        else:
            pairs = [
                (((i * rows) + r) * cols + c, (((i ^ k) * rows) + r) * cols + c)
                for i in range(layers)
                for r, c in members
            ]
            parts.append(lax.ppermute(x, AXES, pairs))
    return parts


def in_order(parts, *late):
    layer = lax.axis_index("layer").astype(jnp.int32)
    parts = parts[:1] + [after(part, *late) for part in parts[1:]]
    ordered = []
    for t in range(len(parts)):
        held = parts[0]
        for k in range(1, len(parts)):
            held = jnp.where(layer ^ t == k, parts[k], held)
        ordered.append(held)
    return jnp.stack(ordered)


def strides(count, least):
    step = 1
    while 2 * step < count:
        step *= 2
    out = []
    while step >= least:
        out.append(step)
        step //= 2
    return out


def after(x, *others):
    return lax.optimization_barrier((x,) + others)[0]


def run(kernel, outs, ins, scratch=(), flops=0, name=None, smem=0, source=pltpu.VMEM):
    vmem = pl.BlockSpec(memory_space=pltpu.VMEM)
    ins_at = [pl.BlockSpec(memory_space=pltpu.SMEM)] * smem + [pl.BlockSpec(memory_space=source)] * (len(ins) - smem)
    return pl.pallas_call(
        kernel,
        out_shape=tuple(jax.ShapeDtypeStruct(s, F32) for s in outs),
        in_specs=ins_at,
        out_specs=tuple(vmem for _ in outs),
        scratch_shapes=[pltpu.VMEM(s, F32) if isinstance(s, tuple) else s for s in scratch],
        compiler_params=pltpu.CompilerParams(vmem_limit_bytes=24 * 1024 * 1024),
        cost_estimate=pl.CostEstimate(flops=flops, bytes_accessed=10**6, transcendentals=0),
        name=name,
    )(*ins)


def on_device(partials, pattern):
    layers, rows, cols = (lax.axis_size(a) for a in AXES)
    layer, row, col = (lax.axis_index(a).astype(jnp.int32) for a in AXES)
    width = partials.shape[3]
    tiles_per = pattern.shape[2]
    tile = width // tiles_per
    slab_rows = width // layers
    piece_rows = slab_rows * tiles_per
    height = 2 * tile + SUB
    even_row, even_col = row % 2 == 0, col % 2 == 0
    index = jnp.stack([layer, row, col])
    square, big = (tile, tile), (width, width)

    mine, *sends = run(
        pack_kernel,
        ((height, tile),) * layers,
        (index, pltpu.with_memory_space_constraint(partials.reshape(width * tiles_per, tile), pltpu.HBM)),
        scratch=((width * tiles_per, tile), pltpu.SemaphoreType.DMA((layers,))),
        name="k0",
        smem=1,
        source=pltpu.HBM,
    )
    front = total([mine] + [trade(x, "layer", k + 1) for k, x in enumerate(sends)])
    piece = front[:piece_rows]

    keep = (pattern.reshape(tiles_per, tiles_per) > 0) | (row < 2) | (col < 2)
    keep = keep.astype(jnp.int32)
    fall = after(piece, keep)
    for s in strides(rows, 2):
        fall_from, fall_got = fall, trade(fall, "row", s)
        if s > 2:
            fall = jnp.where(row % (2 * s) >= s, fall_got, fall_from)

    lead = front
    for s in strides(cols, 2):
        lead = jnp.where(col % (2 * s) >= s, trade(lead, "col", s), lead)
    fall_got = after(fall_got, lead)
    fall = jnp.where(row % 4 >= 2, fall_got, fall_from)
    lead = after(lead, fall_got)
    fall = after(fall, lead)
    fall_other = trade(fall, "row", 1)
    got = trade(lead, "col", 1)
    low, high = jnp.where(even_col, lead, got), jnp.where(even_col, got, lead)
    panels_in = jnp.stack([low[:piece_rows], high[:piece_rows]])
    high = high[:piece_rows]

    low = after(low, fall_other)
    high = after(high, low)
    cols_in = ask_layers(
        jnp.stack([jnp.where(even_row, fall, fall_other), jnp.where(even_row, fall_other, fall)])
    )
    for s in strides(rows, 2):
        low = jnp.where(row % (2 * s) >= s, trade(low, "row", s), low)
    for s in strides(rows, 2):
        high_from, high_got = high, trade(high, "row", s)
        if s > 2:
            high = jnp.where(row % (2 * s) >= s, high_got, high_from)
    high = jnp.where(row % 4 >= 2, after(high_got, low), high_from)
    packed = jnp.where(even_row, low, trade(low, "row", 1))
    lead = jnp.stack([low[:piece_rows], high])
    lead_parts = ask_layers(lead, [(r, c) for r in range(1, rows, 2) for c in range(cols)])
    packed = after(packed, high)

    block0, small_lower, small_inverse, left0, rest0 = run(
        first_kernel,
        (big, square, square, square, square),
        (packed,),
        scratch=(square,),
        flops=5 * 10**9,
        name="k1",
    )
    lead = in_order(lead_parts, rest0)
    lead_other = trade(lead, "row", 1)
    rows_in = ask_layers(after(panels_in, lead))

    lower0, inverse0 = run(
        second_kernel,
        (big, big),
        (small_lower, small_inverse, left0, after(rest0, lead)),
        scratch=(square,),
        flops=5 * 10**9,
        name="k2",
    )
    lead_other = after(lead_other, inverse0)
    lead = jnp.where(even_row, lead_other, lead)
    left1, small_lower, small_inverse, under, rest1 = run(
        third_kernel,
        (big, square, square, square, square),
        (lead, inverse0),
        scratch=(big, big, square),
        flops=5 * 10**9,
        name="k3",
    )
    lower1, inverse1, cross = run(
        fourth_kernel,
        (big, big, big),
        (left1, inverse0, small_lower, small_inverse, under, rest1),
        scratch=(square,),
        flops=5 * 10**9,
        name="k4",
    )
    rows_in, cols_in = in_order(rows_in, cross), in_order(cols_in, cross)
    schur, panels = run(
        final_kernel,
        ((piece_rows, tile), (2, width, width)),
        (index, keep, piece, block0, rows_in, cols_in, lower0, inverse0, lower1, inverse1, left1, cross),
        scratch=((2 * width, width), (2, width, width)),
        flops=10**9,
        name="kf",
        smem=2,
    )
    return (
        schur.reshape(1, 1, 1, slab_rows, 1, 1, width),
        panels.reshape(2, 1, 1, width, width),
    )


def solution(mesh):
    return jax.shard_map(
        on_device,
        mesh=mesh,
        in_specs=(
            P("layer", None, "row", None, None, "col", None),
            P(None, "row", None, None, "col", None),
        ),
        out_specs=(
            P(None, "row", "layer", None, None, "col", None),
            P(None, None, "row", None, None),
        ),
        check_vma=False,
    )
```

```python
import functools

import jax
import jax.numpy as jnp
from jax import lax
from jax.experimental import pallas as pl
from jax.experimental.pallas import tpu as pltpu
from jax.sharding import PartitionSpec as P

F32 = jnp.float32
SUB = 8
NT = (((1,), (1,)), ((), ()))
NN = (((1,), (0,)), ((), ()))


def dot(a, b, dims=NN):
    return lax.dot_general(
        a, b, dims, precision=lax.Precision.HIGHEST, preferred_element_type=F32
    )


def lane_splat(x, lane):
    return jnp.broadcast_to(x[:, lane : lane + 1], x.shape)


def row_splat(x, row):
    return jnp.broadcast_to(x[row : row + 1, :], x.shape)


def recip(x):
    return pl.reciprocal(x, approx=True)


def total(terms):
    while len(terms) > 1:
        terms = [terms[i] + terms[i + 1] for i in range(0, len(terms), 2)]
    return terms[0]


def factor_rows(rows):
    groups = len(rows)
    sub = lax.broadcasted_iota(jnp.int32, rows[0].shape, 0)
    lane = lax.broadcasted_iota(jnp.int32, rows[0].shape, 1)
    here = [sub == j for j in range(SUB)]
    unit = [jnp.where(h, 1.0, 0.0).astype(F32) for h in here]
    held = list(rows)
    out = []
    cols = [lane_splat(held[0], k) for k in range(SUB)]
    for b in range(groups):
        y = held[b]
        last = b + 1 == groups
        if not last:
            near = held[b + 1]
            side = [lane_splat(near, b * SUB + k) for k in range(SUB)]
            ahead = [lane_splat(near, (b + 1) * SUB + k) for k in range(SUB)]
        below = {g: [lane_splat(held[g], b * SUB + k) for k in range(SUB)] for g in range(b + 2, groups)}
        done = jnp.zeros_like(y)
        for j in range(0, SUB, 2):
            c0, c1 = cols[j], cols[j + 1]
            p, q, s = row_splat(c0, j), row_splat(c1, j), row_splat(c1, j + 1)
            r = recip(p * s - q * q)
            m0, m1 = c0 - unit[j], c1 - unit[j + 1]
            if j + 2 < SUB:
                v0, v1 = s * c0 - q * c1, p * c1 - q * c0
            for k in range(j + 2, SUB):
                n0, n1 = row_splat(v0, k), row_splat(v1, k)
                cols[k] = cols[k] - (m0 * n0 + m1 * n1) * r
                if not last:
                    side[k] = side[k] - (side[j] * n0 + side[j + 1] * n1) * r
            y0, y1 = row_splat(y, j), row_splat(y, j + 1)
            w0, w1 = (s * y0 - q * y1) * r, (p * y1 - q * y0) * r
            if not last:
                s0, s1 = side[j], side[j + 1]
                v0, v1 = s * s0 - q * s1, p * s1 - q * s0
                for k in range(SUB):
                    ahead[k] = ahead[k] - (s0 * row_splat(v0, k) + s1 * row_splat(v1, k)) * r
                near = near - (s0 * w0 + s1 * w1)
            y = y - (m0 * w0 + m1 * w1)
            root0 = lax.rsqrt(p)
            ratio = q * root0 * root0
            root1 = lax.rsqrt(s - q * ratio)
            done = jnp.where(here[j], y0 * root0, done)
            done = jnp.where(here[j + 1], (y1 - ratio * y0) * root1, done)
        out.append(jnp.where(lane >= sub + b * SUB, done, 0.0))
        if last:
            break
        held[b + 1] = near
        cols = ahead
        if below:
            yk = [row_splat(y, k) for k in range(SUB)]
        for g, c in below.items():
            held[g] = held[g] - total([c[k] * yk[k] for k in range(SUB)])
    return out


def tile_rows(tile):
    return [tile[g * SUB : (g + 1) * SUB, :] for g in range(tile.shape[0] // SUB)]


def factor(tile, lower_ref, inverse_ref, work):
    order = tile.shape[0]
    half = order // 2
    at_row = lax.broadcasted_iota(jnp.int32, tile.shape, 0)
    at_col = lax.broadcasted_iota(jnp.int32, tile.shape, 1)
    diagonal = jnp.sum(jnp.where(at_row == at_col, tile, 0.0), axis=0, keepdims=True)
    scale = jnp.broadcast_to(lax.rsqrt(diagonal), tile.shape)
    down = scale.T
    a = tile * scale * down
    one = jnp.where(at_row[:half, :half] == at_col[:half, :half], 1.0, 0.0).astype(F32)
    beside = jnp.where(at_row[:half] + half == at_col[:half], 1.0, 0.0).astype(F32)
    work[half:, :half] = a[half:, half:]
    work[half:, half:] = one
    first = jnp.concatenate(factor_rows(tile_rows(jnp.where(at_col[:half] < half, a[:half], beside))), axis=0)
    inverse0 = first[:, half:]
    under = dot(a[half:, :half], inverse0, NT)
    work[half:, :half] -= dot(under, under, NT)
    second = jnp.concatenate(factor_rows(tile_rows(work[half:, :])), axis=0)
    inverse1 = second[:, half:]
    inverse_ref[:half, :half] = inverse0 * scale[:half, :half]
    inverse_ref[:half, half:] = jnp.zeros((half, half), F32)
    inverse_ref[half:, :half] = -dot(inverse1, dot(under, inverse0)) * scale[half:, :half]
    inverse_ref[half:, half:] = inverse1 * scale[half:, half:]
    work[:half, :] = jnp.where(at_col[:half] < half, first, 0.0)
    work[half:, :half] = jnp.zeros((half, half), F32)
    work[half:, half:] = second[:, :half]
    up = recip(down)
    lower_ref[...] = work[...].T * up
    lower_ref[half:, :half] = under * up[half:, :half]


def pack_kernel(index_ref, source_ref, mine_ref, *refs):
    *send_refs, linear_ref, arrived = refs
    load = pltpu.make_async_copy(source_ref, linear_ref, arrived)
    load.start()
    layer = index_ref[0]
    first = (index_ref[1] == 0) & (index_ref[2] == 0)
    height, tile = mine_ref.shape
    load.wait()
    piece = linear_ref.shape[0] // (len(send_refs) + 1)

    @pl.when(first)
    def _():
        at_row = lax.broadcasted_iota(jnp.int32, (tile, tile), 0)
        at_col = lax.broadcasted_iota(jnp.int32, (tile, tile), 1)
        corner = linear_ref[pl.ds(2 * tile + 1, tile, 2), :]
        mixed = jnp.where(at_row >= at_col, linear_ref[pl.ds(0, tile, 2), :], corner)
        below = linear_ref[pl.ds(2 * tile, tile, 2), :]
        diagonal = jnp.sum(jnp.where(at_row == at_col, corner, 0.0), axis=0, keepdims=True)
        for ref in (mine_ref, *send_refs):
            ref[:tile, :] = mixed
            ref[tile : 2 * tile, :] = below
            ref[2 * tile :, :] = jnp.broadcast_to(diagonal, (height - 2 * tile, tile))

    @pl.when(jnp.logical_not(first))
    def _():
        for k, ref in enumerate((mine_ref, *send_refs)):
            start = pl.multiple_of((layer ^ k) * piece, piece)
            ref[:piece, :] = linear_ref[pl.ds(start, piece), :]
            ref[piece:, :] = jnp.zeros((height - piece, tile), F32)


def unpack(pieces, to_ref):
    tile = pieces[0].shape[1]
    slab = pieces[0].shape[0] // 2
    for t, piece in enumerate(pieces):
        to_ref[t * slab : (t + 1) * slab, :tile] = piece[pl.ds(0, slab, 2), :]
        to_ref[t * slab : (t + 1) * slab, tile:] = piece[pl.ds(1, slab, 2), :]


def symmetric(lower, keep):
    part = jnp.where(keep, lower, 0.0)
    at = lax.broadcasted_iota(jnp.int32, lower.shape, 0) == lax.broadcasted_iota(jnp.int32, lower.shape, 1)
    return part + jnp.where(at, 0.0, part).T


def first_kernel(packed_ref, block_ref, lower_ref, inverse_ref, left_ref, rest_ref, work):
    tile = packed_ref.shape[1]
    at_row = lax.broadcasted_iota(jnp.int32, (tile, tile), 0)
    at_col = lax.broadcasted_iota(jnp.int32, (tile, tile), 1)
    mixed = packed_ref[:tile, :]
    below = packed_ref[tile : 2 * tile, :]
    tile0 = symmetric(mixed, at_row >= at_col)
    upper1 = jnp.where(at_row < at_col, mixed, 0.0)
    diagonal = jnp.broadcast_to(packed_ref[2 * tile : 2 * tile + 1, :], (tile, tile))
    tile1 = upper1 + upper1.T + jnp.where(at_row == at_col, diagonal, 0.0)
    block_ref[:tile, :tile] = tile0
    block_ref[tile:, :tile] = below
    block_ref[:tile, tile:] = below.T
    block_ref[tile:, tile:] = tile1
    factor(tile0, lower_ref, inverse_ref, work)
    left = dot(below, inverse_ref[...], NT)
    left_ref[...] = left
    rest_ref[...] = tile1 - dot(left, left, NT)


def second_kernel(lower0_ref, inverse0_ref, left_ref, rest_ref, lower_ref, inverse_ref, work):
    tile = rest_ref.shape[0]
    zero = jnp.zeros((tile, tile), F32)
    first, second = slice(0, tile), slice(tile, 2 * tile)
    lower_ref[first, first] = lower0_ref[...]
    lower_ref[first, second] = zero
    lower_ref[second, first] = left_ref[...]
    inverse_ref[first, first] = inverse0_ref[...]
    inverse_ref[first, second] = zero
    factor(rest_ref[...], lower_ref.at[second, second], inverse_ref.at[second, second], work)
    inverse_ref[second, first] = -dot(inverse_ref[second, second], dot(left_ref[...], inverse0_ref[...]))


def third_kernel(
    corners_ref, belows_ref, inverse0_ref, left_ref, lower_ref, inverse_ref, cross_ref, corner_ref, below_ref, work,
):
    tile = work.shape[0]
    first, second = slice(0, tile), slice(tile, 2 * tile)
    zero = jnp.zeros((tile, tile), F32)
    unpack([belows_ref.at[t] for t in range(belows_ref.shape[0])], below_ref)
    unpack([corners_ref.at[t] for t in range(corners_ref.shape[0])], corner_ref)
    top = dot(below_ref[first, :], inverse0_ref[...], NT)
    factor(corner_ref[first, first] - dot(top, top, NT), lower_ref.at[first, first], inverse_ref.at[first, first], work)
    bottom = dot(below_ref[second, :], inverse0_ref[...], NT)
    left_ref[first, :] = top
    left_ref[second, :] = bottom
    ahead = corner_ref[second, first] - dot(bottom, top, NT)
    rest = corner_ref[second, second] - dot(bottom, bottom, NT)
    under = dot(ahead, inverse_ref[first, first], NT)
    lower_ref[first, second] = zero
    lower_ref[second, first] = under
    inverse_ref[first, second] = zero
    factor(rest - dot(under, under, NT), lower_ref.at[second, second], inverse_ref.at[second, second], work)
    inverse_ref[second, first] = -dot(inverse_ref[second, second], dot(under, inverse_ref[first, first]))
    cross_ref[...] = -dot(inverse_ref[...], dot(left_ref[...], inverse0_ref[...]))


def final_kernel(
    index_ref, keep_ref, own_ref, block_ref, rows_ref, cols_ref,
    lower0_ref, inverse0_ref, lower1_ref, inverse1_ref, left_ref, cross_ref,
    schur_ref, panels_ref, upper_ref, row_ref,
):
    layer, row, col = index_ref[0], index_ref[1], index_ref[2]
    width = upper_ref.shape[1]
    tiles_per = keep_ref.shape[0]
    tile = width // tiles_per
    slabs = rows_ref.shape[0]
    slab_rows = width // slabs

    @pl.when(row == 0)
    def _():
        panels_ref[0] = lower0_ref[...]
        panels_ref[1] = jnp.zeros((width, width), F32)

    @pl.when(row == 1)
    def _():
        panels_ref[0] = left_ref[...]
        panels_ref[1] = lower1_ref[...]

    @pl.when(row > 1)
    def _():
        for k in range(2):
            unpack([rows_ref.at[t, k] for t in range(slabs)], row_ref.at[k])
        panels_ref[0] = dot(row_ref[0], inverse0_ref[...], NT)
        panels_ref[1] = dot(row_ref[0], cross_ref[...], NT) + dot(row_ref[1], inverse1_ref[...], NT)

    @pl.when(col == 0)
    def _():
        upper_ref[...] = jnp.zeros(upper_ref.shape, F32)

    @pl.when(col == 1)
    def _():
        upper_ref[:width, :] = left_ref[...].T
        upper_ref[width:, :] = jnp.zeros((width, width), F32)

    @pl.when(col > 1)
    def _():
        for k in range(2):
            unpack([cols_ref.at[t, k] for t in range(slabs)], row_ref.at[k])
        upper_ref[:width, :] = dot(inverse0_ref[...], row_ref[0])
        upper_ref[width:, :] = dot(cross_ref[...], row_ref[0]) + dot(inverse1_ref[...], row_ref[1])

    slab = pl.ds(pl.multiple_of(layer * slab_rows, slab_rows), slab_rows)
    product = dot(panels_ref[0, slab, :], upper_ref[:width, :]) + dot(panels_ref[1, slab, :], upper_ref[width:, :])
    at_row = (lax.broadcasted_iota(jnp.int32, (slab_rows, tile), 0) + layer * slab_rows) // tile
    for j in range(tiles_per):
        keep = jnp.zeros((slab_rows, tile), jnp.int32)
        for i in range(tiles_per):
            keep = jnp.where(at_row == i, keep_ref[i, j], keep)
        own = own_ref[pl.ds(j, slab_rows, tiles_per), :]
        at = slice(j * tile, (j + 1) * tile)
        own = jnp.where((row == 0) & (col == 0), block_ref[slab, at], own)
        schur_ref[pl.ds(j, slab_rows, tiles_per), :] = own - jnp.where(keep > 0, product[:, at], 0.0)


AXES = ("layer", "row", "col")


def trade(x, axis, k):
    return lax.ppermute(x, axis, [(i, i ^ k) for i in range(lax.axis_size(axis))])


def ask_layers(x):
    return [x] + [trade(x, "layer", k) for k in range(1, lax.axis_size("layer"))]


def in_order(parts, *late):
    layer = lax.axis_index("layer").astype(jnp.int32)
    parts = parts[:1] + [after(part, *late) for part in parts[1:]]
    ordered = []
    for t in range(len(parts)):
        held = parts[0]
        for k in range(1, len(parts)):
            held = jnp.where(layer ^ t == k, parts[k], held)
        ordered.append(held)
    return jnp.stack(ordered)


def strides(count, least):
    step = 1
    while 2 * step < count:
        step *= 2
    out = []
    while step >= least:
        out.append(step)
        step //= 2
    return out


def after(x, *others):
    return lax.optimization_barrier((x,) + others)[0]


def run(kernel, outs, ins, scratch=(), flops=0, name=None, smem=0, source=pltpu.VMEM):
    vmem = pl.BlockSpec(memory_space=pltpu.VMEM)
    ins_at = [pl.BlockSpec(memory_space=pltpu.SMEM)] * smem + [pl.BlockSpec(memory_space=source)] * (len(ins) - smem)
    return pl.pallas_call(
        kernel,
        out_shape=tuple(jax.ShapeDtypeStruct(s, F32) for s in outs),
        in_specs=ins_at,
        out_specs=tuple(vmem for _ in outs),
        scratch_shapes=[pltpu.VMEM(s, F32) if isinstance(s, tuple) else s for s in scratch],
        compiler_params=pltpu.CompilerParams(vmem_limit_bytes=24 * 1024 * 1024),
        cost_estimate=pl.CostEstimate(flops=flops, bytes_accessed=10**6, transcendentals=0),
        name=name,
    )(*ins)


def on_device(partials, pattern):
    layers, rows, cols = (lax.axis_size(a) for a in AXES)
    layer, row, col = (lax.axis_index(a).astype(jnp.int32) for a in AXES)
    width = partials.shape[3]
    tiles_per = pattern.shape[2]
    tile = width // tiles_per
    slab_rows = width // layers
    piece_rows = slab_rows * tiles_per
    height = 2 * tile + SUB
    even_row, even_col = row % 2 == 0, col % 2 == 0
    index = jnp.stack([layer, row, col])
    square, big = (tile, tile), (width, width)

    mine, *sends = run(
        pack_kernel,
        ((height, tile),) * layers,
        (index, pltpu.with_memory_space_constraint(partials.reshape(width * tiles_per, tile), pltpu.HBM)),
        scratch=((width * tiles_per, tile), pltpu.SemaphoreType.DMA),
        name="k0",
        smem=1,
        source=pltpu.HBM,
    )
    front = total([mine] + [trade(x, "layer", k + 1) for k, x in enumerate(sends)])
    piece = front[:piece_rows]

    keep = (pattern.reshape(tiles_per, tiles_per) > 0) | (row < 2) | (col < 2)
    keep = keep.astype(jnp.int32)
    fall = after(piece, keep)
    for s in strides(rows, 2):
        fall_from, fall_got = fall, trade(fall, "row", s)
        if s > 2:
            fall = jnp.where(row % (2 * s) >= s, fall_got, fall_from)

    lead = front
    for s in strides(cols, 2):
        lead = jnp.where(col % (2 * s) >= s, trade(lead, "col", s), lead)
    fall_got = after(fall_got, lead)
    lead = after(lead, fall_got)
    got = trade(lead, "col", 1)
    low, high = jnp.where(even_col, lead, got), jnp.where(even_col, got, lead)
    panels_in = jnp.stack([low[:piece_rows], high[:piece_rows]])
    high = high[:piece_rows]

    high = after(high, low)

    for s in strides(rows, 2):
        low = jnp.where(row % (2 * s) >= s, trade(low, "row", s), low)
    for s in strides(rows, 2):
        high_from, high_got = high, trade(high, "row", s)
        if s > 2:
            high = jnp.where(row % (2 * s) >= s, high_got, high_from)
    high = jnp.where(row % 4 >= 2, after(high_got, low), high_from)
    got = trade(low, "row", 1)
    packed = jnp.where(even_row, low, got)
    lead_parts = ask_layers(jnp.where(even_row, got[:piece_rows], high))
    rows_in = ask_layers(after(panels_in, lead_parts[0]))
    packed = after(packed, high)

    block0, small_lower, small_inverse, left0, rest0 = run(
        first_kernel,
        (big, square, square, square, square),
        (packed,),
        scratch=(square,),
        flops=5 * 10**9,
        name="k1",
    )
    lead = in_order(lead_parts, rest0)
    fall = jnp.where(row % 4 >= 2, fall_got, fall_from)
    lead_other = trade(jnp.concatenate([lead, fall[None]], axis=0), "row", 1)
    lead_other, fall_other = lead_other[:layers], lead_other[layers]
    lower0, inverse0 = run(
        second_kernel,
        (big, big),
        (small_lower, small_inverse, left0, after(rest0, lead)),
        scratch=(square,),
        flops=5 * 10**9,
        name="k2",
    )
    lead_other = after(lead_other, inverse0)
    corners, belows = jnp.where(even_row, lead_other, lead), jnp.where(even_row, lead, lead_other)
    fall_other = after(fall_other, inverse0)
    cols_in = ask_layers(
        jnp.stack([jnp.where(even_row, fall, fall_other), jnp.where(even_row, fall_other, fall)])
    )
    left1, lower1, inverse1, cross = run(
        third_kernel,
        (big, big, big, big),
        (corners, belows, inverse0),
        scratch=(big, big, square),
        flops=10**10,
        name="k3",
    )
    rows_in, cols_in = in_order(rows_in, cross), in_order(cols_in, cross)
    schur, panels = run(
        final_kernel,
        ((piece_rows, tile), (2, width, width)),
        (index, keep, piece, block0, rows_in, cols_in, lower0, inverse0, lower1, inverse1, left1, cross),
        scratch=((2 * width, width), (2, width, width)),
        flops=10**9,
        name="kf",
        smem=2,
    )
    return (
        schur.reshape(1, 1, 1, slab_rows, 1, 1, width),
        panels.reshape(2, 1, 1, width, width),
    )


def solution(mesh):
    return jax.shard_map(
        on_device,
        mesh=mesh,
        in_specs=(
            P("layer", None, "row", None, None, "col", None),
            P(None, "row", None, None, "col", None),
        ),
        out_specs=(
            P(None, "row", "layer", None, None, "col", None),
            P(None, None, "row", None, None),
        ),
        check_vma=False,
    )
```

```python
import functools

import jax
import jax.numpy as jnp
from jax import lax
from jax.experimental import pallas as pl
from jax.experimental.pallas import tpu as pltpu
from jax.sharding import PartitionSpec as P

F32 = jnp.float32
SUB = 8
NT = (((1,), (1,)), ((), ()))
NN = (((1,), (0,)), ((), ()))


def dot(a, b, dims=NN):
    return lax.dot_general(
        a, b, dims, precision=lax.Precision.HIGHEST, preferred_element_type=F32
    )


def split(x):
    high = x.astype(jnp.bfloat16)
    return high, (x - high.astype(F32)).astype(jnp.bfloat16)


def dot_split(a, b, dims=NN):
    part = lambda x, y: lax.dot_general(x, y, dims, preferred_element_type=F32)
    return part(a[0], b[0]) + (part(a[0], b[1]) + part(a[1], b[0]))


def lane_splat(x, lane):
    return jnp.broadcast_to(x[:, lane : lane + 1], x.shape)


def row_splat(x, row):
    return jnp.broadcast_to(x[row : row + 1, :], x.shape)


def recip(x):
    return pl.reciprocal(x, approx=True)


def total(terms):
    while len(terms) > 1:
        terms = [terms[i] + terms[i + 1] for i in range(0, len(terms), 2)]
    return terms[0]


def factor_rows(rows):
    groups = len(rows)
    sub = lax.broadcasted_iota(jnp.int32, rows[0].shape, 0)
    lane = lax.broadcasted_iota(jnp.int32, rows[0].shape, 1)
    here = [sub == j for j in range(SUB)]
    unit = [jnp.where(h, 1.0, 0.0).astype(F32) for h in here]
    held = list(rows)
    out = []
    cols = [lane_splat(held[0], k) for k in range(SUB)]
    for b in range(groups):
        y = held[b]
        last = b + 1 == groups
        if not last:
            near = held[b + 1]
            side = [lane_splat(near, b * SUB + k) for k in range(SUB)]
            ahead = [lane_splat(near, (b + 1) * SUB + k) for k in range(SUB)]
        below = {g: [lane_splat(held[g], b * SUB + k) for k in range(SUB)] for g in range(b + 2, groups)}
        done = jnp.zeros_like(y)
        for j in range(0, SUB, 2):
            c0, c1 = cols[j], cols[j + 1]
            p, q, s = row_splat(c0, j), row_splat(c1, j), row_splat(c1, j + 1)
            r = recip(p * s - q * q)
            m0, m1 = c0 - unit[j], c1 - unit[j + 1]
            if j + 2 < SUB:
                v0, v1 = s * c0 - q * c1, p * c1 - q * c0
            for k in range(j + 2, SUB):
                n0, n1 = row_splat(v0, k), row_splat(v1, k)
                cols[k] = cols[k] - (m0 * n0 + m1 * n1) * r
                if not last:
                    side[k] = side[k] - (side[j] * n0 + side[j + 1] * n1) * r
            y0, y1 = row_splat(y, j), row_splat(y, j + 1)
            w0, w1 = (s * y0 - q * y1) * r, (p * y1 - q * y0) * r
            if not last:
                s0, s1 = side[j], side[j + 1]
                v0, v1 = s * s0 - q * s1, p * s1 - q * s0
                for k in range(SUB):
                    ahead[k] = ahead[k] - (s0 * row_splat(v0, k) + s1 * row_splat(v1, k)) * r
                near = near - (s0 * w0 + s1 * w1)
            y = y - (m0 * w0 + m1 * w1)
            root0 = lax.rsqrt(p)
            ratio = q * root0 * root0
            root1 = lax.rsqrt(s - q * ratio)
            done = jnp.where(here[j], y0 * root0, done)
            done = jnp.where(here[j + 1], (y1 - ratio * y0) * root1, done)
        out.append(jnp.where(lane >= sub + b * SUB, done, 0.0))
        if last:
            break
        held[b + 1] = near
        cols = ahead
        if below:
            yk = [row_splat(y, k) for k in range(SUB)]
        for g, c in below.items():
            held[g] = held[g] - total([c[k] * yk[k] for k in range(SUB)])
    return out


def tile_rows(tile):
    return [tile[g * SUB : (g + 1) * SUB, :] for g in range(tile.shape[0] // SUB)]


def factor(tile, lower_ref, inverse_ref, work):
    order = tile.shape[0]
    half = order // 2
    at_row = lax.broadcasted_iota(jnp.int32, tile.shape, 0)
    at_col = lax.broadcasted_iota(jnp.int32, tile.shape, 1)
    diagonal = jnp.sum(jnp.where(at_row == at_col, tile, 0.0), axis=0, keepdims=True)
    scale = jnp.broadcast_to(lax.rsqrt(diagonal), tile.shape)
    down = scale.T
    a = tile * scale * down
    one = jnp.where(at_row[:half, :half] == at_col[:half, :half], 1.0, 0.0).astype(F32)
    beside = jnp.where(at_row[:half] + half == at_col[:half], 1.0, 0.0).astype(F32)
    work[half:, :half] = a[half:, half:]
    work[half:, half:] = one
    first = jnp.concatenate(factor_rows(tile_rows(jnp.where(at_col[:half] < half, a[:half], beside))), axis=0)
    inverse0 = first[:, half:]
    under = dot(a[half:, :half], inverse0, NT)
    work[half:, :half] -= dot(under, under, NT)
    second = jnp.concatenate(factor_rows(tile_rows(work[half:, :])), axis=0)
    inverse1 = second[:, half:]
    inverse_ref[:half, :half] = inverse0 * scale[:half, :half]
    inverse_ref[:half, half:] = jnp.zeros((half, half), F32)
    inverse_ref[half:, :half] = -dot(inverse1, dot(under, inverse0)) * scale[half:, :half]
    inverse_ref[half:, half:] = inverse1 * scale[half:, half:]
    work[:half, :] = jnp.where(at_col[:half] < half, first, 0.0)
    work[half:, :half] = jnp.zeros((half, half), F32)
    work[half:, half:] = second[:, :half]
    up = recip(down)
    lower_ref[...] = work[...].T * up
    lower_ref[half:, :half] = under * up[half:, :half]


def pack_kernel(index_ref, source_ref, mine_ref, *refs):
    *send_refs, linear_ref, arrived = refs
    load = pltpu.make_async_copy(source_ref, linear_ref, arrived)
    load.start()
    layer = index_ref[0]
    first = (index_ref[1] == 0) & (index_ref[2] == 0)
    height, tile = mine_ref.shape
    load.wait()
    piece = linear_ref.shape[0] // (len(send_refs) + 1)

    @pl.when(first)
    def _():
        at_row = lax.broadcasted_iota(jnp.int32, (tile, tile), 0)
        at_col = lax.broadcasted_iota(jnp.int32, (tile, tile), 1)
        corner = linear_ref[pl.ds(2 * tile + 1, tile, 2), :]
        mixed = jnp.where(at_row >= at_col, linear_ref[pl.ds(0, tile, 2), :], corner)
        below = linear_ref[pl.ds(2 * tile, tile, 2), :]
        diagonal = jnp.sum(jnp.where(at_row == at_col, corner, 0.0), axis=0, keepdims=True)
        for ref in (mine_ref, *send_refs):
            ref[:tile, :] = mixed
            ref[tile : 2 * tile, :] = below
            ref[2 * tile :, :] = jnp.broadcast_to(diagonal, (height - 2 * tile, tile))

    @pl.when(jnp.logical_not(first))
    def _():
        for k, ref in enumerate((mine_ref, *send_refs)):
            start = pl.multiple_of((layer ^ k) * piece, piece)
            ref[:piece, :] = linear_ref[pl.ds(start, piece), :]
            ref[piece:, :] = jnp.zeros((height - piece, tile), F32)


def unpack(pieces, to_ref):
    tile = pieces[0].shape[1]
    slab = pieces[0].shape[0] // 2
    for t, piece in enumerate(pieces):
        to_ref[t * slab : (t + 1) * slab, :tile] = piece[pl.ds(0, slab, 2), :]
        to_ref[t * slab : (t + 1) * slab, tile:] = piece[pl.ds(1, slab, 2), :]


def symmetric(lower, keep):
    part = jnp.where(keep, lower, 0.0)
    at = lax.broadcasted_iota(jnp.int32, lower.shape, 0) == lax.broadcasted_iota(jnp.int32, lower.shape, 1)
    return part + jnp.where(at, 0.0, part).T


def first_kernel(packed_ref, block_ref, lower_ref, inverse_ref, left_ref, rest_ref, work):
    tile = packed_ref.shape[1]
    at_row = lax.broadcasted_iota(jnp.int32, (tile, tile), 0)
    at_col = lax.broadcasted_iota(jnp.int32, (tile, tile), 1)
    mixed = packed_ref[:tile, :]
    below = packed_ref[tile : 2 * tile, :]
    tile0 = symmetric(mixed, at_row >= at_col)
    upper1 = jnp.where(at_row < at_col, mixed, 0.0)
    diagonal = jnp.broadcast_to(packed_ref[2 * tile : 2 * tile + 1, :], (tile, tile))
    tile1 = upper1 + upper1.T + jnp.where(at_row == at_col, diagonal, 0.0)
    block_ref[:tile, :tile] = tile0
    block_ref[tile:, :tile] = below
    block_ref[:tile, tile:] = below.T
    block_ref[tile:, tile:] = tile1
    factor(tile0, lower_ref, inverse_ref, work)
    left = dot(below, inverse_ref[...], NT)
    left_ref[...] = left
    rest_ref[...] = tile1 - dot(left, left, NT)


def second_kernel(lower0_ref, inverse0_ref, left_ref, rest_ref, lower_ref, inverse_ref, work):
    tile = rest_ref.shape[0]
    zero = jnp.zeros((tile, tile), F32)
    first, second = slice(0, tile), slice(tile, 2 * tile)
    lower_ref[first, first] = lower0_ref[...]
    lower_ref[first, second] = zero
    lower_ref[second, first] = left_ref[...]
    inverse_ref[first, first] = inverse0_ref[...]
    inverse_ref[first, second] = zero
    factor(rest_ref[...], lower_ref.at[second, second], inverse_ref.at[second, second], work)
    inverse_ref[second, first] = -dot(inverse_ref[second, second], dot(left_ref[...], inverse0_ref[...]))


def third_kernel(
    corners_ref, belows_ref, inverse0_ref, left_ref, lower_ref, inverse_ref, cross_ref, corner_ref, below_ref, work,
):
    tile = work.shape[0]
    first, second = slice(0, tile), slice(tile, 2 * tile)
    zero = jnp.zeros((tile, tile), F32)
    unpack([belows_ref.at[t] for t in range(belows_ref.shape[0])], below_ref)
    unpack([corners_ref.at[t] for t in range(corners_ref.shape[0])], corner_ref)
    top = dot(below_ref[first, :], inverse0_ref[...], NT)
    factor(corner_ref[first, first] - dot(top, top, NT), lower_ref.at[first, first], inverse_ref.at[first, first], work)
    bottom = dot(below_ref[second, :], inverse0_ref[...], NT)
    left_ref[first, :] = top
    left_ref[second, :] = bottom
    ahead = corner_ref[second, first] - dot(bottom, top, NT)
    rest = corner_ref[second, second] - dot(bottom, bottom, NT)
    under = dot(ahead, inverse_ref[first, first], NT)
    lower_ref[first, second] = zero
    lower_ref[second, first] = under
    inverse_ref[first, second] = zero
    factor(rest - dot(under, under, NT), lower_ref.at[second, second], inverse_ref.at[second, second], work)
    inverse_ref[second, first] = -dot(inverse_ref[second, second], dot(under, inverse_ref[first, first]))
    cross_ref[...] = -dot(inverse_ref[...], dot(left_ref[...], inverse0_ref[...]))


def final_kernel(
    index_ref, keep_ref, own_ref, block_ref, rows_ref, col0_ref, col1_ref,
    lower0_ref, inverse0_ref, lower1_ref, inverse1_ref, left_ref, cross_ref,
    schur_ref, panels_ref, upper_ref, row_ref,
):
    layer, row, col = index_ref[0], index_ref[1], index_ref[2]
    width = upper_ref.shape[1]
    tiles_per = keep_ref.shape[0]
    tile = width // tiles_per
    slabs = rows_ref.shape[0]
    slab_rows = width // slabs

    @pl.when(row == 0)
    def _():
        panels_ref[0] = lower0_ref[...]
        panels_ref[1] = jnp.zeros((width, width), F32)

    @pl.when(row == 1)
    def _():
        panels_ref[0] = left_ref[...]
        panels_ref[1] = lower1_ref[...]

    @pl.when(row > 1)
    def _():
        for k in range(2):
            unpack([rows_ref.at[t, k] for t in range(slabs)], row_ref.at[k])
        f0, f1 = split(row_ref[0]), split(row_ref[1])
        panels_ref[0] = dot_split(f0, split(inverse0_ref[...]), NT)
        panels_ref[1] = dot_split(f0, split(cross_ref[...]), NT) + dot_split(f1, split(inverse1_ref[...]), NT)

    @pl.when(col == 0)
    def _():
        upper_ref[...] = jnp.zeros(upper_ref.shape, F32)

    @pl.when(col == 1)
    def _():
        upper_ref[:width, :] = left_ref[...].T
        upper_ref[width:, :] = jnp.zeros((width, width), F32)

    @pl.when(col > 1)
    def _():
        for k, ref in enumerate((col0_ref, col1_ref)):
            unpack([ref.at[t] for t in range(slabs)], row_ref.at[k])
        g0, g1 = split(row_ref[0]), split(row_ref[1])
        upper_ref[:width, :] = dot_split(split(inverse0_ref[...]), g0)
        upper_ref[width:, :] = dot_split(split(cross_ref[...]), g0) + dot_split(split(inverse1_ref[...]), g1)

    slab = pl.ds(pl.multiple_of(layer * slab_rows, slab_rows), slab_rows)
    product = dot_split(split(panels_ref[0, slab, :]), split(upper_ref[:width, :]))
    product += dot_split(split(panels_ref[1, slab, :]), split(upper_ref[width:, :]))
    at_row = (lax.broadcasted_iota(jnp.int32, (slab_rows, tile), 0) + layer * slab_rows) // tile
    for j in range(tiles_per):
        keep = jnp.zeros((slab_rows, tile), jnp.int32)
        for i in range(tiles_per):
            keep = jnp.where(at_row == i, keep_ref[i, j], keep)
        own = own_ref[pl.ds(j, slab_rows, tiles_per), :]
        at = slice(j * tile, (j + 1) * tile)
        own = jnp.where((row == 0) & (col == 0), block_ref[slab, at], own)
        schur_ref[pl.ds(j, slab_rows, tiles_per), :] = own - jnp.where(keep > 0, product[:, at], 0.0)


AXES = ("layer", "row", "col")


def trade(x, axis, k):
    return lax.ppermute(x, axis, [(i, i ^ k) for i in range(lax.axis_size(axis))])


def ask_layers(x):
    return [x] + [trade(x, "layer", k) for k in range(1, lax.axis_size("layer"))]


def in_order(parts, *late):
    layer = lax.axis_index("layer").astype(jnp.int32)
    parts = parts[:1] + [after(part, *late) for part in parts[1:]]
    ordered = []
    for t in range(len(parts)):
        held = parts[0]
        for k in range(1, len(parts)):
            held = jnp.where(layer ^ t == k, parts[k], held)
        ordered.append(held)
    return jnp.stack(ordered)


def strides(count, least):
    step = 1
    while 2 * step < count:
        step *= 2
    out = []
    while step >= least:
        out.append(step)
        step //= 2
    return out


def after(x, *others):
    return lax.optimization_barrier((x,) + others)[0]


def run(kernel, outs, ins, scratch=(), flops=0, name=None, smem=0, source=pltpu.VMEM):
    vmem = pl.BlockSpec(memory_space=pltpu.VMEM)
    ins_at = [pl.BlockSpec(memory_space=pltpu.SMEM)] * smem + [pl.BlockSpec(memory_space=source)] * (len(ins) - smem)
    return pl.pallas_call(
        kernel,
        out_shape=tuple(jax.ShapeDtypeStruct(s, F32) for s in outs),
        in_specs=ins_at,
        out_specs=tuple(vmem for _ in outs),
        scratch_shapes=[pltpu.VMEM(s, F32) if isinstance(s, tuple) else s for s in scratch],
        compiler_params=pltpu.CompilerParams(vmem_limit_bytes=24 * 1024 * 1024),
        cost_estimate=pl.CostEstimate(flops=flops, bytes_accessed=10**6, transcendentals=0),
        name=name,
    )(*ins)


def on_device(partials, pattern):
    layers, rows, cols = (lax.axis_size(a) for a in AXES)
    layer, row, col = (lax.axis_index(a).astype(jnp.int32) for a in AXES)
    width = partials.shape[3]
    tiles_per = pattern.shape[2]
    tile = width // tiles_per
    slab_rows = width // layers
    piece_rows = slab_rows * tiles_per
    height = 2 * tile + SUB
    even_row, even_col = row % 2 == 0, col % 2 == 0
    index = jnp.stack([layer, row, col])
    square, big = (tile, tile), (width, width)

    mine, *sends = run(
        pack_kernel,
        ((height, tile),) * layers,
        (index, pltpu.with_memory_space_constraint(partials.reshape(width * tiles_per, tile), pltpu.HBM)),
        scratch=((width * tiles_per, tile), pltpu.SemaphoreType.DMA),
        name="k0",
        smem=1,
        source=pltpu.HBM,
    )
    front = total([mine] + [trade(x, "layer", k + 1) for k, x in enumerate(sends)])
    piece = front[:piece_rows]

    keep = (pattern.reshape(tiles_per, tiles_per) > 0) | (row < 2) | (col < 2)
    keep = keep.astype(jnp.int32)
    fall = after(piece, keep)
    for s in strides(rows, 2):
        fall_from, fall_got = fall, trade(fall, "row", s)
        if s > 2:
            fall = jnp.where(row % (2 * s) >= s, fall_got, fall_from)

    lead = front
    for s in strides(cols, 2):
        lead = jnp.where(col % (2 * s) >= s, trade(lead, "col", s), lead)
    fall_got = after(fall_got, lead)
    lead = after(lead, fall_got)
    got = trade(lead, "col", 1)
    low, high = jnp.where(even_col, lead, got), jnp.where(even_col, got, lead)
    panels_in = jnp.stack([low[:piece_rows], high[:piece_rows]])
    high = high[:piece_rows]

    high = after(high, low)

    for s in strides(rows, 2):
        low = jnp.where(row % (2 * s) >= s, trade(low, "row", s), low)
    for s in strides(rows, 2):
        high_from, high_got = high, trade(high, "row", s)
        if s > 2:
            high = jnp.where(row % (2 * s) >= s, high_got, high_from)
    high = jnp.where(row % 4 >= 2, after(high_got, low), high_from)
    got = trade(low, "row", 1)
    packed = jnp.where(even_row, low, got)
    lead_parts = ask_layers(jnp.where(even_row, got[:piece_rows], high))
    fall = jnp.where(row % 4 >= 2, fall_got, fall_from)
    fall_parts = ask_layers(after(fall, lead_parts[0]))
    rows_in = ask_layers(after(panels_in, lead_parts[0]))
    packed = after(packed, high)

    block0, small_lower, small_inverse, left0, rest0 = run(
        first_kernel,
        (big, square, square, square, square),
        (packed,),
        scratch=(square,),
        flops=5 * 10**9,
        name="k1",
    )
    lead = in_order(lead_parts, rest0)
    lead_other = trade(lead, "row", 1)
    lower0, inverse0 = run(
        second_kernel,
        (big, big),
        (small_lower, small_inverse, left0, after(rest0, lead)),
        scratch=(square,),
        flops=5 * 10**9,
        name="k2",
    )
    lead_other = after(lead_other, inverse0)
    corners, belows = jnp.where(even_row, lead_other, lead), jnp.where(even_row, lead, lead_other)
    fall = in_order(fall_parts, inverse0)
    fall_other = trade(fall, "row", 1)
    left1, lower1, inverse1, cross = run(
        third_kernel,
        (big, big, big, big),
        (corners, belows, inverse0),
        scratch=(big, big, square),
        flops=10**10,
        name="k3",
    )
    rows_in, fall_other = in_order(rows_in, cross), after(fall_other, cross)
    col0, col1 = jnp.where(even_row, fall, fall_other), jnp.where(even_row, fall_other, fall)
    schur, panels = run(
        final_kernel,
        ((piece_rows, tile), (2, width, width)),
        (index, keep, piece, block0, rows_in, col0, col1, lower0, inverse0, lower1, inverse1, left1, cross),
        scratch=((2 * width, width), (2, width, width)),
        flops=10**9,
        name="kf",
        smem=2,
    )
    return (
        schur.reshape(1, 1, 1, slab_rows, 1, 1, width),
        panels.reshape(2, 1, 1, width, width),
    )


def solution(mesh):
    return jax.shard_map(
        on_device,
        mesh=mesh,
        in_specs=(
            P("layer", None, "row", None, None, "col", None),
            P(None, "row", None, None, "col", None),
        ),
        out_specs=(
            P(None, "row", "layer", None, None, "col", None),
            P(None, None, "row", None, None),
        ),
        check_vma=False,
    )
```

```python
import functools

import jax
import jax.numpy as jnp
from jax import lax
from jax.experimental import pallas as pl
from jax.experimental.pallas import tpu as pltpu
from jax.sharding import PartitionSpec as P

F32 = jnp.float32
SUB = 8
NT = (((1,), (1,)), ((), ()))
NN = (((1,), (0,)), ((), ()))


def dot(a, b, dims=NN):
    return lax.dot_general(
        a, b, dims, precision=lax.Precision.HIGHEST, preferred_element_type=F32
    )


def split(x):
    high = x.astype(jnp.bfloat16)
    return high, (x - high.astype(F32)).astype(jnp.bfloat16)


def dot_split(a, b, dims=NN):
    part = lambda x, y: lax.dot_general(x, y, dims, preferred_element_type=F32)
    return part(a[0], b[0]) + (part(a[0], b[1]) + part(a[1], b[0]))


def lane_splat(x, lane):
    return jnp.broadcast_to(x[:, lane : lane + 1], x.shape)


def row_splat(x, row):
    return jnp.broadcast_to(x[row : row + 1, :], x.shape)


def recip(x):
    return pl.reciprocal(x, approx=True)


def total(terms):
    while len(terms) > 1:
        terms = [terms[i] + terms[i + 1] for i in range(0, len(terms), 2)]
    return terms[0]


def factor_rows(rows):
    groups = len(rows)
    sub = lax.broadcasted_iota(jnp.int32, rows[0].shape, 0)
    lane = lax.broadcasted_iota(jnp.int32, rows[0].shape, 1)
    here = [sub == j for j in range(SUB)]
    unit = [jnp.where(h, 1.0, 0.0).astype(F32) for h in here]
    held = list(rows)
    out = []
    cols = [lane_splat(held[0], k) for k in range(SUB)]
    for b in range(groups):
        y = held[b]
        last = b + 1 == groups
        if not last:
            near = held[b + 1]
            side = [lane_splat(near, b * SUB + k) for k in range(SUB)]
            ahead = [lane_splat(near, (b + 1) * SUB + k) for k in range(SUB)]
        below = {g: [lane_splat(held[g], b * SUB + k) for k in range(SUB)] for g in range(b + 2, groups)}
        done = jnp.zeros_like(y)
        for j in range(0, SUB, 2):
            c0, c1 = cols[j], cols[j + 1]
            p, q, s = row_splat(c0, j), row_splat(c1, j), row_splat(c1, j + 1)
            r = recip(p * s - q * q)
            m0, m1 = c0 - unit[j], c1 - unit[j + 1]
            if j + 2 < SUB:
                v0, v1 = s * c0 - q * c1, p * c1 - q * c0
            for k in range(j + 2, SUB):
                n0, n1 = row_splat(v0, k), row_splat(v1, k)
                cols[k] = cols[k] - (m0 * n0 + m1 * n1) * r
                if not last:
                    side[k] = side[k] - (side[j] * n0 + side[j + 1] * n1) * r
            y0, y1 = row_splat(y, j), row_splat(y, j + 1)
            w0, w1 = (s * y0 - q * y1) * r, (p * y1 - q * y0) * r
            if not last:
                s0, s1 = side[j], side[j + 1]
                v0, v1 = s * s0 - q * s1, p * s1 - q * s0
                for k in range(SUB):
                    ahead[k] = ahead[k] - (s0 * row_splat(v0, k) + s1 * row_splat(v1, k)) * r
                near = near - (s0 * w0 + s1 * w1)
            y = y - (m0 * w0 + m1 * w1)
            root0 = lax.rsqrt(p)
            ratio = q * root0 * root0
            root1 = lax.rsqrt(s - q * ratio)
            done = jnp.where(here[j], y0 * root0, done)
            done = jnp.where(here[j + 1], (y1 - ratio * y0) * root1, done)
        out.append(jnp.where(lane >= sub + b * SUB, done, 0.0))
        if last:
            break
        held[b + 1] = near
        cols = ahead
        if below:
            yk = [row_splat(y, k) for k in range(SUB)]
        for g, c in below.items():
            held[g] = held[g] - total([c[k] * yk[k] for k in range(SUB)])
    return out


def tile_rows(tile):
    return [tile[g * SUB : (g + 1) * SUB, :] for g in range(tile.shape[0] // SUB)]


def factor(tile, turned_ref, inverse_ref, work):
    order = tile.shape[0]
    half = order // 2
    at_row = lax.broadcasted_iota(jnp.int32, tile.shape, 0)
    at_col = lax.broadcasted_iota(jnp.int32, tile.shape, 1)
    diagonal = jnp.sum(jnp.where(at_row == at_col, tile, 0.0), axis=0, keepdims=True)
    scale = jnp.broadcast_to(lax.rsqrt(diagonal), tile.shape)
    down = scale.T
    a = tile * scale * down
    one = jnp.where(at_row[:half, :half] == at_col[:half, :half], 1.0, 0.0).astype(F32)
    beside = jnp.where(at_row[:half] + half == at_col[:half], 1.0, 0.0).astype(F32)
    work[half:, :half] = a[half:, half:]
    work[half:, half:] = one
    first = jnp.concatenate(factor_rows(tile_rows(jnp.where(at_col[:half] < half, a[:half], beside))), axis=0)
    inverse0 = first[:, half:]
    under = dot(a[half:, :half], inverse0, NT)
    work[half:, :half] -= dot(under, under, NT)
    second = jnp.concatenate(factor_rows(tile_rows(work[half:, :])), axis=0)
    inverse1 = second[:, half:]
    inverse_ref[:half, :half] = inverse0 * scale[:half, :half]
    inverse_ref[:half, half:] = jnp.zeros((half, half), F32)
    inverse_ref[half:, :half] = -dot(inverse1, dot(under, inverse0)) * scale[half:, :half]
    inverse_ref[half:, half:] = inverse1 * scale[half:, half:]
    across, up = recip(scale), recip(down)
    turned_ref[:half, :half] = first[:, :half] * across[:half, :half]
    turned_ref[:half, half:] = jnp.zeros((half, half), F32)
    turned_ref[half:, :half] = under * up[half:, :half]
    turned_ref[half:, half:] = second[:, :half] * across[half:, half:]


def turn_back(from_ref, to_ref, tile):
    width = from_ref.shape[0]
    at_row = lax.broadcasted_iota(jnp.int32, (tile, tile), 0)
    at_col = lax.broadcasted_iota(jnp.int32, (tile, tile), 1)
    same = at_row // (tile // 2) == at_col // (tile // 2)
    to_ref[...] = from_ref[...]
    for t in range(0, width, tile):
        at = slice(t, t + tile)
        held = from_ref[at, at]
        to_ref[at, at] = jnp.where(same, held.T, held)


def pack_kernel(index_ref, source_ref, mine_ref, *refs):
    *send_refs, linear_ref, arrived = refs
    load = pltpu.make_async_copy(source_ref, linear_ref, arrived)
    load.start()
    layer = index_ref[0]
    first = (index_ref[1] == 0) & (index_ref[2] == 0)
    height, tile = mine_ref.shape
    load.wait()
    piece = linear_ref.shape[0] // (len(send_refs) + 1)

    @pl.when(first)
    def _():
        at_row = lax.broadcasted_iota(jnp.int32, (tile, tile), 0)
        at_col = lax.broadcasted_iota(jnp.int32, (tile, tile), 1)
        corner = linear_ref[pl.ds(2 * tile + 1, tile, 2), :]
        mixed = jnp.where(at_row >= at_col, linear_ref[pl.ds(0, tile, 2), :], corner)
        below = linear_ref[pl.ds(2 * tile, tile, 2), :]
        diagonal = jnp.sum(jnp.where(at_row == at_col, corner, 0.0), axis=0, keepdims=True)
        for ref in (mine_ref, *send_refs):
            ref[:tile, :] = mixed
            ref[tile : 2 * tile, :] = below
            ref[2 * tile :, :] = jnp.broadcast_to(diagonal, (height - 2 * tile, tile))

    @pl.when(jnp.logical_not(first))
    def _():
        for k, ref in enumerate((mine_ref, *send_refs)):
            start = pl.multiple_of((layer ^ k) * piece, piece)
            ref[:piece, :] = linear_ref[pl.ds(start, piece), :]
            ref[piece:, :] = jnp.zeros((height - piece, tile), F32)


def unpack(pieces, to_ref):
    tile = pieces[0].shape[1]
    slab = pieces[0].shape[0] // 2
    for t, piece in enumerate(pieces):
        to_ref[t * slab : (t + 1) * slab, :tile] = piece[pl.ds(0, slab, 2), :]
        to_ref[t * slab : (t + 1) * slab, tile:] = piece[pl.ds(1, slab, 2), :]


def symmetric(lower, keep):
    part = jnp.where(keep, lower, 0.0)
    at = lax.broadcasted_iota(jnp.int32, lower.shape, 0) == lax.broadcasted_iota(jnp.int32, lower.shape, 1)
    return part + jnp.where(at, 0.0, part).T


def open_packed(packed_ref):
    tile = packed_ref.shape[1]
    at_row = lax.broadcasted_iota(jnp.int32, (tile, tile), 0)
    at_col = lax.broadcasted_iota(jnp.int32, (tile, tile), 1)
    mixed = packed_ref[:tile, :]
    tile0 = symmetric(mixed, at_row >= at_col)
    upper1 = jnp.where(at_row < at_col, mixed, 0.0)
    diagonal = jnp.broadcast_to(packed_ref[2 * tile : 2 * tile + 1, :], (tile, tile))
    tile1 = upper1 + upper1.T + jnp.where(at_row == at_col, diagonal, 0.0)
    return tile0, packed_ref[tile : 2 * tile, :], tile1


def first_kernel(packed_ref, lower_ref, inverse_ref, left_ref, rest_ref, work):
    tile0, below, tile1 = open_packed(packed_ref)
    factor(tile0, lower_ref, inverse_ref, work)
    left = dot(below, inverse_ref[...], NT)
    left_ref[...] = left
    rest_ref[...] = tile1 - dot(left, left, NT)


def second_kernel(lower0_ref, inverse0_ref, left_ref, rest_ref, lower_ref, inverse_ref, work):
    tile = rest_ref.shape[0]
    zero = jnp.zeros((tile, tile), F32)
    first, second = slice(0, tile), slice(tile, 2 * tile)
    lower_ref[first, first] = lower0_ref[...]
    lower_ref[first, second] = zero
    lower_ref[second, first] = left_ref[...]
    inverse_ref[first, first] = inverse0_ref[...]
    inverse_ref[first, second] = zero
    factor(rest_ref[...], lower_ref.at[second, second], inverse_ref.at[second, second], work)
    inverse_ref[second, first] = -dot(inverse_ref[second, second], dot(left_ref[...], inverse0_ref[...]))


def third_kernel(
    corners_ref, belows_ref, inverse0_ref, left_ref, lower_ref, inverse_ref, cross_ref, corner_ref, below_ref, work,
):
    tile = work.shape[0]
    first, second = slice(0, tile), slice(tile, 2 * tile)
    zero = jnp.zeros((tile, tile), F32)
    unpack([belows_ref.at[t] for t in range(belows_ref.shape[0])], below_ref)
    unpack([corners_ref.at[t] for t in range(corners_ref.shape[0])], corner_ref)
    top = dot(below_ref[first, :], inverse0_ref[...], NT)
    factor(corner_ref[first, first] - dot(top, top, NT), lower_ref.at[first, first], inverse_ref.at[first, first], work)
    bottom = dot(below_ref[second, :], inverse0_ref[...], NT)
    left_ref[first, :] = top
    left_ref[second, :] = bottom
    ahead = corner_ref[second, first] - dot(bottom, top, NT)
    rest = corner_ref[second, second] - dot(bottom, bottom, NT)
    under = dot(ahead, inverse_ref[first, first], NT)
    lower_ref[first, second] = zero
    lower_ref[second, first] = under
    inverse_ref[first, second] = zero
    factor(rest - dot(under, under, NT), lower_ref.at[second, second], inverse_ref.at[second, second], work)
    corner = dot_split(split(under), split(inverse_ref[first, first]))
    inverse_ref[second, first] = -dot_split(split(inverse_ref[second, second]), split(corner))
    cross = dot_split(split(left_ref[...]), split(inverse0_ref[...]))
    cross_ref[...] = -dot_split(split(inverse_ref[...]), split(cross))


def final_kernel(
    index_ref, keep_ref, own_ref, packed_ref, rows_ref, col0_ref, col1_ref,
    lower0_ref, inverse0_ref, lower1_ref, inverse1_ref, left_ref, cross_ref,
    schur_ref, panels_ref, upper_ref, row_ref,
):
    layer, row, col = index_ref[0], index_ref[1], index_ref[2]
    width = upper_ref.shape[1]
    tiles_per = keep_ref.shape[0]
    tile = width // tiles_per
    slabs = rows_ref.shape[0]
    slab_rows = width // slabs

    @pl.when(row == 0)
    def _():
        turn_back(lower0_ref, panels_ref.at[0], tile)
        panels_ref[1] = jnp.zeros((width, width), F32)

    @pl.when(row == 1)
    def _():
        panels_ref[0] = left_ref[...]
        turn_back(lower1_ref, panels_ref.at[1], tile)

    @pl.when(row > 1)
    def _():
        for k in range(2):
            unpack([rows_ref.at[t, k] for t in range(slabs)], row_ref.at[k])
        f0, f1 = split(row_ref[0]), split(row_ref[1])
        panels_ref[0] = dot_split(f0, split(inverse0_ref[...]), NT)
        panels_ref[1] = dot_split(f0, split(cross_ref[...]), NT) + dot_split(f1, split(inverse1_ref[...]), NT)

    @pl.when(col == 0)
    def _():
        upper_ref[...] = jnp.zeros(upper_ref.shape, F32)

    @pl.when((row == 0) & (col == 0))
    def _():
        tile0, below, tile1 = open_packed(packed_ref)
        row_ref[0, :tile, :tile] = tile0
        row_ref[0, tile:, :tile] = below
        row_ref[0, :tile, tile:] = below.T
        row_ref[0, tile:, tile:] = tile1

    @pl.when(col == 1)
    def _():
        upper_ref[:width, :] = left_ref[...].T
        upper_ref[width:, :] = jnp.zeros((width, width), F32)

    @pl.when(col > 1)
    def _():
        for k, ref in enumerate((col0_ref, col1_ref)):
            unpack([ref.at[t] for t in range(slabs)], row_ref.at[k])
        g0, g1 = split(row_ref[0]), split(row_ref[1])
        upper_ref[:width, :] = dot_split(split(inverse0_ref[...]), g0)
        upper_ref[width:, :] = dot_split(split(cross_ref[...]), g0) + dot_split(split(inverse1_ref[...]), g1)

    slab = pl.ds(pl.multiple_of(layer * slab_rows, slab_rows), slab_rows)
    product = dot_split(split(panels_ref[0, slab, :]), split(upper_ref[:width, :]))
    product += dot_split(split(panels_ref[1, slab, :]), split(upper_ref[width:, :]))
    at_row = (lax.broadcasted_iota(jnp.int32, (slab_rows, tile), 0) + layer * slab_rows) // tile
    for j in range(tiles_per):
        keep = jnp.zeros((slab_rows, tile), jnp.int32)
        for i in range(tiles_per):
            keep = jnp.where(at_row == i, keep_ref[i, j], keep)
        own = own_ref[pl.ds(j, slab_rows, tiles_per), :]
        at = slice(j * tile, (j + 1) * tile)
        own = jnp.where((row == 0) & (col == 0), row_ref[0, slab, at], own)
        schur_ref[pl.ds(j, slab_rows, tiles_per), :] = own - jnp.where(keep > 0, product[:, at], 0.0)


AXES = ("layer", "row", "col")


def trade(x, axis, k):
    return lax.ppermute(x, axis, [(i, i ^ k) for i in range(lax.axis_size(axis))])


def ask_layers(x):
    return [x] + [trade(x, "layer", k) for k in range(1, lax.axis_size("layer"))]


def in_order(parts, *late):
    layer = lax.axis_index("layer").astype(jnp.int32)
    parts = parts[:1] + [after(part, *late) for part in parts[1:]]
    ordered = []
    for t in range(len(parts)):
        held = parts[0]
        for k in range(1, len(parts)):
            held = jnp.where(layer ^ t == k, parts[k], held)
        ordered.append(held)
    return jnp.stack(ordered)


def strides(count, least):
    step = 1
    while 2 * step < count:
        step *= 2
    out = []
    while step >= least:
        out.append(step)
        step //= 2
    return out


def after(x, *others):
    return lax.optimization_barrier((x,) + others)[0]


def run(kernel, outs, ins, scratch=(), flops=0, name=None, smem=0, source=pltpu.VMEM):
    vmem = pl.BlockSpec(memory_space=pltpu.VMEM)
    ins_at = [pl.BlockSpec(memory_space=pltpu.SMEM)] * smem + [pl.BlockSpec(memory_space=source)] * (len(ins) - smem)
    return pl.pallas_call(
        kernel,
        out_shape=tuple(jax.ShapeDtypeStruct(s, F32) for s in outs),
        in_specs=ins_at,
        out_specs=tuple(vmem for _ in outs),
        scratch_shapes=[pltpu.VMEM(s, F32) if isinstance(s, tuple) else s for s in scratch],
        compiler_params=pltpu.CompilerParams(vmem_limit_bytes=24 * 1024 * 1024),
        cost_estimate=pl.CostEstimate(flops=flops, bytes_accessed=10**6, transcendentals=0),
        name=name,
    )(*ins)


def on_device(partials, pattern):
    layers, rows, cols = (lax.axis_size(a) for a in AXES)
    layer, row, col = (lax.axis_index(a).astype(jnp.int32) for a in AXES)
    width = partials.shape[3]
    tiles_per = pattern.shape[2]
    tile = width // tiles_per
    slab_rows = width // layers
    piece_rows = slab_rows * tiles_per
    height = 2 * tile + SUB
    even_row, even_col = row % 2 == 0, col % 2 == 0
    index = jnp.stack([layer, row, col])
    square, big = (tile, tile), (width, width)

    mine, *sends = run(
        pack_kernel,
        ((height, tile),) * layers,
        (index, pltpu.with_memory_space_constraint(partials.reshape(width * tiles_per, tile), pltpu.HBM)),
        scratch=((width * tiles_per, tile), pltpu.SemaphoreType.DMA),
        name="k0",
        smem=1,
        source=pltpu.HBM,
    )
    front = total([mine] + [trade(x, "layer", k + 1) for k, x in enumerate(sends)])
    piece = front[:piece_rows]

    keep = (pattern.reshape(tiles_per, tiles_per) > 0) | (row < 2) | (col < 2)
    keep = keep.astype(jnp.int32)
    fall = after(piece, keep)
    for s in strides(rows, 2):
        fall_from, fall_got = fall, trade(fall, "row", s)
        if s > 2:
            fall = jnp.where(row % (2 * s) >= s, fall_got, fall_from)

    lead = front
    for s in strides(cols, 2):
        lead = jnp.where(col % (2 * s) >= s, trade(lead, "col", s), lead)
    fall_got = after(fall_got, lead)
    lead = after(lead, fall_got)
    got = trade(lead, "col", 1)
    fall_from, fall_got = after(fall_from, lead), after(fall_got, lead)
    fall = jnp.where(row % 4 >= 2, fall_got, fall_from)
    fall_parts = ask_layers(fall)
    low, high = jnp.where(even_col, lead, got), jnp.where(even_col, got, lead)
    panels_in = jnp.stack([low[:piece_rows], high[:piece_rows]])
    high = high[:piece_rows]

    high = after(high, low)

    for s in strides(rows, 2):
        low = jnp.where(row % (2 * s) >= s, trade(low, "row", s), low)
    for s in strides(rows, 2):
        high_from, high_got = high, trade(high, "row", s)
        if s > 2:
            high = jnp.where(row % (2 * s) >= s, high_got, high_from)
    high = jnp.where(row % 4 >= 2, after(high_got, low), high_from)
    got = trade(low, "row", 1)
    packed = jnp.where(even_row, low, got)
    lead_parts = ask_layers(jnp.where(even_row, got[:piece_rows], high))
    rows_in = ask_layers(after(panels_in, lead_parts[0]))
    packed = after(packed, high)

    small_lower, small_inverse, left0, rest0 = run(
        first_kernel,
        (square, square, square, square),
        (packed,),
        scratch=(square,),
        flops=5 * 10**9,
        name="k1",
    )
    lead = in_order(lead_parts, rest0)
    lead_other = trade(lead, "row", 1)
    lower0, inverse0 = run(
        second_kernel,
        (big, big),
        (small_lower, small_inverse, left0, after(rest0, lead)),
        scratch=(square,),
        flops=5 * 10**9,
        name="k2",
    )
    lead_other = after(lead_other, inverse0)
    corners, belows = jnp.where(even_row, lead_other, lead), jnp.where(even_row, lead, lead_other)
    fall = in_order(fall_parts, inverse0)
    fall_other = trade(fall, "row", 1)
    left1, lower1, inverse1, cross = run(
        third_kernel,
        (big, big, big, big),
        (corners, belows, inverse0),
        scratch=(big, big, square),
        flops=10**10,
        name="k3",
    )
    rows_in, fall_other = in_order(rows_in, cross), after(fall_other, cross)
    col0, col1 = jnp.where(even_row, fall, fall_other), jnp.where(even_row, fall_other, fall)
    schur, panels = run(
        final_kernel,
        ((piece_rows, tile), (2, width, width)),
        (index, keep, piece, packed, rows_in, col0, col1, lower0, inverse0, lower1, inverse1, left1, cross),
        scratch=((2 * width, width), (2, width, width)),
        flops=10**9,
        name="kf",
        smem=2,
    )
    return (
        schur.reshape(1, 1, 1, slab_rows, 1, 1, width),
        panels.reshape(2, 1, 1, width, width),
    )


def solution(mesh):
    return jax.shard_map(
        on_device,
        mesh=mesh,
        in_specs=(
            P("layer", None, "row", None, None, "col", None),
            P(None, "row", None, None, "col", None),
        ),
        out_specs=(
            P(None, "row", "layer", None, None, "col", None),
            P(None, None, "row", None, None),
        ),
        check_vma=False,
    )
```

```python
import functools

import jax
import jax.numpy as jnp
from jax import lax
from jax.experimental import pallas as pl
from jax.experimental.pallas import tpu as pltpu
from jax.sharding import PartitionSpec as P

F32 = jnp.float32
SUB = 8
NT = (((1,), (1,)), ((), ()))
NN = (((1,), (0,)), ((), ()))


def dot(a, b, dims=NN):
    return lax.dot_general(
        a, b, dims, precision=lax.Precision.HIGHEST, preferred_element_type=F32
    )


def split(x):
    high = x.astype(jnp.bfloat16)
    return high, (x - high.astype(F32)).astype(jnp.bfloat16)


def dot_split(a, b, dims=NN):
    part = lambda x, y: lax.dot_general(x, y, dims, preferred_element_type=F32)
    return part(a[0], b[0]) + (part(a[0], b[1]) + part(a[1], b[0]))


def lane_splat(x, lane):
    return jnp.broadcast_to(x[:, lane : lane + 1], x.shape)


def row_splat(x, row):
    return jnp.broadcast_to(x[row : row + 1, :], x.shape)


def recip(x):
    return pl.reciprocal(x, approx=True)


def total(terms):
    while len(terms) > 1:
        terms = [terms[i] + terms[i + 1] for i in range(0, len(terms), 2)]
    return terms[0]


def factor_rows(rows):
    groups = len(rows)
    sub = lax.broadcasted_iota(jnp.int32, rows[0].shape, 0)
    lane = lax.broadcasted_iota(jnp.int32, rows[0].shape, 1)
    here = [sub == j for j in range(SUB)]
    unit = [jnp.where(h, 1.0, 0.0).astype(F32) for h in here]
    held = list(rows)
    out = []
    cols = [lane_splat(held[0], k) for k in range(SUB)]
    for b in range(groups):
        y = held[b]
        last = b + 1 == groups
        if not last:
            near = held[b + 1]
            side = [lane_splat(near, b * SUB + k) for k in range(SUB)]
            ahead = [lane_splat(near, (b + 1) * SUB + k) for k in range(SUB)]
        below = {g: [lane_splat(held[g], b * SUB + k) for k in range(SUB)] for g in range(b + 2, groups)}
        done = jnp.zeros_like(y)
        for j in range(0, SUB, 2):
            c0, c1 = cols[j], cols[j + 1]
            p, q, s = row_splat(c0, j), row_splat(c1, j), row_splat(c1, j + 1)
            r = recip(p * s - q * q)
            m0, m1 = c0 - unit[j], c1 - unit[j + 1]
            if j + 2 < SUB:
                v0, v1 = s * c0 - q * c1, p * c1 - q * c0
            for k in range(j + 2, SUB):
                n0, n1 = row_splat(v0, k), row_splat(v1, k)
                cols[k] = cols[k] - (m0 * n0 + m1 * n1) * r
                if not last:
                    side[k] = side[k] - (side[j] * n0 + side[j + 1] * n1) * r
            y0, y1 = row_splat(y, j), row_splat(y, j + 1)
            w0, w1 = (s * y0 - q * y1) * r, (p * y1 - q * y0) * r
            if not last:
                s0, s1 = side[j], side[j + 1]
                v0, v1 = s * s0 - q * s1, p * s1 - q * s0
                for k in range(SUB):
                    ahead[k] = ahead[k] - (s0 * row_splat(v0, k) + s1 * row_splat(v1, k)) * r
                near = near - (s0 * w0 + s1 * w1)
            y = y - (m0 * w0 + m1 * w1)
            root0 = lax.rsqrt(p)
            ratio = q * root0 * root0
            root1 = lax.rsqrt(s - q * ratio)
            done = jnp.where(here[j], y0 * root0, done)
            done = jnp.where(here[j + 1], (y1 - ratio * y0) * root1, done)
        out.append(jnp.where(lane >= sub + b * SUB, done, 0.0))
        if last:
            break
        held[b + 1] = near
        cols = ahead
        if below:
            yk = [row_splat(y, k) for k in range(SUB)]
        for g, c in below.items():
            held[g] = held[g] - total([c[k] * yk[k] for k in range(SUB)])
    return out


def tile_rows(tile):
    return [tile[g * SUB : (g + 1) * SUB, :] for g in range(tile.shape[0] // SUB)]


def scales(tile):
    at_row = lax.broadcasted_iota(jnp.int32, tile.shape, 0)
    at_col = lax.broadcasted_iota(jnp.int32, tile.shape, 1)
    diagonal = jnp.sum(jnp.where(at_row == at_col, tile, 0.0), axis=0, keepdims=True)
    along = jnp.broadcast_to(lax.rsqrt(diagonal), tile.shape)
    return along, along.T


def factor(tile, along, down, turned_ref, inverse_ref, work):
    half = tile.shape[0] // 2
    at_row = lax.broadcasted_iota(jnp.int32, (half, 2 * half), 0)
    at_col = lax.broadcasted_iota(jnp.int32, (half, 2 * half), 1)
    a = tile * along * down
    one = jnp.where(at_row[:, :half] == at_col[:, :half], 1.0, 0.0).astype(F32)
    beside = jnp.where(at_row + half == at_col, 1.0, 0.0).astype(F32)
    work[:half, :half] = jnp.zeros((half, half), F32)
    work[:half, half:] = a[half:, :half]
    work[half:, :half] = a[half:, half:]
    work[half:, half:] = one
    first = jnp.concatenate(factor_rows(tile_rows(jnp.where(at_col < half, a[:half], beside))), axis=0)
    under = dot(work[:half, :], first, NT)
    work[half:, :half] -= dot(under, under, NT)
    second = jnp.concatenate(factor_rows(tile_rows(work[half:, :])), axis=0)
    inverse0, inverse1 = first[:, half:], second[:, half:]
    inverse_ref[:half, :half] = inverse0 * along[:half, :half]
    inverse_ref[:half, half:] = jnp.zeros((half, half), F32)
    inverse_ref[half:, :half] = -dot(inverse1, dot(under, inverse0)) * along[half:, :half]
    inverse_ref[half:, half:] = inverse1 * along[half:, half:]
    across, up = recip(along), recip(down)
    turned_ref[:half, :half] = first[:, :half] * across[:half, :half]
    turned_ref[:half, half:] = jnp.zeros((half, half), F32)
    turned_ref[half:, :half] = under * up[half:, :half]
    turned_ref[half:, half:] = second[:, :half] * across[half:, half:]


def turn_back(from_ref, to_ref, tile):
    width = from_ref.shape[0]
    at_row = lax.broadcasted_iota(jnp.int32, (tile, tile), 0)
    at_col = lax.broadcasted_iota(jnp.int32, (tile, tile), 1)
    same = at_row // (tile // 2) == at_col // (tile // 2)
    to_ref[...] = from_ref[...]
    for t in range(0, width, tile):
        at = slice(t, t + tile)
        held = from_ref[at, at]
        to_ref[at, at] = jnp.where(same, held.T, held)


def pack_kernel(index_ref, source_ref, mine_ref, *refs):
    *send_refs, linear_ref, arrived = refs
    load = pltpu.make_async_copy(source_ref, linear_ref, arrived)
    load.start()
    layer = index_ref[0]
    first = (index_ref[1] == 0) & (index_ref[2] == 0)
    height, tile = mine_ref.shape
    load.wait()
    piece = linear_ref.shape[0] // (len(send_refs) + 1)

    @pl.when(first)
    def _():
        at_row = lax.broadcasted_iota(jnp.int32, (tile, tile), 0)
        at_col = lax.broadcasted_iota(jnp.int32, (tile, tile), 1)
        corner = linear_ref[pl.ds(2 * tile + 1, tile, 2), :]
        mixed = jnp.where(at_row >= at_col, linear_ref[pl.ds(0, tile, 2), :], corner)
        below = linear_ref[pl.ds(2 * tile, tile, 2), :]
        diagonal = jnp.sum(jnp.where(at_row == at_col, corner, 0.0), axis=0, keepdims=True)
        for ref in (mine_ref, *send_refs):
            ref[:tile, :] = mixed
            ref[tile : 2 * tile, :] = below
            ref[2 * tile :, :] = jnp.broadcast_to(diagonal, (height - 2 * tile, tile))

    @pl.when(jnp.logical_not(first))
    def _():
        for k, ref in enumerate((mine_ref, *send_refs)):
            start = pl.multiple_of((layer ^ k) * piece, piece)
            ref[:piece, :] = linear_ref[pl.ds(start, piece), :]
            ref[piece:, :] = jnp.zeros((height - piece, tile), F32)


def unpack(pieces, to_ref):
    tile = pieces[0].shape[1]
    slab = pieces[0].shape[0] // 2
    for t, piece in enumerate(pieces):
        to_ref[t * slab : (t + 1) * slab, :tile] = piece[pl.ds(0, slab, 2), :]
        to_ref[t * slab : (t + 1) * slab, tile:] = piece[pl.ds(1, slab, 2), :]


def symmetric(lower, keep):
    part = jnp.where(keep, lower, 0.0)
    at = lax.broadcasted_iota(jnp.int32, lower.shape, 0) == lax.broadcasted_iota(jnp.int32, lower.shape, 1)
    return part + jnp.where(at, 0.0, part).T


def open_packed(packed_ref):
    tile = packed_ref.shape[1]
    at_row = lax.broadcasted_iota(jnp.int32, (tile, tile), 0)
    at_col = lax.broadcasted_iota(jnp.int32, (tile, tile), 1)
    mixed = packed_ref[:tile, :]
    tile0 = symmetric(mixed, at_row >= at_col)
    upper1 = jnp.where(at_row < at_col, mixed, 0.0)
    diagonal = jnp.broadcast_to(packed_ref[2 * tile : 2 * tile + 1, :], (tile, tile))
    tile1 = upper1 + upper1.T + jnp.where(at_row == at_col, diagonal, 0.0)
    return tile0, packed_ref[tile : 2 * tile, :], tile1


def first_kernel(packed_ref, lower_ref, inverse_ref, left_ref, rest_ref, along_ref, down_ref, work):
    tile0, below, tile1 = open_packed(packed_ref)
    along, down = scales(tile1)
    along_ref[...] = along
    down_ref[...] = down
    factor(tile0, *scales(tile0), lower_ref, inverse_ref, work)
    left = dot(below, inverse_ref[...], NT)
    left_ref[...] = left
    rest_ref[...] = tile1 - dot(left, left, NT)


def second_kernel(
    lower0_ref, inverse0_ref, left_ref, rest_ref, along_ref, down_ref, lower_ref, inverse_ref, work
):
    tile = rest_ref.shape[0]
    zero = jnp.zeros((tile, tile), F32)
    first, second = slice(0, tile), slice(tile, 2 * tile)
    lower_ref[first, first] = lower0_ref[...]
    lower_ref[first, second] = zero
    lower_ref[second, first] = left_ref[...]
    inverse_ref[first, first] = inverse0_ref[...]
    inverse_ref[first, second] = zero
    factor(
        rest_ref[...], along_ref[...], down_ref[...], lower_ref.at[second, second], inverse_ref.at[second, second], work
    )
    inverse_ref[second, first] = -dot(inverse_ref[second, second], dot(left_ref[...], inverse0_ref[...]))


def third_kernel(
    corners_ref, belows_ref, inverse0_ref, left_ref, lower_ref, inverse_ref, cross_ref, corner_ref, below_ref, work,
):
    tile = work.shape[0]
    first, second = slice(0, tile), slice(tile, 2 * tile)
    zero = jnp.zeros((tile, tile), F32)
    unpack([belows_ref.at[t] for t in range(belows_ref.shape[0])], below_ref)
    unpack([corners_ref.at[t] for t in range(corners_ref.shape[0])], corner_ref)
    scales0, scales1 = scales(corner_ref[first, first]), scales(corner_ref[second, second])
    top = dot(below_ref[first, :], inverse0_ref[...], NT)
    factor(
        corner_ref[first, first] - dot(top, top, NT),
        *scales0, lower_ref.at[first, first], inverse_ref.at[first, first], work,
    )
    bottom = dot(below_ref[second, :], inverse0_ref[...], NT)
    left_ref[first, :] = top
    left_ref[second, :] = bottom
    ahead = corner_ref[second, first] - dot(bottom, top, NT)
    rest = corner_ref[second, second] - dot(bottom, bottom, NT)
    under = dot(ahead, inverse_ref[first, first], NT)
    lower_ref[first, second] = zero
    lower_ref[second, first] = under
    inverse_ref[first, second] = zero
    factor(
        rest - dot(under, under, NT),
        *scales1, lower_ref.at[second, second], inverse_ref.at[second, second], work,
    )
    corner = dot_split(split(under), split(inverse_ref[first, first]))
    inverse_ref[second, first] = -dot_split(split(inverse_ref[second, second]), split(corner))
    cross = dot_split(split(left_ref[...]), split(inverse0_ref[...]))
    cross_ref[...] = -dot_split(split(inverse_ref[...]), split(cross))


def final_kernel(
    index_ref, keep_ref, own_ref, packed_ref, rows_ref, col0_ref, col1_ref,
    lower0_ref, inverse0_ref, lower1_ref, inverse1_ref, left_ref, cross_ref,
    schur_ref, panels_ref, upper_ref, row_ref,
):
    layer, row, col = index_ref[0], index_ref[1], index_ref[2]
    width = upper_ref.shape[1]
    tiles_per = keep_ref.shape[0]
    tile = width // tiles_per
    slabs = rows_ref.shape[0]
    slab_rows = width // slabs

    @pl.when(row == 0)
    def _():
        turn_back(lower0_ref, panels_ref.at[0], tile)
        panels_ref[1] = jnp.zeros((width, width), F32)

    @pl.when(row == 1)
    def _():
        panels_ref[0] = left_ref[...]
        turn_back(lower1_ref, panels_ref.at[1], tile)

    @pl.when(row > 1)
    def _():
        for k in range(2):
            unpack([rows_ref.at[t, k] for t in range(slabs)], row_ref.at[k])
        f0, f1 = split(row_ref[0]), split(row_ref[1])
        panels_ref[0] = dot_split(f0, split(inverse0_ref[...]), NT)
        panels_ref[1] = dot_split(f0, split(cross_ref[...]), NT) + dot_split(f1, split(inverse1_ref[...]), NT)

    @pl.when(col == 0)
    def _():
        upper_ref[...] = jnp.zeros(upper_ref.shape, F32)

    @pl.when((row == 0) & (col == 0))
    def _():
        tile0, below, tile1 = open_packed(packed_ref)
        row_ref[0, :tile, :tile] = tile0
        row_ref[0, tile:, :tile] = below
        row_ref[0, :tile, tile:] = below.T
        row_ref[0, tile:, tile:] = tile1

    @pl.when(col == 1)
    def _():
        upper_ref[:width, :] = left_ref[...].T
        upper_ref[width:, :] = jnp.zeros((width, width), F32)

    @pl.when(col > 1)
    def _():
        for k, ref in enumerate((col0_ref, col1_ref)):
            unpack([ref.at[t] for t in range(slabs)], row_ref.at[k])
        g0, g1 = split(row_ref[0]), split(row_ref[1])
        upper_ref[:width, :] = dot_split(split(inverse0_ref[...]), g0)
        upper_ref[width:, :] = dot_split(split(cross_ref[...]), g0) + dot_split(split(inverse1_ref[...]), g1)

    slab = pl.ds(pl.multiple_of(layer * slab_rows, slab_rows), slab_rows)
    product = dot_split(split(panels_ref[0, slab, :]), split(upper_ref[:width, :]))
    product += dot_split(split(panels_ref[1, slab, :]), split(upper_ref[width:, :]))
    at_row = (lax.broadcasted_iota(jnp.int32, (slab_rows, tile), 0) + layer * slab_rows) // tile
    for j in range(tiles_per):
        keep = jnp.zeros((slab_rows, tile), jnp.int32)
        for i in range(tiles_per):
            keep = jnp.where(at_row == i, keep_ref[i, j], keep)
        own = own_ref[pl.ds(j, slab_rows, tiles_per), :]
        at = slice(j * tile, (j + 1) * tile)
        own = jnp.where((row == 0) & (col == 0), row_ref[0, slab, at], own)
        schur_ref[pl.ds(j, slab_rows, tiles_per), :] = own - jnp.where(keep > 0, product[:, at], 0.0)


AXES = ("layer", "row", "col")


def trade(x, axis, k):
    return lax.ppermute(x, axis, [(i, i ^ k) for i in range(lax.axis_size(axis))])


def ask_layers(x):
    return [x] + [trade(x, "layer", k) for k in range(1, lax.axis_size("layer"))]


def in_order(parts, *late):
    layer = lax.axis_index("layer").astype(jnp.int32)
    parts = parts[:1] + [after(part, *late) for part in parts[1:]]
    ordered = []
    for t in range(len(parts)):
        held = parts[0]
        for k in range(1, len(parts)):
            held = jnp.where(layer ^ t == k, parts[k], held)
        ordered.append(held)
    return jnp.stack(ordered)


def strides(count, least):
    step = 1
    while 2 * step < count:
        step *= 2
    out = []
    while step >= least:
        out.append(step)
        step //= 2
    return out


def after(x, *others):
    return lax.optimization_barrier((x,) + others)[0]


def run(kernel, outs, ins, scratch=(), flops=0, name=None, smem=0, source=pltpu.VMEM):
    vmem = pl.BlockSpec(memory_space=pltpu.VMEM)
    ins_at = [pl.BlockSpec(memory_space=pltpu.SMEM)] * smem + [pl.BlockSpec(memory_space=source)] * (len(ins) - smem)
    return pl.pallas_call(
        kernel,
        out_shape=tuple(jax.ShapeDtypeStruct(s, F32) for s in outs),
        in_specs=ins_at,
        out_specs=tuple(vmem for _ in outs),
        scratch_shapes=[pltpu.VMEM(s, F32) if isinstance(s, tuple) else s for s in scratch],
        compiler_params=pltpu.CompilerParams(vmem_limit_bytes=24 * 1024 * 1024),
        cost_estimate=pl.CostEstimate(flops=flops, bytes_accessed=10**6, transcendentals=0),
        name=name,
    )(*ins)


def on_device(partials, pattern):
    layers, rows, cols = (lax.axis_size(a) for a in AXES)
    layer, row, col = (lax.axis_index(a).astype(jnp.int32) for a in AXES)
    width = partials.shape[3]
    tiles_per = pattern.shape[2]
    tile = width // tiles_per
    slab_rows = width // layers
    piece_rows = slab_rows * tiles_per
    height = 2 * tile + SUB
    even_row, even_col = row % 2 == 0, col % 2 == 0
    index = jnp.stack([layer, row, col])
    square, big = (tile, tile), (width, width)

    mine, *sends = run(
        pack_kernel,
        ((height, tile),) * layers,
        (index, pltpu.with_memory_space_constraint(partials.reshape(width * tiles_per, tile), pltpu.HBM)),
        scratch=((width * tiles_per, tile), pltpu.SemaphoreType.DMA),
        name="k0",
        smem=1,
        source=pltpu.HBM,
    )
    front = total([mine] + [trade(x, "layer", k + 1) for k, x in enumerate(sends)])
    piece = front[:piece_rows]

    keep = (pattern.reshape(tiles_per, tiles_per) > 0) | (row < 2) | (col < 2)
    keep = keep.astype(jnp.int32)
    fall = after(piece, keep)
    for s in strides(rows, 2):
        fall_from, fall_got = fall, trade(fall, "row", s)
        if s > 2:
            fall = jnp.where(row % (2 * s) >= s, fall_got, fall_from)

    lead = front
    for s in strides(cols, 2):
        lead = jnp.where(col % (2 * s) >= s, trade(lead, "col", s), lead)
    fall_got = after(fall_got, lead)
    lead = after(lead, fall_got)
    got = trade(lead, "col", 1)
    fall_from, fall_got = after(fall_from, lead), after(fall_got, lead)
    fall = jnp.where(row % 4 >= 2, fall_got, fall_from)
    fall_parts = ask_layers(fall)
    low, high = jnp.where(even_col, lead, got), jnp.where(even_col, got, lead)
    panels_in = jnp.stack([low[:piece_rows], high[:piece_rows]])
    high = high[:piece_rows]

    high = after(high, low)

    for s in strides(rows, 2):
        low = jnp.where(row % (2 * s) >= s, trade(low, "row", s), low)
    for s in strides(rows, 2):
        high_from, high_got = high, trade(high, "row", s)
        if s > 2:
            high = jnp.where(row % (2 * s) >= s, high_got, high_from)
    high = jnp.where(row % 4 >= 2, after(high_got, low), high_from)
    got = trade(low, "row", 1)
    packed = jnp.where(even_row, low, got)
    lead_parts = ask_layers(jnp.where(even_row, got[:piece_rows], high))
    rows_in = ask_layers(after(panels_in, lead_parts[0]))
    packed = after(packed, high)

    small_lower, small_inverse, left0, rest0, *scales0 = run(
        first_kernel,
        (square,) * 6,
        (packed,),
        scratch=(square,),
        flops=5 * 10**9,
        name="k1",
    )
    lead = in_order(lead_parts, rest0)
    lead_other = trade(lead, "row", 1)
    lower0, inverse0 = run(
        second_kernel,
        (big, big),
        (small_lower, small_inverse, left0, after(rest0, lead), *scales0),
        scratch=(square,),
        flops=5 * 10**9,
        name="k2",
    )
    lead_other = after(lead_other, inverse0)
    corners, belows = jnp.where(even_row, lead_other, lead), jnp.where(even_row, lead, lead_other)
    fall = in_order(fall_parts, inverse0)
    fall_other = trade(fall, "row", 1)
    left1, lower1, inverse1, cross = run(
        third_kernel,
        (big, big, big, big),
        (corners, belows, inverse0),
        scratch=(big, big, square),
        flops=10**10,
        name="k3",
    )
    rows_in, fall_other = in_order(rows_in, cross), after(fall_other, cross)
    col0, col1 = jnp.where(even_row, fall, fall_other), jnp.where(even_row, fall_other, fall)
    schur, panels = run(
        final_kernel,
        ((piece_rows, tile), (2, width, width)),
        (index, keep, piece, packed, rows_in, col0, col1, lower0, inverse0, lower1, inverse1, left1, cross),
        scratch=((2 * width, width), (2, width, width)),
        flops=10**9,
        name="kf",
        smem=2,
    )
    return (
        schur.reshape(1, 1, 1, slab_rows, 1, 1, width),
        panels.reshape(2, 1, 1, width, width),
    )


def solution(mesh):
    return jax.shard_map(
        on_device,
        mesh=mesh,
        in_specs=(
            P("layer", None, "row", None, None, "col", None),
            P(None, "row", None, None, "col", None),
        ),
        out_specs=(
            P(None, "row", "layer", None, None, "col", None),
            P(None, None, "row", None, None),
        ),
        check_vma=False,
    )
```

```python
import functools

import jax
import jax.numpy as jnp
from jax import lax
from jax.experimental import pallas as pl
from jax.experimental.pallas import tpu as pltpu
from jax.sharding import PartitionSpec as P

F32 = jnp.float32
SUB = 8
NT = (((1,), (1,)), ((), ()))
NN = (((1,), (0,)), ((), ()))


def dot(a, b, dims=NN):
    return lax.dot_general(
        a, b, dims, precision=lax.Precision.HIGHEST, preferred_element_type=F32
    )


def split(x):
    high = x.astype(jnp.bfloat16)
    return high, (x - high.astype(F32)).astype(jnp.bfloat16)


def dot_split(a, b, dims=NN):
    part = lambda x, y: lax.dot_general(x, y, dims, preferred_element_type=F32)
    return part(a[0], b[0]) + (part(a[0], b[1]) + part(a[1], b[0]))


def lane_splat(x, lane):
    return jnp.broadcast_to(x[:, lane : lane + 1], x.shape)


def row_splat(x, row):
    return jnp.broadcast_to(x[row : row + 1, :], x.shape)


def recip(x):
    return pl.reciprocal(x, approx=True)


def total(terms):
    while len(terms) > 1:
        terms = [terms[i] + terms[i + 1] for i in range(0, len(terms), 2)]
    return terms[0]


def factor_rows(rows):
    groups = len(rows)
    sub = lax.broadcasted_iota(jnp.int32, rows[0].shape, 0)
    lane = lax.broadcasted_iota(jnp.int32, rows[0].shape, 1)
    here = [sub == j for j in range(SUB)]
    unit = [jnp.where(h, 1.0, 0.0).astype(F32) for h in here]
    held = list(rows)
    out = []
    cols = [lane_splat(held[0], k) for k in range(SUB)]
    for b in range(groups):
        y = held[b]
        last = b + 1 == groups
        if not last:
            near = held[b + 1]
            side = [lane_splat(near, b * SUB + k) for k in range(SUB)]
            ahead = [lane_splat(near, (b + 1) * SUB + k) for k in range(SUB)]
        below = {g: [lane_splat(held[g], b * SUB + k) for k in range(SUB)] for g in range(b + 2, groups)}
        done = jnp.zeros_like(y)
        for j in range(0, SUB, 2):
            c0, c1 = cols[j], cols[j + 1]
            p, q, s = row_splat(c0, j), row_splat(c1, j), row_splat(c1, j + 1)
            r = recip(p * s - q * q)
            m0, m1 = c0 - unit[j], c1 - unit[j + 1]
            if j + 2 < SUB:
                v0, v1 = s * c0 - q * c1, p * c1 - q * c0
            for k in range(j + 2, SUB):
                n0, n1 = row_splat(v0, k), row_splat(v1, k)
                cols[k] = cols[k] - (m0 * n0 + m1 * n1) * r
                if not last:
                    side[k] = side[k] - (side[j] * n0 + side[j + 1] * n1) * r
            y0, y1 = row_splat(y, j), row_splat(y, j + 1)
            w0, w1 = (s * y0 - q * y1) * r, (p * y1 - q * y0) * r
            if not last:
                s0, s1 = side[j], side[j + 1]
                v0, v1 = s * s0 - q * s1, p * s1 - q * s0
                for k in range(SUB):
                    ahead[k] = ahead[k] - (s0 * row_splat(v0, k) + s1 * row_splat(v1, k)) * r
                near = near - (s0 * w0 + s1 * w1)
            y = y - (m0 * w0 + m1 * w1)
            root0 = lax.rsqrt(p)
            ratio = q * root0 * root0
            root1 = lax.rsqrt(s - q * ratio)
            done = jnp.where(here[j], y0 * root0, done)
            done = jnp.where(here[j + 1], (y1 - ratio * y0) * root1, done)
        out.append(jnp.where(lane >= sub + b * SUB, done, 0.0))
        if last:
            break
        held[b + 1] = near
        cols = ahead
        if below:
            yk = [row_splat(y, k) for k in range(SUB)]
        for g, c in below.items():
            held[g] = held[g] - total([c[k] * yk[k] for k in range(SUB)])
    return out


def tile_rows(tile):
    return [tile[g * SUB : (g + 1) * SUB, :] for g in range(tile.shape[0] // SUB)]


def scales(tile):
    at_row = lax.broadcasted_iota(jnp.int32, tile.shape, 0)
    at_col = lax.broadcasted_iota(jnp.int32, tile.shape, 1)
    diagonal = jnp.sum(jnp.where(at_row == at_col, tile, 0.0), axis=0, keepdims=True)
    along = jnp.broadcast_to(lax.rsqrt(diagonal), tile.shape)
    return along, along.T


def factor(tile, along, down, turned_ref, inverse_ref, work):
    half = tile.shape[0] // 2
    at_row = lax.broadcasted_iota(jnp.int32, (half, 2 * half), 0)
    at_col = lax.broadcasted_iota(jnp.int32, (half, 2 * half), 1)
    a = tile * along * down
    one = jnp.where(at_row[:, :half] == at_col[:, :half], 1.0, 0.0).astype(F32)
    beside = jnp.where(at_row + half == at_col, 1.0, 0.0).astype(F32)
    work[:half, :half] = jnp.zeros((half, half), F32)
    work[:half, half:] = a[half:, :half]
    work[half:, :half] = a[half:, half:]
    work[half:, half:] = one
    first = jnp.concatenate(factor_rows(tile_rows(jnp.where(at_col < half, a[:half], beside))), axis=0)
    under = dot(work[:half, :], first, NT)
    work[half:, :half] -= dot(under, under, NT)
    second = jnp.concatenate(factor_rows(tile_rows(work[half:, :])), axis=0)
    inverse0, inverse1 = first[:, half:], second[:, half:]
    inverse_ref[:half, :half] = inverse0 * along[:half, :half]
    inverse_ref[:half, half:] = jnp.zeros((half, half), F32)
    inverse_ref[half:, :half] = -dot(inverse1, dot(under, inverse0)) * along[half:, :half]
    inverse_ref[half:, half:] = inverse1 * along[half:, half:]
    across, up = recip(along), recip(down)
    turned_ref[:half, :half] = first[:, :half] * across[:half, :half]
    turned_ref[:half, half:] = jnp.zeros((half, half), F32)
    turned_ref[half:, :half] = under * up[half:, :half]
    turned_ref[half:, half:] = second[:, :half] * across[half:, half:]


def turn_back(from_ref, to_ref, tile):
    width = from_ref.shape[0]
    at_row = lax.broadcasted_iota(jnp.int32, (tile, tile), 0)
    at_col = lax.broadcasted_iota(jnp.int32, (tile, tile), 1)
    same = at_row // (tile // 2) == at_col // (tile // 2)
    to_ref[...] = from_ref[...]
    for t in range(0, width, tile):
        at = slice(t, t + tile)
        held = from_ref[at, at]
        to_ref[at, at] = jnp.where(same, held.T, held)


def pack_kernel(index_ref, source_ref, mine_ref, *refs):
    *send_refs, linear_ref, arrived = refs
    load = pltpu.make_async_copy(source_ref, linear_ref, arrived)
    load.start()
    layer = index_ref[0]
    first = (index_ref[1] == 0) & (index_ref[2] == 0)
    height, tile = mine_ref.shape
    load.wait()
    piece = linear_ref.shape[0] // (len(send_refs) + 1)

    @pl.when(first)
    def _():
        at_row = lax.broadcasted_iota(jnp.int32, (tile, tile), 0)
        at_col = lax.broadcasted_iota(jnp.int32, (tile, tile), 1)
        corner = linear_ref[pl.ds(2 * tile + 1, tile, 2), :]
        mixed = jnp.where(at_row >= at_col, linear_ref[pl.ds(0, tile, 2), :], corner)
        below = linear_ref[pl.ds(2 * tile, tile, 2), :]
        diagonal = jnp.sum(jnp.where(at_row == at_col, corner, 0.0), axis=0, keepdims=True)
        for ref in (mine_ref, *send_refs):
            ref[:tile, :] = mixed
            ref[tile : 2 * tile, :] = below
            ref[2 * tile :, :] = jnp.broadcast_to(diagonal, (height - 2 * tile, tile))

    @pl.when(jnp.logical_not(first))
    def _():
        for k, ref in enumerate((mine_ref, *send_refs)):
            start = pl.multiple_of((layer ^ k) * piece, piece)
            ref[:piece, :] = linear_ref[pl.ds(start, piece), :]
            ref[piece:, :] = jnp.zeros((height - piece, tile), F32)


def unpack(pieces, to_ref):
    tile = pieces[0].shape[1]
    slab = pieces[0].shape[0] // 2
    for t, piece in enumerate(pieces):
        to_ref[t * slab : (t + 1) * slab, :tile] = piece[pl.ds(0, slab, 2), :]
        to_ref[t * slab : (t + 1) * slab, tile:] = piece[pl.ds(1, slab, 2), :]


def symmetric(lower, keep):
    part = jnp.where(keep, lower, 0.0)
    at = lax.broadcasted_iota(jnp.int32, lower.shape, 0) == lax.broadcasted_iota(jnp.int32, lower.shape, 1)
    return part + jnp.where(at, 0.0, part).T


def open_packed(packed_ref):
    tile = packed_ref.shape[1]
    at_row = lax.broadcasted_iota(jnp.int32, (tile, tile), 0)
    at_col = lax.broadcasted_iota(jnp.int32, (tile, tile), 1)
    mixed = packed_ref[:tile, :]
    tile0 = symmetric(mixed, at_row >= at_col)
    upper1 = jnp.where(at_row < at_col, mixed, 0.0)
    diagonal = jnp.broadcast_to(packed_ref[2 * tile : 2 * tile + 1, :], (tile, tile))
    tile1 = upper1 + upper1.T + jnp.where(at_row == at_col, diagonal, 0.0)
    return tile0, packed_ref[tile : 2 * tile, :], tile1


def first_kernel(packed_ref, lower_ref, inverse_ref, left_ref, rest_ref, along_ref, down_ref, work):
    tile0, below, tile1 = open_packed(packed_ref)
    along, down = scales(tile1)
    along_ref[...] = along
    down_ref[...] = down
    factor(tile0, *scales(tile0), lower_ref, inverse_ref, work)
    left = dot(below, inverse_ref[...], NT)
    left_ref[...] = left
    rest_ref[...] = tile1 - dot(left, left, NT)


def second_kernel(
    lower0_ref, inverse0_ref, left_ref, rest_ref, along_ref, down_ref, lower_ref, inverse_ref, work
):
    tile = rest_ref.shape[0]
    zero = jnp.zeros((tile, tile), F32)
    first, second = slice(0, tile), slice(tile, 2 * tile)
    lower_ref[first, first] = lower0_ref[...]
    lower_ref[first, second] = zero
    lower_ref[second, first] = left_ref[...]
    inverse_ref[first, first] = inverse0_ref[...]
    inverse_ref[first, second] = zero
    factor(
        rest_ref[...], along_ref[...], down_ref[...], lower_ref.at[second, second], inverse_ref.at[second, second], work
    )
    inverse_ref[second, first] = -dot(inverse_ref[second, second], dot(left_ref[...], inverse0_ref[...]))


def third_kernel(
    corners_ref, belows_ref, inverse0_ref, left_ref, lower_ref, inverse_ref, cross_ref, corner_ref, below_ref, work,
):
    tile = work.shape[0]
    first, second = slice(0, tile), slice(tile, 2 * tile)
    zero = jnp.zeros((tile, tile), F32)
    unpack([belows_ref.at[t] for t in range(belows_ref.shape[0])], below_ref)
    unpack([corners_ref.at[t] for t in range(corners_ref.shape[0])], corner_ref)
    scales0, scales1 = scales(corner_ref[first, first]), scales(corner_ref[second, second])
    top = dot(below_ref[first, :], inverse0_ref[...], NT)
    factor(
        corner_ref[first, first] - dot(top, top, NT),
        *scales0, lower_ref.at[first, first], inverse_ref.at[first, first], work,
    )
    bottom = dot(below_ref[second, :], inverse0_ref[...], NT)
    left_ref[first, :] = top
    left_ref[second, :] = bottom
    ahead = corner_ref[second, first] - dot(bottom, top, NT)
    rest = corner_ref[second, second] - dot(bottom, bottom, NT)
    under = dot(ahead, inverse_ref[first, first], NT)
    lower_ref[first, second] = zero
    lower_ref[second, first] = under
    inverse_ref[first, second] = zero
    factor(
        rest - dot(under, under, NT),
        *scales1, lower_ref.at[second, second], inverse_ref.at[second, second], work,
    )
    corner = dot_split(split(under), split(inverse_ref[first, first]))
    inverse_ref[second, first] = -dot_split(split(inverse_ref[second, second]), split(corner))
    cross = dot_split(split(left_ref[...]), split(inverse0_ref[...]))
    cross_ref[...] = -dot_split(split(inverse_ref[...]), split(cross))


def final_kernel(
    index_ref, keep_ref, own_ref, packed_ref, rows_ref, col0_ref, col1_ref,
    lower0_ref, inverse0_ref, lower1_ref, inverse1_ref, left_ref, cross_ref,
    schur_ref, panels_ref, upper_ref, row_ref,
):
    layer, row, col = index_ref[0], index_ref[1], index_ref[2]
    width = upper_ref.shape[1]
    tiles_per = keep_ref.shape[0]
    tile = width // tiles_per
    slabs = rows_ref.shape[0]
    slab_rows = width // slabs

    @pl.when(row == 0)
    def _():
        turn_back(lower0_ref, panels_ref.at[0], tile)
        panels_ref[1] = jnp.zeros((width, width), F32)

    @pl.when(row == 1)
    def _():
        panels_ref[0] = left_ref[...]
        turn_back(lower1_ref, panels_ref.at[1], tile)

    @pl.when(row > 1)
    def _():
        for k in range(2):
            unpack([rows_ref.at[t, k] for t in range(slabs)], row_ref.at[k])
        f0, f1 = split(row_ref[0]), split(row_ref[1])
        panels_ref[0] = dot_split(f0, split(inverse0_ref[...]), NT)
        panels_ref[1] = dot_split(f0, split(cross_ref[...]), NT) + dot_split(f1, split(inverse1_ref[...]), NT)

    @pl.when(col == 0)
    def _():
        upper_ref[...] = jnp.zeros(upper_ref.shape, F32)

    @pl.when((row == 0) & (col == 0))
    def _():
        tile0, below, tile1 = open_packed(packed_ref)
        row_ref[0, :tile, :tile] = tile0
        row_ref[0, tile:, :tile] = below
        row_ref[0, :tile, tile:] = below.T
        row_ref[0, tile:, tile:] = tile1

    @pl.when(col == 1)
    def _():
        upper_ref[:width, :] = left_ref[...].T
        upper_ref[width:, :] = jnp.zeros((width, width), F32)

    @pl.when(col > 1)
    def _():
        for k, ref in enumerate((col0_ref, col1_ref)):
            unpack([ref.at[t] for t in range(slabs)], row_ref.at[k])
        g0, g1 = split(row_ref[0]), split(row_ref[1])
        upper_ref[:width, :] = dot_split(split(inverse0_ref[...]), g0)
        upper_ref[width:, :] = dot_split(split(cross_ref[...]), g0) + dot_split(split(inverse1_ref[...]), g1)

    slab = pl.ds(pl.multiple_of(layer * slab_rows, slab_rows), slab_rows)
    product = dot_split(split(panels_ref[0, slab, :]), split(upper_ref[:width, :]))
    product += dot_split(split(panels_ref[1, slab, :]), split(upper_ref[width:, :]))
    at_row = (lax.broadcasted_iota(jnp.int32, (slab_rows, tile), 0) + layer * slab_rows) // tile
    for j in range(tiles_per):
        keep = jnp.zeros((slab_rows, tile), jnp.int32)
        for i in range(tiles_per):
            keep = jnp.where(at_row == i, keep_ref[i, j], keep)
        own = own_ref[pl.ds(j, slab_rows, tiles_per), :]
        at = slice(j * tile, (j + 1) * tile)
        own = jnp.where((row == 0) & (col == 0), row_ref[0, slab, at], own)
        schur_ref[pl.ds(j, slab_rows, tiles_per), :] = own - jnp.where(keep > 0, product[:, at], 0.0)


AXES = ("layer", "row", "col")


def trade(x, axis, k):
    return lax.ppermute(x, axis, [(i, i ^ k) for i in range(lax.axis_size(axis))])


def ask_layers(x):
    return [x] + [trade(x, "layer", k) for k in range(1, lax.axis_size("layer"))]


def in_order(parts, *late):
    layer = lax.axis_index("layer").astype(jnp.int32)
    parts = parts[:1] + [after(part, *late) for part in parts[1:]]
    ordered = []
    for t in range(len(parts)):
        held = parts[0]
        for k in range(1, len(parts)):
            held = jnp.where(layer ^ t == k, parts[k], held)
        ordered.append(held)
    return jnp.stack(ordered)


def strides(count, least):
    step = 1
    while 2 * step < count:
        step *= 2
    out = []
    while step >= least:
        out.append(step)
        step //= 2
    return out


def after(x, *others):
    return lax.optimization_barrier((x,) + others)[0]


def run(kernel, outs, ins, scratch=(), flops=0, name=None, smem=0, source=pltpu.VMEM):
    vmem = pl.BlockSpec(memory_space=pltpu.VMEM)
    ins_at = [pl.BlockSpec(memory_space=pltpu.SMEM)] * smem + [pl.BlockSpec(memory_space=source)] * (len(ins) - smem)
    return pl.pallas_call(
        kernel,
        out_shape=tuple(jax.ShapeDtypeStruct(s, F32) for s in outs),
        in_specs=ins_at,
        out_specs=tuple(vmem for _ in outs),
        scratch_shapes=[pltpu.VMEM(s, F32) if isinstance(s, tuple) else s for s in scratch],
        compiler_params=pltpu.CompilerParams(vmem_limit_bytes=24 * 1024 * 1024),
        cost_estimate=pl.CostEstimate(flops=flops, bytes_accessed=10**6, transcendentals=0),
        name=name,
    )(*ins)


def on_device(partials, pattern):
    layers, rows, cols = (lax.axis_size(a) for a in AXES)
    layer, row, col = (lax.axis_index(a).astype(jnp.int32) for a in AXES)
    width = partials.shape[3]
    tiles_per = pattern.shape[2]
    tile = width // tiles_per
    slab_rows = width // layers
    piece_rows = slab_rows * tiles_per
    height = 2 * tile + SUB
    even_row, even_col = row % 2 == 0, col % 2 == 0
    index = jnp.stack([layer, row, col])
    square, big = (tile, tile), (width, width)

    mine, *sends = run(
        pack_kernel,
        ((height, tile),) * layers,
        (index, pltpu.with_memory_space_constraint(partials.reshape(width * tiles_per, tile), pltpu.HBM)),
        scratch=((width * tiles_per, tile), pltpu.SemaphoreType.DMA),
        name="k0",
        smem=1,
        source=pltpu.HBM,
    )
    front = total([mine] + [trade(x, "layer", k + 1) for k, x in enumerate(sends)])
    piece = front[:piece_rows]

    keep = (pattern.reshape(tiles_per, tiles_per) > 0) | (row < 2) | (col < 2)
    keep = keep.astype(jnp.int32)
    fall = after(piece, keep)
    for s in strides(rows, 2):
        fall_from, fall_got = fall, trade(fall, "row", s)
        if s > 2:
            fall = jnp.where(row % (2 * s) >= s, fall_got, fall_from)

    lead = front
    for s in strides(cols, 2):
        lead = jnp.where(col % (2 * s) >= s, trade(lead, "col", s), lead)
    fall_got = after(fall_got, lead)
    lead = after(lead, fall_got)
    got = trade(lead, "col", 1)
    fall_from, fall_got = after(fall_from, lead), after(fall_got, lead)
    fall = jnp.where(row % 4 >= 2, fall_got, fall_from)
    fall_parts = ask_layers(fall)
    low, high = jnp.where(even_col, lead, got), jnp.where(even_col, got, lead)
    panels_in = jnp.stack([low[:piece_rows], high[:piece_rows]])
    high = high[:piece_rows]

    high = after(high, low)

    for s in strides(rows, 2):
        low = jnp.where(row % (2 * s) >= s, trade(low, "row", s), low)
    for s in strides(rows, 2):
        high_from, high_got = high, trade(high, "row", s)
        if s > 2:
            high = jnp.where(row % (2 * s) >= s, high_got, high_from)
    high = jnp.where(row % 4 >= 2, after(high_got, low), high_from)
    got = trade(low, "row", 1)
    packed = jnp.where(even_row, low, got)
    lead_parts = ask_layers(jnp.where(even_row, got[:piece_rows], high))
    packed = after(packed, high)

    small_lower, small_inverse, left0, rest0, *scales0 = run(
        first_kernel,
        (square,) * 6,
        (packed,),
        scratch=(square,),
        flops=5 * 10**9,
        name="k1",
    )
    rows_in = ask_layers(after(panels_in, rest0))
    lead = in_order(lead_parts, rest0)
    lead_other = trade(lead, "row", 1)
    lower0, inverse0 = run(
        second_kernel,
        (big, big),
        (small_lower, small_inverse, left0, after(rest0, lead), *scales0),
        scratch=(square,),
        flops=5 * 10**9,
        name="k2",
    )
    lead_other = after(lead_other, inverse0)
    corners, belows = jnp.where(even_row, lead_other, lead), jnp.where(even_row, lead, lead_other)
    fall = in_order(fall_parts, inverse0)
    fall_other = trade(fall, "row", 1)
    left1, lower1, inverse1, cross = run(
        third_kernel,
        (big, big, big, big),
        (corners, belows, inverse0),
        scratch=(big, big, square),
        flops=10**10,
        name="k3",
    )
    rows_in, fall_other = in_order(rows_in, cross), after(fall_other, cross)
    col0, col1 = jnp.where(even_row, fall, fall_other), jnp.where(even_row, fall_other, fall)
    schur, panels = run(
        final_kernel,
        ((piece_rows, tile), (2, width, width)),
        (index, keep, piece, packed, rows_in, col0, col1, lower0, inverse0, lower1, inverse1, left1, cross),
        scratch=((2 * width, width), (2, width, width)),
        flops=10**9,
        name="kf",
        smem=2,
    )
    return (
        schur.reshape(1, 1, 1, slab_rows, 1, 1, width),
        panels.reshape(2, 1, 1, width, width),
    )


def solution(mesh):
    return jax.shard_map(
        on_device,
        mesh=mesh,
        in_specs=(
            P("layer", None, "row", None, None, "col", None),
            P(None, "row", None, None, "col", None),
        ),
        out_specs=(
            P(None, "row", "layer", None, None, "col", None),
            P(None, None, "row", None, None),
        ),
        check_vma=False,
    )
```

```python
import functools

import jax
import jax.numpy as jnp
from jax import lax
from jax.experimental import pallas as pl
from jax.experimental.pallas import tpu as pltpu
from jax.sharding import PartitionSpec as P

F32 = jnp.float32
SUB = 8
NT = (((1,), (1,)), ((), ()))
NN = (((1,), (0,)), ((), ()))


def dot(a, b, dims=NN):
    return lax.dot_general(
        a, b, dims, precision=lax.Precision.HIGHEST, preferred_element_type=F32
    )


AXES = ("layer", "row", "col")


def position():
    return tuple(lax.axis_index(a).astype(jnp.int32) for a in AXES)


def split(x):
    high = x.astype(jnp.bfloat16)
    return high, (x - high.astype(F32)).astype(jnp.bfloat16)


def dot_split(a, b, dims=NN):
    part = lambda x, y: lax.dot_general(x, y, dims, preferred_element_type=F32)
    return part(a[0], b[0]) + (part(a[0], b[1]) + part(a[1], b[0]))


def lane_splat(x, lane):
    return jnp.broadcast_to(x[:, lane : lane + 1], x.shape)


def row_splat(x, row):
    return jnp.broadcast_to(x[row : row + 1, :], x.shape)


def recip(x):
    return pl.reciprocal(x, approx=True)


def total(terms):
    while len(terms) > 1:
        terms = [terms[i] + terms[i + 1] for i in range(0, len(terms), 2)]
    return terms[0]


def factor_rows(rows):
    groups = len(rows)
    sub = lax.broadcasted_iota(jnp.int32, rows[0].shape, 0)
    lane = lax.broadcasted_iota(jnp.int32, rows[0].shape, 1)
    here = [sub == j for j in range(SUB)]
    unit = [jnp.where(h, 1.0, 0.0).astype(F32) for h in here]
    held = list(rows)
    out = []
    cols = [lane_splat(held[0], k) for k in range(SUB)]
    for b in range(groups):
        y = held[b]
        last = b + 1 == groups
        if not last:
            near = held[b + 1]
            side = [lane_splat(near, b * SUB + k) for k in range(SUB)]
            ahead = [lane_splat(near, (b + 1) * SUB + k) for k in range(SUB)]
        below = {g: [lane_splat(held[g], b * SUB + k) for k in range(SUB)] for g in range(b + 2, groups)}
        done = jnp.zeros_like(y)
        for j in range(0, SUB, 2):
            c0, c1 = cols[j], cols[j + 1]
            p, q, s = row_splat(c0, j), row_splat(c1, j), row_splat(c1, j + 1)
            r = recip(p * s - q * q)
            m0, m1 = c0 - unit[j], c1 - unit[j + 1]
            if j + 2 < SUB:
                v0, v1 = s * c0 - q * c1, p * c1 - q * c0
            for k in range(j + 2, SUB):
                n0, n1 = row_splat(v0, k), row_splat(v1, k)
                cols[k] = cols[k] - (m0 * n0 + m1 * n1) * r
                if not last:
                    side[k] = side[k] - (side[j] * n0 + side[j + 1] * n1) * r
            y0, y1 = row_splat(y, j), row_splat(y, j + 1)
            w0, w1 = (s * y0 - q * y1) * r, (p * y1 - q * y0) * r
            if not last:
                s0, s1 = side[j], side[j + 1]
                v0, v1 = s * s0 - q * s1, p * s1 - q * s0
                final = j + 2 == SUB
                if not final:
                    v0, v1 = v0 * r, v1 * r
                for k in range(SUB):
                    step = s0 * row_splat(v0, k) + s1 * row_splat(v1, k)
                    ahead[k] = ahead[k] - (step * r if final else step)
                near = near - (s0 * w0 + s1 * w1)
            y = y - (m0 * w0 + m1 * w1)
            root0 = lax.rsqrt(p)
            ratio = q * root0 * root0
            root1 = lax.rsqrt(s - q * ratio)
            done = jnp.where(here[j], y0 * root0, done)
            done = jnp.where(here[j + 1], (y1 - ratio * y0) * root1, done)
        out.append(jnp.where(lane >= sub + b * SUB, done, 0.0))
        if last:
            break
        held[b + 1] = near
        cols = ahead
        if below:
            yk = [row_splat(y, k) for k in range(SUB)]
        for g, c in below.items():
            held[g] = held[g] - total([c[k] * yk[k] for k in range(SUB)])
    return out


def tile_rows(tile):
    return [tile[g * SUB : (g + 1) * SUB, :] for g in range(tile.shape[0] // SUB)]


def scales(tile):
    at_row = lax.broadcasted_iota(jnp.int32, tile.shape, 0)
    at_col = lax.broadcasted_iota(jnp.int32, tile.shape, 1)
    diagonal = jnp.sum(jnp.where(at_row == at_col, tile, 0.0), axis=0, keepdims=True)
    along = jnp.broadcast_to(lax.rsqrt(diagonal), tile.shape)
    return along, along.T


def factor(tile, along, down, turned_ref, inverse_ref, work):
    half = tile.shape[0] // 2
    at_row = lax.broadcasted_iota(jnp.int32, (half, 2 * half), 0)
    at_col = lax.broadcasted_iota(jnp.int32, (half, 2 * half), 1)
    a = tile * along * down
    one = jnp.where(at_row[:, :half] == at_col[:, :half], 1.0, 0.0).astype(F32)
    beside = jnp.where(at_row + half == at_col, 1.0, 0.0).astype(F32)
    work[:half, :half] = jnp.zeros((half, half), F32)
    work[:half, half:] = a[half:, :half]
    work[half:, :half] = a[half:, half:]
    work[half:, half:] = one
    first = jnp.concatenate(factor_rows(tile_rows(jnp.where(at_col < half, a[:half], beside))), axis=0)
    under = dot(work[:half, :], first, NT)
    work[half:, :half] -= dot(under, under, NT)
    second = jnp.concatenate(factor_rows(tile_rows(work[half:, :])), axis=0)
    inverse0, inverse1 = first[:, half:], second[:, half:]
    inverse_ref[:half, :half] = inverse0 * along[:half, :half]
    inverse_ref[:half, half:] = jnp.zeros((half, half), F32)
    inverse_ref[half:, :half] = -dot(inverse1, dot(under, inverse0)) * along[half:, :half]
    inverse_ref[half:, half:] = inverse1 * along[half:, half:]
    across, up = recip(along), recip(down)
    turned_ref[:half, :half] = first[:, :half] * across[:half, :half]
    turned_ref[:half, half:] = jnp.zeros((half, half), F32)
    turned_ref[half:, :half] = under * up[half:, :half]
    turned_ref[half:, half:] = second[:, :half] * across[half:, half:]


def turn_back(from_ref, to_ref, tile):
    width = from_ref.shape[0]
    at_row = lax.broadcasted_iota(jnp.int32, (tile, tile), 0)
    at_col = lax.broadcasted_iota(jnp.int32, (tile, tile), 1)
    same = at_row // (tile // 2) == at_col // (tile // 2)
    to_ref[...] = from_ref[...]
    for t in range(0, width, tile):
        at = slice(t, t + tile)
        held = from_ref[at, at]
        to_ref[at, at] = jnp.where(same, held.T, held)


def pack_kernel(source_ref, mine_ref, *refs):
    *send_refs, linear_ref, arrived = refs
    load = pltpu.make_async_copy(source_ref, linear_ref, arrived)
    load.start()
    layer, row, col = position()
    first = (row == 0) & (col == 0)
    height, tile = mine_ref.shape
    load.wait()
    piece = linear_ref.shape[0] // (len(send_refs) + 1)

    @pl.when(first)
    def _():
        at_row = lax.broadcasted_iota(jnp.int32, (tile, tile), 0)
        at_col = lax.broadcasted_iota(jnp.int32, (tile, tile), 1)
        corner = linear_ref[pl.ds(2 * tile + 1, tile, 2), :]
        mixed = jnp.where(at_row >= at_col, linear_ref[pl.ds(0, tile, 2), :], corner)
        below = linear_ref[pl.ds(2 * tile, tile, 2), :]
        diagonal = jnp.sum(jnp.where(at_row == at_col, corner, 0.0), axis=0, keepdims=True)
        for ref in (mine_ref, *send_refs):
            ref[:tile, :] = mixed
            ref[tile : 2 * tile, :] = below
            ref[2 * tile :, :] = jnp.broadcast_to(diagonal, (height - 2 * tile, tile))

    @pl.when(jnp.logical_not(first))
    def _():
        for k, ref in enumerate((mine_ref, *send_refs)):
            start = pl.multiple_of((layer ^ k) * piece, piece)
            ref[:piece, :] = linear_ref[pl.ds(start, piece), :]
            ref[piece:, :] = jnp.zeros((height - piece, tile), F32)


def unpack(pieces, to_ref):
    tile = pieces[0].shape[1]
    slab = pieces[0].shape[0] // 2
    for t, piece in enumerate(pieces):
        to_ref[t * slab : (t + 1) * slab, :tile] = piece[pl.ds(0, slab, 2), :]
        to_ref[t * slab : (t + 1) * slab, tile:] = piece[pl.ds(1, slab, 2), :]


def symmetric(lower, keep):
    part = jnp.where(keep, lower, 0.0)
    at = lax.broadcasted_iota(jnp.int32, lower.shape, 0) == lax.broadcasted_iota(jnp.int32, lower.shape, 1)
    return part + jnp.where(at, 0.0, part).T


def open_packed(packed_ref):
    tile = packed_ref.shape[1]
    at_row = lax.broadcasted_iota(jnp.int32, (tile, tile), 0)
    at_col = lax.broadcasted_iota(jnp.int32, (tile, tile), 1)
    mixed = packed_ref[:tile, :]
    tile0 = symmetric(mixed, at_row >= at_col)
    upper1 = jnp.where(at_row < at_col, mixed, 0.0)
    diagonal = jnp.broadcast_to(packed_ref[2 * tile : 2 * tile + 1, :], (tile, tile))
    tile1 = upper1 + upper1.T + jnp.where(at_row == at_col, diagonal, 0.0)
    return tile0, packed_ref[tile : 2 * tile, :], tile1


def first_kernel(packed_ref, lower_ref, inverse_ref, left_ref, rest_ref, along_ref, down_ref, work):
    tile0, below, tile1 = open_packed(packed_ref)
    along, down = scales(tile1)
    along_ref[...] = along
    down_ref[...] = down
    factor(tile0, *scales(tile0), lower_ref, inverse_ref, work)
    left = dot(below, inverse_ref[...], NT)
    left_ref[...] = left
    rest_ref[...] = tile1 - dot(left, left, NT)


def second_kernel(
    lower0_ref, inverse0_ref, left_ref, rest_ref, along_ref, down_ref, lower_ref, inverse_ref, work
):
    tile = rest_ref.shape[0]
    zero = jnp.zeros((tile, tile), F32)
    first, second = slice(0, tile), slice(tile, 2 * tile)
    lower_ref[first, first] = lower0_ref[...]
    lower_ref[first, second] = zero
    lower_ref[second, first] = left_ref[...]
    inverse_ref[first, first] = inverse0_ref[...]
    inverse_ref[first, second] = zero
    factor(
        rest_ref[...], along_ref[...], down_ref[...], lower_ref.at[second, second], inverse_ref.at[second, second], work
    )
    inverse_ref[second, first] = -dot(inverse_ref[second, second], dot(left_ref[...], inverse0_ref[...]))


def third_kernel(
    corners_ref, belows_ref, inverse0_ref, left_ref, lower_ref, inverse_ref, cross_ref, corner_ref, below_ref, work,
):
    tile = work.shape[0]
    first, second = slice(0, tile), slice(tile, 2 * tile)
    zero = jnp.zeros((tile, tile), F32)
    unpack([belows_ref.at[t] for t in range(belows_ref.shape[0])], below_ref)
    unpack([corners_ref.at[t] for t in range(corners_ref.shape[0])], corner_ref)
    scales0, scales1 = scales(corner_ref[first, first]), scales(corner_ref[second, second])
    top = dot(below_ref[first, :], inverse0_ref[...], NT)
    factor(
        corner_ref[first, first] - dot(top, top, NT),
        *scales0, lower_ref.at[first, first], inverse_ref.at[first, first], work,
    )
    bottom = dot(below_ref[second, :], inverse0_ref[...], NT)
    left_ref[first, :] = top
    left_ref[second, :] = bottom
    ahead = corner_ref[second, first] - dot(bottom, top, NT)
    rest = corner_ref[second, second] - dot(bottom, bottom, NT)
    under = dot(ahead, inverse_ref[first, first], NT)
    lower_ref[first, second] = zero
    lower_ref[second, first] = under
    inverse_ref[first, second] = zero
    factor(
        rest - dot(under, under, NT),
        *scales1, lower_ref.at[second, second], inverse_ref.at[second, second], work,
    )
    corner = dot_split(split(under), split(inverse_ref[first, first]))
    inverse_ref[second, first] = -dot_split(split(inverse_ref[second, second]), split(corner))
    cross = dot_split(split(left_ref[...]), split(inverse0_ref[...]))
    cross_ref[...] = -dot_split(split(inverse_ref[...]), split(cross))


def final_kernel(
    keep_ref, own_ref, packed_ref, rows_ref, col0_ref, col1_ref,
    lower0_ref, inverse0_ref, lower1_ref, inverse1_ref, left_ref, cross_ref,
    schur_ref, panels_ref, upper_ref, row_ref,
):
    layer, row, col = position()
    width = upper_ref.shape[1]
    tiles_per = keep_ref.shape[0]
    tile = width // tiles_per
    slabs = rows_ref.shape[0]
    slab_rows = width // slabs

    @pl.when(row == 0)
    def _():
        turn_back(lower0_ref, panels_ref.at[0], tile)
        panels_ref[1] = jnp.zeros((width, width), F32)

    @pl.when(row == 1)
    def _():
        panels_ref[0] = left_ref[...]
        turn_back(lower1_ref, panels_ref.at[1], tile)

    @pl.when(row > 1)
    def _():
        for k in range(2):
            unpack([rows_ref.at[t, k] for t in range(slabs)], row_ref.at[k])
        f0, f1 = split(row_ref[0]), split(row_ref[1])
        panels_ref[0] = dot_split(f0, split(inverse0_ref[...]), NT)
        panels_ref[1] = dot_split(f0, split(cross_ref[...]), NT) + dot_split(f1, split(inverse1_ref[...]), NT)

    @pl.when(col == 0)
    def _():
        upper_ref[...] = jnp.zeros(upper_ref.shape, F32)

    @pl.when((row == 0) & (col == 0))
    def _():
        tile0, below, tile1 = open_packed(packed_ref)
        row_ref[0, :tile, :tile] = tile0
        row_ref[0, tile:, :tile] = below
        row_ref[0, :tile, tile:] = below.T
        row_ref[0, tile:, tile:] = tile1

    @pl.when(col == 1)
    def _():
        upper_ref[:width, :] = left_ref[...].T
        upper_ref[width:, :] = jnp.zeros((width, width), F32)

    @pl.when(col > 1)
    def _():
        for k, ref in enumerate((col0_ref, col1_ref)):
            unpack([ref.at[t] for t in range(slabs)], row_ref.at[k])
        g0, g1 = split(row_ref[0]), split(row_ref[1])
        upper_ref[:width, :] = dot_split(split(inverse0_ref[...]), g0)
        upper_ref[width:, :] = dot_split(split(cross_ref[...]), g0) + dot_split(split(inverse1_ref[...]), g1)

    slab = pl.ds(pl.multiple_of(layer * slab_rows, slab_rows), slab_rows)
    product = dot_split(split(panels_ref[0, slab, :]), split(upper_ref[:width, :]))
    product += dot_split(split(panels_ref[1, slab, :]), split(upper_ref[width:, :]))
    at_row = (lax.broadcasted_iota(jnp.int32, (slab_rows, tile), 0) + layer * slab_rows) // tile
    for j in range(tiles_per):
        keep = jnp.zeros((slab_rows, tile), jnp.int32)
        for i in range(tiles_per):
            keep = jnp.where(at_row == i, keep_ref[i, j], keep)
        own = own_ref[pl.ds(j, slab_rows, tiles_per), :]
        at = slice(j * tile, (j + 1) * tile)
        own = jnp.where((row == 0) & (col == 0), row_ref[0, slab, at], own)
        schur_ref[pl.ds(j, slab_rows, tiles_per), :] = own - jnp.where(keep > 0, product[:, at], 0.0)


def trade(x, axis, k):
    return lax.ppermute(x, axis, [(i, i ^ k) for i in range(lax.axis_size(axis))])


def ask_layers(x):
    return [x] + [trade(x, "layer", k) for k in range(1, lax.axis_size("layer"))]


def in_order(parts, *late):
    layer = lax.axis_index("layer").astype(jnp.int32)
    parts = parts[:1] + [after(part, *late) for part in parts[1:]]
    ordered = []
    for t in range(len(parts)):
        held = parts[0]
        for k in range(1, len(parts)):
            held = jnp.where(layer ^ t == k, parts[k], held)
        ordered.append(held)
    return jnp.stack(ordered)


def strides(count, least):
    step = 1
    while 2 * step < count:
        step *= 2
    out = []
    while step >= least:
        out.append(step)
        step //= 2
    return out


def after(x, *others):
    return lax.optimization_barrier((x,) + others)[0]


def run(kernel, outs, ins, scratch=(), flops=0, name=None, smem=0, source=pltpu.VMEM):
    vmem = pl.BlockSpec(memory_space=pltpu.VMEM)
    ins_at = [pl.BlockSpec(memory_space=pltpu.SMEM)] * smem + [pl.BlockSpec(memory_space=source)] * (len(ins) - smem)
    return pl.pallas_call(
        kernel,
        out_shape=tuple(jax.ShapeDtypeStruct(s, F32) for s in outs),
        in_specs=ins_at,
        out_specs=tuple(vmem for _ in outs),
        scratch_shapes=[pltpu.VMEM(s, F32) if isinstance(s, tuple) else s for s in scratch],
        compiler_params=pltpu.CompilerParams(vmem_limit_bytes=24 * 1024 * 1024),
        cost_estimate=pl.CostEstimate(flops=flops, bytes_accessed=10**6, transcendentals=0),
        name=name,
    )(*ins)


def on_device(partials, pattern):
    layers, rows, cols = (lax.axis_size(a) for a in AXES)
    layer, row, col = position()
    width = partials.shape[3]
    tiles_per = pattern.shape[2]
    tile = width // tiles_per
    slab_rows = width // layers
    piece_rows = slab_rows * tiles_per
    height = 2 * tile + SUB
    even_row, even_col = row % 2 == 0, col % 2 == 0
    square, big = (tile, tile), (width, width)

    mine, *sends = run(
        pack_kernel,
        ((height, tile),) * layers,
        (pltpu.with_memory_space_constraint(partials.reshape(width * tiles_per, tile), pltpu.HBM),),
        scratch=((width * tiles_per, tile), pltpu.SemaphoreType.DMA),
        name="k0",
        source=pltpu.HBM,
    )
    front = total([mine] + [trade(x, "layer", k + 1) for k, x in enumerate(sends)])
    piece = front[:piece_rows]

    keep = (pattern.reshape(tiles_per, tiles_per) > 0) | (row < 2) | (col < 2)
    keep = keep.astype(jnp.int32)
    fall = after(piece, keep)
    for s in strides(rows, 2):
        fall_from, fall_got = fall, trade(fall, "row", s)
        if s > 2:
            fall = jnp.where(row % (2 * s) >= s, fall_got, fall_from)

    lead = front
    for s in strides(cols, 2):
        lead = jnp.where(col % (2 * s) >= s, trade(lead, "col", s), lead)
    fall_got = after(fall_got, lead)
    lead = after(lead, fall_got)
    got = trade(lead, "col", 1)
    fall_from, fall_got = after(fall_from, lead), after(fall_got, lead)
    fall = jnp.where(row % 4 >= 2, fall_got, fall_from)
    fall_parts = ask_layers(fall)
    low, high = jnp.where(even_col, lead, got), jnp.where(even_col, got, lead)
    panels_in = jnp.stack([low[:piece_rows], high[:piece_rows]])
    high = high[:piece_rows]

    high = after(high, low)

    for s in strides(rows, 2):
        low = jnp.where(row % (2 * s) >= s, trade(low, "row", s), low)
    for s in strides(rows, 2):
        high_from, high_got = high, trade(high, "row", s)
        if s > 2:
            high = jnp.where(row % (2 * s) >= s, high_got, high_from)
    high = jnp.where(row % 4 >= 2, after(high_got, low), high_from)
    got = trade(low, "row", 1)
    packed = jnp.where(even_row, low, got)
    lead_parts = ask_layers(jnp.where(even_row, got[:piece_rows], high))
    packed = after(packed, high)

    small_lower, small_inverse, left0, rest0, *scales0 = run(
        first_kernel,
        (square,) * 6,
        (packed,),
        scratch=(square,),
        flops=5 * 10**9,
        name="k1",
    )
    rows_in = ask_layers(after(panels_in, rest0))
    lead = in_order(lead_parts, rest0)
    lead_other = trade(lead, "row", 1)
    lower0, inverse0 = run(
        second_kernel,
        (big, big),
        (small_lower, small_inverse, left0, after(rest0, lead), *scales0),
        scratch=(square,),
        flops=5 * 10**9,
        name="k2",
    )
    lead_other = after(lead_other, inverse0)
    corners, belows = jnp.where(even_row, lead_other, lead), jnp.where(even_row, lead, lead_other)
    fall = in_order(fall_parts, inverse0)
    fall_other = trade(fall, "row", 1)
    left1, lower1, inverse1, cross = run(
        third_kernel,
        (big, big, big, big),
        (corners, belows, inverse0),
        scratch=(big, big, square),
        flops=10**10,
        name="k3",
    )
    rows_in, fall_other = in_order(rows_in, cross), after(fall_other, cross)
    col0, col1 = jnp.where(even_row, fall, fall_other), jnp.where(even_row, fall_other, fall)
    schur, panels = run(
        final_kernel,
        ((piece_rows, tile), (2, width, width)),
        (keep, piece, packed, rows_in, col0, col1, lower0, inverse0, lower1, inverse1, left1, cross),
        scratch=((2 * width, width), (2, width, width)),
        flops=10**9,
        name="kf",
        smem=1,
    )
    return (
        schur.reshape(1, 1, 1, slab_rows, 1, 1, width),
        panels.reshape(2, 1, 1, width, width),
    )


def solution(mesh):
    return jax.shard_map(
        on_device,
        mesh=mesh,
        in_specs=(
            P("layer", None, "row", None, None, "col", None),
            P(None, "row", None, None, "col", None),
        ),
        out_specs=(
            P(None, "row", "layer", None, None, "col", None),
            P(None, None, "row", None, None),
        ),
        check_vma=False,
    )
```

```python
import functools

import jax
import jax.numpy as jnp
from jax import lax
from jax.experimental import pallas as pl
from jax.experimental.pallas import tpu as pltpu
from jax.sharding import PartitionSpec as P

F32 = jnp.float32
SUB = 8
NT = (((1,), (1,)), ((), ()))
NN = (((1,), (0,)), ((), ()))


def dot(a, b, dims=NN):
    return lax.dot_general(
        a, b, dims, precision=lax.Precision.HIGHEST, preferred_element_type=F32
    )


AXES = ("layer", "row", "col")


def position():
    return tuple(lax.axis_index(a).astype(jnp.int32) for a in AXES)


def split(x):
    high = x.astype(jnp.bfloat16)
    return high, (x - high.astype(F32)).astype(jnp.bfloat16)


def dot_split(a, b, dims=NN):
    part = lambda x, y: lax.dot_general(x, y, dims, preferred_element_type=F32)
    return part(a[0], b[0]) + (part(a[0], b[1]) + part(a[1], b[0]))


def lane_splat(x, lane):
    return jnp.broadcast_to(x[:, lane : lane + 1], x.shape)


def row_splat(x, row):
    return jnp.broadcast_to(x[row : row + 1, :], x.shape)


def recip(x):
    return pl.reciprocal(x, approx=True)


def total(terms):
    while len(terms) > 1:
        terms = [terms[i] + terms[i + 1] for i in range(0, len(terms), 2)]
    return terms[0]


def factor_rows(rows):
    groups = len(rows)
    sub = lax.broadcasted_iota(jnp.int32, rows[0].shape, 0)
    lane = lax.broadcasted_iota(jnp.int32, rows[0].shape, 1)
    here = [sub == j for j in range(SUB)]
    unit = [jnp.where(h, 1.0, 0.0).astype(F32) for h in here]
    held = list(rows)
    out = []
    cols = [lane_splat(held[0], k) for k in range(SUB)]
    for b in range(groups):
        y = held[b]
        last = b + 1 == groups
        if not last:
            near = held[b + 1]
            side = [lane_splat(near, b * SUB + k) for k in range(SUB)]
            ahead = [lane_splat(near, (b + 1) * SUB + k) for k in range(SUB)]
        below = {g: [lane_splat(held[g], b * SUB + k) for k in range(SUB)] for g in range(b + 2, groups)}
        done = jnp.zeros_like(y)
        for j in range(0, SUB, 2):
            c0, c1 = cols[j], cols[j + 1]
            p, q, s = row_splat(c0, j), row_splat(c1, j), row_splat(c1, j + 1)
            r = recip(p * s - q * q)
            m0, m1 = c0 - unit[j], c1 - unit[j + 1]
            if j + 2 < SUB:
                v0, v1 = s * c0 - q * c1, p * c1 - q * c0
            for k in range(j + 2, SUB):
                n0, n1 = row_splat(v0, k), row_splat(v1, k)
                cols[k] = cols[k] - (m0 * n0 + m1 * n1) * r
                if not last:
                    side[k] = side[k] - (side[j] * n0 + side[j + 1] * n1) * r
            y0, y1 = row_splat(y, j), row_splat(y, j + 1)
            w0, w1 = (s * y0 - q * y1) * r, (p * y1 - q * y0) * r
            if not last:
                s0, s1 = side[j], side[j + 1]
                v0, v1 = s * s0 - q * s1, p * s1 - q * s0
                final = j + 2 == SUB
                if not final:
                    v0, v1 = v0 * r, v1 * r
                for k in range(SUB):
                    step = s0 * row_splat(v0, k) + s1 * row_splat(v1, k)
                    ahead[k] = ahead[k] - (step * r if final else step)
                near = near - (s0 * w0 + s1 * w1)
            y = y - (m0 * w0 + m1 * w1)
            root0 = lax.rsqrt(p)
            ratio = q * root0 * root0
            root1 = lax.rsqrt(s - q * ratio)
            done = jnp.where(here[j], y0 * root0, done)
            done = jnp.where(here[j + 1], (y1 - ratio * y0) * root1, done)
        out.append(jnp.where(lane >= sub + b * SUB, done, 0.0))
        if last:
            break
        held[b + 1] = near
        cols = ahead
        if below:
            yk = [row_splat(y, k) for k in range(SUB)]
        for g, c in below.items():
            held[g] = held[g] - total([c[k] * yk[k] for k in range(SUB)])
    return out


def tile_rows(tile):
    return [tile[g * SUB : (g + 1) * SUB, :] for g in range(tile.shape[0] // SUB)]


def scales(tile):
    at_row = lax.broadcasted_iota(jnp.int32, tile.shape, 0)
    at_col = lax.broadcasted_iota(jnp.int32, tile.shape, 1)
    diagonal = jnp.sum(jnp.where(at_row == at_col, tile, 0.0), axis=0, keepdims=True)
    along = jnp.broadcast_to(lax.rsqrt(diagonal), tile.shape)
    return along, along.T


def factor(tile, along, down, turned_ref, inverse_ref, work):
    half = tile.shape[0] // 2
    at_row = lax.broadcasted_iota(jnp.int32, (half, 2 * half), 0)
    at_col = lax.broadcasted_iota(jnp.int32, (half, 2 * half), 1)
    a = tile * along * down
    one = jnp.where(at_row[:, :half] == at_col[:, :half], 1.0, 0.0).astype(F32)
    beside = jnp.where(at_row + half == at_col, 1.0, 0.0).astype(F32)
    work[:half, :half] = jnp.zeros((half, half), F32)
    work[:half, half:] = a[half:, :half]
    work[half:, :half] = a[half:, half:]
    work[half:, half:] = one
    first = jnp.concatenate(factor_rows(tile_rows(jnp.where(at_col < half, a[:half], beside))), axis=0)
    under = dot(work[:half, :], first, NT)
    work[half:, :half] -= dot(under, under, NT)
    second = jnp.concatenate(factor_rows(tile_rows(work[half:, :])), axis=0)
    inverse0, inverse1 = first[:, half:], second[:, half:]
    inverse_ref[:half, :half] = inverse0 * along[:half, :half]
    inverse_ref[:half, half:] = jnp.zeros((half, half), F32)
    inverse_ref[half:, :half] = -dot(inverse1, dot(under, inverse0)) * along[half:, :half]
    inverse_ref[half:, half:] = inverse1 * along[half:, half:]
    across, up = recip(along), recip(down)
    turned_ref[:half, :half] = first[:, :half] * across[:half, :half]
    turned_ref[:half, half:] = jnp.zeros((half, half), F32)
    turned_ref[half:, :half] = under * up[half:, :half]
    turned_ref[half:, half:] = second[:, :half] * across[half:, half:]


def turn_back(from_ref, to_ref, tile):
    width = from_ref.shape[0]
    at_row = lax.broadcasted_iota(jnp.int32, (tile, tile), 0)
    at_col = lax.broadcasted_iota(jnp.int32, (tile, tile), 1)
    same = at_row // (tile // 2) == at_col // (tile // 2)
    to_ref[...] = from_ref[...]
    for t in range(0, width, tile):
        at = slice(t, t + tile)
        held = from_ref[at, at]
        to_ref[at, at] = jnp.where(same, held.T, held)


def pack_kernel(source_ref, mine_ref, *refs):
    *send_refs, linear_ref, arrived = refs
    load = pltpu.make_async_copy(source_ref, linear_ref, arrived)
    load.start()
    layer, row, col = position()
    first = (row == 0) & (col == 0)
    height, tile = mine_ref.shape
    load.wait()
    piece = linear_ref.shape[0] // (len(send_refs) + 1)

    @pl.when(first)
    def _():
        at_row = lax.broadcasted_iota(jnp.int32, (tile, tile), 0)
        at_col = lax.broadcasted_iota(jnp.int32, (tile, tile), 1)
        corner = linear_ref[pl.ds(2 * tile + 1, tile, 2), :]
        mixed = jnp.where(at_row >= at_col, linear_ref[pl.ds(0, tile, 2), :], corner)
        below = linear_ref[pl.ds(2 * tile, tile, 2), :]
        diagonal = jnp.sum(jnp.where(at_row == at_col, corner, 0.0), axis=0, keepdims=True)
        for ref in (mine_ref, *send_refs):
            ref[:tile, :] = mixed
            ref[tile : 2 * tile, :] = below
            ref[2 * tile :, :] = jnp.broadcast_to(diagonal, (height - 2 * tile, tile))

    @pl.when(jnp.logical_not(first))
    def _():
        for k, ref in enumerate((mine_ref, *send_refs)):
            start = pl.multiple_of((layer ^ k) * piece, piece)
            ref[:piece, :] = linear_ref[pl.ds(start, piece), :]
            ref[piece:, :] = jnp.zeros((height - piece, tile), F32)


def unpack(pieces, to_ref):
    tile = pieces[0].shape[1]
    slab = pieces[0].shape[0] // 2
    for t, piece in enumerate(pieces):
        to_ref[t * slab : (t + 1) * slab, :tile] = piece[pl.ds(0, slab, 2), :]
        to_ref[t * slab : (t + 1) * slab, tile:] = piece[pl.ds(1, slab, 2), :]


def symmetric(lower, keep):
    part = jnp.where(keep, lower, 0.0)
    at = lax.broadcasted_iota(jnp.int32, lower.shape, 0) == lax.broadcasted_iota(jnp.int32, lower.shape, 1)
    return part + jnp.where(at, 0.0, part).T


def open_packed(packed_ref):
    tile = packed_ref.shape[1]
    at_row = lax.broadcasted_iota(jnp.int32, (tile, tile), 0)
    at_col = lax.broadcasted_iota(jnp.int32, (tile, tile), 1)
    mixed = packed_ref[:tile, :]
    tile0 = symmetric(mixed, at_row >= at_col)
    upper1 = jnp.where(at_row < at_col, mixed, 0.0)
    diagonal = jnp.broadcast_to(packed_ref[2 * tile : 2 * tile + 1, :], (tile, tile))
    tile1 = upper1 + upper1.T + jnp.where(at_row == at_col, diagonal, 0.0)
    return tile0, packed_ref[tile : 2 * tile, :], tile1


def first_kernel(packed_ref, lower_ref, inverse_ref, left_ref, rest_ref, along_ref, down_ref, work):
    tile0, below, tile1 = open_packed(packed_ref)
    along, down = scales(tile1)
    along_ref[...] = along
    down_ref[...] = down
    factor(tile0, *scales(tile0), lower_ref, inverse_ref, work)
    left = dot(below, inverse_ref[...], NT)
    left_ref[...] = left
    rest_ref[...] = tile1 - dot(left, left, NT)


def second_kernel(
    lower0_ref, inverse0_ref, left_ref, rest_ref, along_ref, down_ref, lower_ref, inverse_ref, work
):
    tile = rest_ref.shape[0]
    zero = jnp.zeros((tile, tile), F32)
    first, second = slice(0, tile), slice(tile, 2 * tile)
    lower_ref[first, first] = lower0_ref[...]
    lower_ref[first, second] = zero
    lower_ref[second, first] = left_ref[...]
    inverse_ref[first, first] = inverse0_ref[...]
    inverse_ref[first, second] = zero
    factor(
        rest_ref[...], along_ref[...], down_ref[...], lower_ref.at[second, second], inverse_ref.at[second, second], work
    )
    inverse_ref[second, first] = -dot(inverse_ref[second, second], dot(left_ref[...], inverse0_ref[...]))


def third_kernel(
    corners_ref, belows_ref, inverse0_ref, left_ref, lower_ref, inverse_ref, cross_ref, corner_ref, below_ref, work,
):
    tile = work.shape[0]
    first, second = slice(0, tile), slice(tile, 2 * tile)
    zero = jnp.zeros((tile, tile), F32)
    unpack([belows_ref.at[t] for t in range(belows_ref.shape[0])], below_ref)
    unpack([corners_ref.at[t] for t in range(corners_ref.shape[0])], corner_ref)
    scales0, scales1 = scales(corner_ref[first, first]), scales(corner_ref[second, second])
    top = dot(below_ref[first, :], inverse0_ref[...], NT)
    factor(
        corner_ref[first, first] - dot(top, top, NT),
        *scales0, lower_ref.at[first, first], inverse_ref.at[first, first], work,
    )
    bottom = dot(below_ref[second, :], inverse0_ref[...], NT)
    left_ref[first, :] = top
    left_ref[second, :] = bottom
    ahead = corner_ref[second, first] - dot(bottom, top, NT)
    rest = corner_ref[second, second] - dot(bottom, bottom, NT)
    under = dot(ahead, inverse_ref[first, first], NT)
    lower_ref[first, second] = zero
    lower_ref[second, first] = under
    inverse_ref[first, second] = zero
    factor(
        rest - dot(under, under, NT),
        *scales1, lower_ref.at[second, second], inverse_ref.at[second, second], work,
    )
    corner = dot_split(split(under), split(inverse_ref[first, first]))
    inverse_ref[second, first] = -dot_split(split(inverse_ref[second, second]), split(corner))
    cross = dot_split(split(left_ref[...]), split(inverse0_ref[...]))
    cross_ref[...] = -dot_split(split(inverse_ref[...]), split(cross))


def final_kernel(
    keep_ref, own_ref, packed_ref, rows_ref, col0_ref, col1_ref,
    lower0_ref, inverse0_ref, lower1_ref, inverse1_ref, left_ref, cross_ref,
    schur_ref, panels_ref, upper_ref, row_ref,
):
    layer, row, col = position()
    width = upper_ref.shape[1]
    tiles_per = keep_ref.shape[0]
    tile = width // tiles_per
    slabs = rows_ref.shape[0]
    slab_rows = width // slabs

    @pl.when(row == 0)
    def _():
        turn_back(lower0_ref, panels_ref.at[0], tile)
        panels_ref[1] = jnp.zeros((width, width), F32)

    @pl.when(row == 1)
    def _():
        panels_ref[0] = left_ref[...]
        turn_back(lower1_ref, panels_ref.at[1], tile)

    @pl.when(row > 1)
    def _():
        for k in range(2):
            unpack([rows_ref.at[t, k] for t in range(slabs)], row_ref.at[k])
        f0, f1 = split(row_ref[0]), split(row_ref[1])
        panels_ref[0] = dot_split(f0, split(inverse0_ref[...]), NT)
        panels_ref[1] = dot_split(f0, split(cross_ref[...]), NT) + dot_split(f1, split(inverse1_ref[...]), NT)

    @pl.when(col == 0)
    def _():
        upper_ref[...] = jnp.zeros(upper_ref.shape, F32)

    @pl.when((row == 0) & (col == 0))
    def _():
        tile0, below, tile1 = open_packed(packed_ref)
        row_ref[0, :tile, :tile] = tile0
        row_ref[0, tile:, :tile] = below
        row_ref[0, :tile, tile:] = below.T
        row_ref[0, tile:, tile:] = tile1

    @pl.when(col == 1)
    def _():
        upper_ref[:width, :] = left_ref[...].T
        upper_ref[width:, :] = jnp.zeros((width, width), F32)

    @pl.when(col > 1)
    def _():
        for k, ref in enumerate((col0_ref, col1_ref)):
            unpack([ref.at[t] for t in range(slabs)], row_ref.at[k])
        g0, g1 = split(row_ref[0]), split(row_ref[1])
        upper_ref[:width, :] = dot_split(split(inverse0_ref[...]), g0)
        upper_ref[width:, :] = dot_split(split(cross_ref[...]), g0) + dot_split(split(inverse1_ref[...]), g1)

    slab = pl.ds(pl.multiple_of(layer * slab_rows, slab_rows), slab_rows)
    product = dot_split(split(panels_ref[0, slab, :]), split(upper_ref[:width, :]))
    product += dot_split(split(panels_ref[1, slab, :]), split(upper_ref[width:, :]))
    at_row = (lax.broadcasted_iota(jnp.int32, (slab_rows, tile), 0) + layer * slab_rows) // tile
    for j in range(tiles_per):
        keep = jnp.zeros((slab_rows, tile), jnp.int32)
        for i in range(tiles_per):
            keep = jnp.where(at_row == i, jnp.broadcast_to(keep_ref[i : i + 1, j : j + 1], keep.shape), keep)
        own = own_ref[pl.ds(j, slab_rows, tiles_per), :]
        at = slice(j * tile, (j + 1) * tile)
        own = jnp.where((row == 0) & (col == 0), row_ref[0, slab, at], own)
        schur_ref[pl.ds(j, slab_rows, tiles_per), :] = own - jnp.where(keep > 0, product[:, at], 0.0)


def trade(x, axis, k):
    return lax.ppermute(x, axis, [(i, i ^ k) for i in range(lax.axis_size(axis))])


def ask_layers(x):
    return [x] + [trade(x, "layer", k) for k in range(1, lax.axis_size("layer"))]


def in_order(parts, *late):
    layer = lax.axis_index("layer").astype(jnp.int32)
    parts = parts[:1] + [after(part, *late) for part in parts[1:]]
    ordered = []
    for t in range(len(parts)):
        held = parts[0]
        for k in range(1, len(parts)):
            held = jnp.where(layer ^ t == k, parts[k], held)
        ordered.append(held)
    return jnp.stack(ordered)


def strides(count, least):
    step = 1
    while 2 * step < count:
        step *= 2
    out = []
    while step >= least:
        out.append(step)
        step //= 2
    return out


def after(x, *others):
    return lax.optimization_barrier((x,) + others)[0]


def run(kernel, outs, ins, scratch=(), flops=0, name=None, source=pltpu.VMEM):
    vmem = pl.BlockSpec(memory_space=pltpu.VMEM)
    return pl.pallas_call(
        kernel,
        out_shape=tuple(jax.ShapeDtypeStruct(s, F32) for s in outs),
        in_specs=[pl.BlockSpec(memory_space=source)] * len(ins),
        out_specs=tuple(vmem for _ in outs),
        scratch_shapes=[pltpu.VMEM(s, F32) if isinstance(s, tuple) else s for s in scratch],
        compiler_params=pltpu.CompilerParams(vmem_limit_bytes=24 * 1024 * 1024),
        cost_estimate=pl.CostEstimate(flops=flops, bytes_accessed=10**6, transcendentals=0),
        name=name,
    )(*ins)


def on_device(partials, pattern):
    layers, rows, cols = (lax.axis_size(a) for a in AXES)
    layer, row, col = position()
    width = partials.shape[3]
    tiles_per = pattern.shape[2]
    tile = width // tiles_per
    slab_rows = width // layers
    piece_rows = slab_rows * tiles_per
    height = 2 * tile + SUB
    even_row, even_col = row % 2 == 0, col % 2 == 0
    square, big = (tile, tile), (width, width)

    mine, *sends = run(
        pack_kernel,
        ((height, tile),) * layers,
        (pltpu.with_memory_space_constraint(partials.reshape(width * tiles_per, tile), pltpu.HBM),),
        scratch=((width * tiles_per, tile), pltpu.SemaphoreType.DMA),
        name="k0",
        source=pltpu.HBM,
    )
    front = total([mine] + [trade(x, "layer", k + 1) for k, x in enumerate(sends)])
    piece = front[:piece_rows]

    keep = (pattern.reshape(tiles_per, tiles_per) > 0) | (row < 2) | (col < 2)
    keep = keep.astype(jnp.int32)
    fall = after(piece, keep)
    for s in strides(rows, 2):
        fall_from, fall_got = fall, trade(fall, "row", s)
        if s > 2:
            fall = jnp.where(row % (2 * s) >= s, fall_got, fall_from)

    lead = front
    for s in strides(cols, 2):
        lead = jnp.where(col % (2 * s) >= s, trade(lead, "col", s), lead)
    fall_got = after(fall_got, lead)
    lead = after(lead, fall_got)
    got = trade(lead, "col", 1)
    fall_from, fall_got = after(fall_from, lead), after(fall_got, lead)
    fall = jnp.where(row % 4 >= 2, fall_got, fall_from)
    fall_parts = ask_layers(fall)
    low, high = jnp.where(even_col, lead, got), jnp.where(even_col, got, lead)
    panels_in = jnp.stack([low[:piece_rows], high[:piece_rows]])
    high = high[:piece_rows]

    high = after(high, low)

    for s in strides(rows, 2):
        low = jnp.where(row % (2 * s) >= s, trade(low, "row", s), low)
    for s in strides(rows, 2):
        high_from, high_got = high, trade(high, "row", s)
        if s > 2:
            high = jnp.where(row % (2 * s) >= s, high_got, high_from)
    high = jnp.where(row % 4 >= 2, after(high_got, low), high_from)
    got = trade(low, "row", 1)
    packed = jnp.where(even_row, low, got)
    lead_parts = ask_layers(jnp.where(even_row, got[:piece_rows], high))
    packed = after(packed, high)

    small_lower, small_inverse, left0, rest0, *scales0 = run(
        first_kernel,
        (square,) * 6,
        (packed,),
        scratch=(square,),
        flops=5 * 10**9,
        name="k1",
    )
    rows_in = ask_layers(after(panels_in, rest0))
    lead = in_order(lead_parts, rest0)
    lead_other = trade(lead, "row", 1)
    lower0, inverse0 = run(
        second_kernel,
        (big, big),
        (small_lower, small_inverse, left0, after(rest0, lead), *scales0),
        scratch=(square,),
        flops=5 * 10**9,
        name="k2",
    )
    lead_other = after(lead_other, inverse0)
    corners, belows = jnp.where(even_row, lead_other, lead), jnp.where(even_row, lead, lead_other)
    fall = in_order(fall_parts, inverse0)
    fall_other = trade(fall, "row", 1)
    left1, lower1, inverse1, cross = run(
        third_kernel,
        (big, big, big, big),
        (corners, belows, inverse0),
        scratch=(big, big, square),
        flops=10**10,
        name="k3",
    )
    rows_in, fall_other = in_order(rows_in, cross), after(fall_other, cross)
    col0, col1 = jnp.where(even_row, fall, fall_other), jnp.where(even_row, fall_other, fall)
    schur, panels = run(
        final_kernel,
        ((piece_rows, tile), (2, width, width)),
        (keep, piece, packed, rows_in, col0, col1, lower0, inverse0, lower1, inverse1, left1, cross),
        scratch=((2 * width, width), (2, width, width)),
        flops=10**9,
        name="kf",
    )
    return (
        schur.reshape(1, 1, 1, slab_rows, 1, 1, width),
        panels.reshape(2, 1, 1, width, width),
    )


def solution(mesh):
    return jax.shard_map(
        on_device,
        mesh=mesh,
        in_specs=(
            P("layer", None, "row", None, None, "col", None),
            P(None, "row", None, None, "col", None),
        ),
        out_specs=(
            P(None, "row", "layer", None, None, "col", None),
            P(None, None, "row", None, None),
        ),
        check_vma=False,
    )
```

```python
import functools

import jax
import jax.numpy as jnp
from jax import lax
from jax.experimental import pallas as pl
from jax.experimental.pallas import tpu as pltpu
from jax.sharding import PartitionSpec as P

F32 = jnp.float32
SUB = 8
NT = (((1,), (1,)), ((), ()))
NN = (((1,), (0,)), ((), ()))


def dot(a, b, dims=NN):
    return lax.dot_general(
        a, b, dims, precision=lax.Precision.HIGHEST, preferred_element_type=F32
    )


AXES = ("layer", "row", "col")


def position():
    return tuple(lax.axis_index(a).astype(jnp.int32) for a in AXES)


def split(x):
    high = x.astype(jnp.bfloat16)
    return high, (x - high.astype(F32)).astype(jnp.bfloat16)


def dot_split(a, b, dims=NN):
    part = lambda x, y: lax.dot_general(x, y, dims, preferred_element_type=F32)
    return part(a[0], b[0]) + (part(a[0], b[1]) + part(a[1], b[0]))


def lane_splat(x, lane):
    return jnp.broadcast_to(x[:, lane : lane + 1], x.shape)


def row_splat(x, row):
    return jnp.broadcast_to(x[row : row + 1, :], x.shape)


def recip(x):
    return pl.reciprocal(x, approx=True)


def total(terms):
    while len(terms) > 1:
        terms = [terms[i] + terms[i + 1] for i in range(0, len(terms), 2)]
    return terms[0]


def factor_rows(rows):
    groups = len(rows)
    sub = lax.broadcasted_iota(jnp.int32, rows[0].shape, 0)
    lane = lax.broadcasted_iota(jnp.int32, rows[0].shape, 1)
    here = [sub == j for j in range(SUB)]
    unit = [jnp.where(h, 1.0, 0.0).astype(F32) for h in here]
    held = list(rows)
    out = []
    cols = [lane_splat(held[0], k) for k in range(SUB)]
    for b in range(groups):
        y = held[b]
        last = b + 1 == groups
        if not last:
            near = held[b + 1]
            side = [lane_splat(near, b * SUB + k) for k in range(SUB)]
            ahead = [lane_splat(near, (b + 1) * SUB + k) for k in range(SUB)]
        below = {g: [lane_splat(held[g], b * SUB + k) for k in range(SUB)] for g in range(b + 2, groups)}
        done = jnp.zeros_like(y)
        for j in range(0, SUB, 2):
            c0, c1 = cols[j], cols[j + 1]
            p, q, s = row_splat(c0, j), row_splat(c1, j), row_splat(c1, j + 1)
            r = recip(p * s - q * q)
            m0, m1 = c0 - unit[j], c1 - unit[j + 1]
            if j + 2 < SUB:
                v0, v1 = s * c0 - q * c1, p * c1 - q * c0
            for k in range(j + 2, SUB):
                n0, n1 = row_splat(v0, k), row_splat(v1, k)
                cols[k] = cols[k] - (m0 * n0 + m1 * n1) * r
                if not last:
                    side[k] = side[k] - (side[j] * n0 + side[j + 1] * n1) * r
            y0, y1 = row_splat(y, j), row_splat(y, j + 1)
            w0, w1 = (s * y0 - q * y1) * r, (p * y1 - q * y0) * r
            if not last:
                s0, s1 = side[j], side[j + 1]
                v0, v1 = s * s0 - q * s1, p * s1 - q * s0
                final = j + 2 == SUB
                if not final:
                    v0, v1 = v0 * r, v1 * r
                for k in range(SUB):
                    step = s0 * row_splat(v0, k) + s1 * row_splat(v1, k)
                    ahead[k] = ahead[k] - (step * r if final else step)
                near = near - (s0 * w0 + s1 * w1)
            y = y - (m0 * w0 + m1 * w1)
            root0 = lax.rsqrt(p)
            ratio = q * root0 * root0
            root1 = lax.rsqrt(s - q * ratio)
            done = jnp.where(here[j], y0 * root0, done)
            done = jnp.where(here[j + 1], (y1 - ratio * y0) * root1, done)
        out.append(jnp.where(lane >= sub + b * SUB, done, 0.0))
        if last:
            break
        held[b + 1] = near
        cols = ahead
        if below:
            yk = [row_splat(y, k) for k in range(SUB)]
        for g, c in below.items():
            held[g] = held[g] - total([c[k] * yk[k] for k in range(SUB)])
    return out


def tile_rows(tile):
    return [tile[g * SUB : (g + 1) * SUB, :] for g in range(tile.shape[0] // SUB)]


def scales(tile):
    at_row = lax.broadcasted_iota(jnp.int32, tile.shape, 0)
    at_col = lax.broadcasted_iota(jnp.int32, tile.shape, 1)
    diagonal = jnp.sum(jnp.where(at_row == at_col, tile, 0.0), axis=0, keepdims=True)
    along = jnp.broadcast_to(lax.rsqrt(diagonal), tile.shape)
    return along, along.T


def factor(tile, along, down, turned_ref, inverse_ref, work):
    half = tile.shape[0] // 2
    at_row = lax.broadcasted_iota(jnp.int32, (half, 2 * half), 0)
    at_col = lax.broadcasted_iota(jnp.int32, (half, 2 * half), 1)
    a = tile * along * down
    one = jnp.where(at_row[:, :half] == at_col[:, :half], 1.0, 0.0).astype(F32)
    beside = jnp.where(at_row + half == at_col, 1.0, 0.0).astype(F32)
    work[:half, :half] = jnp.zeros((half, half), F32)
    work[:half, half:] = a[half:, :half]
    work[half:, :half] = a[half:, half:]
    work[half:, half:] = one
    first = jnp.concatenate(factor_rows(tile_rows(jnp.where(at_col < half, a[:half], beside))), axis=0)
    under = dot(work[:half, :], first, NT)
    work[half:, :half] -= dot(under, under, NT)
    second = jnp.concatenate(factor_rows(tile_rows(work[half:, :])), axis=0)
    inverse0, inverse1 = first[:, half:], second[:, half:]
    inverse_ref[:half, :half] = inverse0 * along[:half, :half]
    inverse_ref[:half, half:] = jnp.zeros((half, half), F32)
    inverse_ref[half:, :half] = -dot(inverse1, dot(under, inverse0)) * along[half:, :half]
    inverse_ref[half:, half:] = inverse1 * along[half:, half:]
    across, up = recip(along), recip(down)
    turned_ref[:half, :half] = first[:, :half] * across[:half, :half]
    turned_ref[:half, half:] = jnp.zeros((half, half), F32)
    turned_ref[half:, :half] = under * up[half:, :half]
    turned_ref[half:, half:] = second[:, :half] * across[half:, half:]


def turn_back(from_ref, to_ref, tile):
    width = from_ref.shape[0]
    at_row = lax.broadcasted_iota(jnp.int32, (tile, tile), 0)
    at_col = lax.broadcasted_iota(jnp.int32, (tile, tile), 1)
    same = at_row // (tile // 2) == at_col // (tile // 2)
    to_ref[...] = from_ref[...]
    for t in range(0, width, tile):
        at = slice(t, t + tile)
        held = from_ref[at, at]
        to_ref[at, at] = jnp.where(same, held.T, held)


def pack_kernel(source_ref, mine_ref, *refs):
    *send_refs, linear_ref, arrived = refs
    load = pltpu.make_async_copy(source_ref, linear_ref, arrived)
    load.start()
    layer, row, col = position()
    first = (row == 0) & (col == 0)
    height, tile = mine_ref.shape
    load.wait()
    piece = linear_ref.shape[0] // (len(send_refs) + 1)

    @pl.when(first)
    def _():
        at_row = lax.broadcasted_iota(jnp.int32, (tile, tile), 0)
        at_col = lax.broadcasted_iota(jnp.int32, (tile, tile), 1)
        corner = linear_ref[pl.ds(2 * tile + 1, tile, 2), :]
        mixed = jnp.where(at_row >= at_col, linear_ref[pl.ds(0, tile, 2), :], corner)
        below = linear_ref[pl.ds(2 * tile, tile, 2), :]
        diagonal = jnp.sum(jnp.where(at_row == at_col, corner, 0.0), axis=0, keepdims=True)
        for ref in (mine_ref, *send_refs):
            ref[:tile, :] = mixed
            ref[tile : 2 * tile, :] = below
            ref[2 * tile :, :] = jnp.broadcast_to(diagonal, (height - 2 * tile, tile))

    @pl.when(jnp.logical_not(first))
    def _():
        for k, ref in enumerate((mine_ref, *send_refs)):
            start = pl.multiple_of((layer ^ k) * piece, piece)
            ref[:piece, :] = linear_ref[pl.ds(start, piece), :]
            ref[piece:, :] = jnp.zeros((height - piece, tile), F32)


def joined(pieces):
    slab = pieces[0].shape[0] // 2
    halves = [[piece[pl.ds(j, slab, 2), :] for j in range(2)] for piece in pieces]
    return jnp.concatenate([jnp.concatenate(half, axis=1) for half in halves], axis=0)


def symmetric(lower, keep):
    part = jnp.where(keep, lower, 0.0)
    at = lax.broadcasted_iota(jnp.int32, lower.shape, 0) == lax.broadcasted_iota(jnp.int32, lower.shape, 1)
    return part + jnp.where(at, 0.0, part).T


def open_packed(packed_ref):
    tile = packed_ref.shape[1]
    at_row = lax.broadcasted_iota(jnp.int32, (tile, tile), 0)
    at_col = lax.broadcasted_iota(jnp.int32, (tile, tile), 1)
    mixed = packed_ref[:tile, :]
    tile0 = symmetric(mixed, at_row >= at_col)
    upper1 = jnp.where(at_row < at_col, mixed, 0.0)
    diagonal = jnp.broadcast_to(packed_ref[2 * tile : 2 * tile + 1, :], (tile, tile))
    tile1 = upper1 + upper1.T + jnp.where(at_row == at_col, diagonal, 0.0)
    return tile0, packed_ref[tile : 2 * tile, :], tile1


def first_kernel(packed_ref, lower_ref, inverse_ref, left_ref, rest_ref, along_ref, down_ref, work):
    tile0, below, tile1 = open_packed(packed_ref)
    along, down = scales(tile1)
    along_ref[...] = along
    down_ref[...] = down
    factor(tile0, *scales(tile0), lower_ref, inverse_ref, work)
    left = dot(below, inverse_ref[...], NT)
    left_ref[...] = left
    rest_ref[...] = tile1 - dot(left, left, NT)


def second_kernel(
    lower0_ref, inverse0_ref, left_ref, rest_ref, along_ref, down_ref, lower_ref, inverse_ref, work
):
    tile = rest_ref.shape[0]
    zero = jnp.zeros((tile, tile), F32)
    first, second = slice(0, tile), slice(tile, 2 * tile)
    lower_ref[first, first] = lower0_ref[...]
    lower_ref[first, second] = zero
    lower_ref[second, first] = left_ref[...]
    inverse_ref[first, first] = inverse0_ref[...]
    inverse_ref[first, second] = zero
    factor(
        rest_ref[...], along_ref[...], down_ref[...], lower_ref.at[second, second], inverse_ref.at[second, second], work
    )
    inverse_ref[second, first] = -dot(inverse_ref[second, second], dot(left_ref[...], inverse0_ref[...]))


def third_kernel(
    corners_ref, belows_ref, inverse0_ref, left_ref, lower_ref, inverse_ref, cross_ref, work,
):
    tile = work.shape[0]
    first, second = slice(0, tile), slice(tile, 2 * tile)
    zero = jnp.zeros((tile, tile), F32)
    below = joined([belows_ref.at[t] for t in range(belows_ref.shape[0])])
    corner = joined([corners_ref.at[t] for t in range(corners_ref.shape[0])])
    scales0, scales1 = scales(corner[first, first]), scales(corner[second, second])
    top = dot(below[first, :], inverse0_ref[...], NT)
    factor(
        corner[first, first] - dot(top, top, NT),
        *scales0, lower_ref.at[first, first], inverse_ref.at[first, first], work,
    )
    bottom = dot(below[second, :], inverse0_ref[...], NT)
    left_ref[first, :] = top
    left_ref[second, :] = bottom
    ahead = corner[second, first] - dot(bottom, top, NT)
    rest = corner[second, second] - dot(bottom, bottom, NT)
    under = dot(ahead, inverse_ref[first, first], NT)
    lower_ref[first, second] = zero
    lower_ref[second, first] = under
    inverse_ref[first, second] = zero
    factor(
        rest - dot(under, under, NT),
        *scales1, lower_ref.at[second, second], inverse_ref.at[second, second], work,
    )
    bridge = dot_split(split(under), split(inverse_ref[first, first]))
    inverse_ref[second, first] = -dot_split(split(inverse_ref[second, second]), split(bridge))
    cross = dot_split(split(left_ref[...]), split(inverse0_ref[...]))
    cross_ref[...] = -dot_split(split(inverse_ref[...]), split(cross))


def final_kernel(
    keep_ref, own_ref, packed_ref, rows_ref, col0_ref, col1_ref,
    lower0_ref, inverse0_ref, lower1_ref, inverse1_ref, left_ref, cross_ref,
    schur_ref, panels_ref, upper_ref, row_ref,
):
    layer, row, col = position()
    width = upper_ref.shape[1]
    tiles_per = keep_ref.shape[0]
    tile = width // tiles_per
    slabs = rows_ref.shape[0]
    slab_rows = width // slabs

    @pl.when(row == 0)
    def _():
        turn_back(lower0_ref, panels_ref.at[0], tile)
        panels_ref[1] = jnp.zeros((width, width), F32)

    @pl.when(row == 1)
    def _():
        panels_ref[0] = left_ref[...]
        turn_back(lower1_ref, panels_ref.at[1], tile)

    @pl.when(row > 1)
    def _():
        f0, f1 = (split(joined([rows_ref.at[t, k] for t in range(slabs)])) for k in range(2))
        panels_ref[0] = dot_split(f0, split(inverse0_ref[...]), NT)
        panels_ref[1] = dot_split(f0, split(cross_ref[...]), NT) + dot_split(f1, split(inverse1_ref[...]), NT)

    @pl.when(col == 0)
    def _():
        upper_ref[...] = jnp.zeros(upper_ref.shape, F32)

    @pl.when((row == 0) & (col == 0))
    def _():
        tile0, below, tile1 = open_packed(packed_ref)
        row_ref[0, :tile, :tile] = tile0
        row_ref[0, tile:, :tile] = below
        row_ref[0, :tile, tile:] = below.T
        row_ref[0, tile:, tile:] = tile1

    @pl.when(col == 1)
    def _():
        upper_ref[:width, :] = left_ref[...].T
        upper_ref[width:, :] = jnp.zeros((width, width), F32)

    @pl.when(col > 1)
    def _():
        g0, g1 = (split(joined([ref.at[t] for t in range(slabs)])) for ref in (col0_ref, col1_ref))
        upper_ref[:width, :] = dot_split(split(inverse0_ref[...]), g0)
        upper_ref[width:, :] = dot_split(split(cross_ref[...]), g0) + dot_split(split(inverse1_ref[...]), g1)

    slab = pl.ds(pl.multiple_of(layer * slab_rows, slab_rows), slab_rows)
    product = dot_split(split(panels_ref[0, slab, :]), split(upper_ref[:width, :]))
    product += dot_split(split(panels_ref[1, slab, :]), split(upper_ref[width:, :]))
    at_row = (lax.broadcasted_iota(jnp.int32, (slab_rows, tile), 0) + layer * slab_rows) // tile
    for j in range(tiles_per):
        keep = jnp.zeros((slab_rows, tile), jnp.int32)
        for i in range(tiles_per):
            keep = jnp.where(at_row == i, jnp.broadcast_to(keep_ref[i : i + 1, j : j + 1], keep.shape), keep)
        own = own_ref[pl.ds(j, slab_rows, tiles_per), :]
        at = slice(j * tile, (j + 1) * tile)
        own = jnp.where((row == 0) & (col == 0), row_ref[0, slab, at], own)
        schur_ref[pl.ds(j, slab_rows, tiles_per), :] = own - jnp.where(keep > 0, product[:, at], 0.0)


def trade(x, axis, k):
    return lax.ppermute(x, axis, [(i, i ^ k) for i in range(lax.axis_size(axis))])


def ask_layers(x):
    return [x] + [trade(x, "layer", k) for k in range(1, lax.axis_size("layer"))]


def in_order(parts, *late):
    layer = lax.axis_index("layer").astype(jnp.int32)
    parts = parts[:1] + [after(part, *late) for part in parts[1:]]
    ordered = []
    for t in range(len(parts)):
        held = parts[0]
        for k in range(1, len(parts)):
            held = jnp.where(layer ^ t == k, parts[k], held)
        ordered.append(held)
    return jnp.stack(ordered)


def strides(count, least):
    step = 1
    while 2 * step < count:
        step *= 2
    out = []
    while step >= least:
        out.append(step)
        step //= 2
    return out


def after(x, *others):
    return lax.optimization_barrier((x,) + others)[0]


def run(kernel, outs, ins, scratch=(), flops=0, name=None, source=pltpu.VMEM):
    vmem = pl.BlockSpec(memory_space=pltpu.VMEM)
    return pl.pallas_call(
        kernel,
        out_shape=tuple(jax.ShapeDtypeStruct(s, F32) for s in outs),
        in_specs=[pl.BlockSpec(memory_space=source)] * len(ins),
        out_specs=tuple(vmem for _ in outs),
        scratch_shapes=[pltpu.VMEM(s, F32) if isinstance(s, tuple) else s for s in scratch],
        compiler_params=pltpu.CompilerParams(vmem_limit_bytes=24 * 1024 * 1024),
        cost_estimate=pl.CostEstimate(flops=flops, bytes_accessed=10**6, transcendentals=0),
        name=name,
    )(*ins)


def on_device(partials, pattern):
    layers, rows, cols = (lax.axis_size(a) for a in AXES)
    layer, row, col = position()
    width = partials.shape[3]
    tiles_per = pattern.shape[2]
    tile = width // tiles_per
    slab_rows = width // layers
    piece_rows = slab_rows * tiles_per
    height = 2 * tile + SUB
    even_row, even_col = row % 2 == 0, col % 2 == 0
    square, big = (tile, tile), (width, width)

    mine, *sends = run(
        pack_kernel,
        ((height, tile),) * layers,
        (pltpu.with_memory_space_constraint(partials.reshape(width * tiles_per, tile), pltpu.HBM),),
        scratch=((width * tiles_per, tile), pltpu.SemaphoreType.DMA),
        name="k0",
        source=pltpu.HBM,
    )
    front = total([mine] + [trade(x, "layer", k + 1) for k, x in enumerate(sends)])
    piece = front[:piece_rows]

    keep = (pattern.reshape(tiles_per, tiles_per) > 0) | (row < 2) | (col < 2)
    keep = keep.astype(jnp.int32)
    fall = after(piece, keep)
    for s in strides(rows, 2):
        fall_from, fall_got = fall, trade(fall, "row", s)
        if s > 2:
            fall = jnp.where(row % (2 * s) >= s, fall_got, fall_from)

    lead = front
    for s in strides(cols, 2):
        lead = jnp.where(col % (2 * s) >= s, trade(lead, "col", s), lead)
    fall_got = after(fall_got, lead)
    lead = after(lead, fall_got)
    got = trade(lead, "col", 1)
    fall_from, fall_got = after(fall_from, lead), after(fall_got, lead)
    fall = jnp.where(row % 4 >= 2, fall_got, fall_from)
    fall_parts = ask_layers(fall)
    low, high = jnp.where(even_col, lead, got), jnp.where(even_col, got, lead)
    panels_in = jnp.stack([low[:piece_rows], high[:piece_rows]])
    high = high[:piece_rows]

    high = after(high, low)

    for s in strides(rows, 2):
        low = jnp.where(row % (2 * s) >= s, trade(low, "row", s), low)
    for s in strides(rows, 2):
        high_from, high_got = high, trade(high, "row", s)
        if s > 2:
            high = jnp.where(row % (2 * s) >= s, high_got, high_from)
    high = jnp.where(row % 4 >= 2, after(high_got, low), high_from)
    got = trade(low, "row", 1)
    packed = jnp.where(even_row, low, got)
    lead_parts = ask_layers(jnp.where(even_row, got[:piece_rows], high))
    packed = after(packed, high)

    small_lower, small_inverse, left0, rest0, *scales0 = run(
        first_kernel,
        (square,) * 6,
        (packed,),
        scratch=(square,),
        flops=5 * 10**9,
        name="k1",
    )
    rows_in = ask_layers(after(panels_in, rest0))
    lead = in_order(lead_parts, rest0)
    lead_other = trade(lead, "row", 1)
    lower0, inverse0 = run(
        second_kernel,
        (big, big),
        (small_lower, small_inverse, left0, after(rest0, lead), *scales0),
        scratch=(square,),
        flops=5 * 10**9,
        name="k2",
    )
    lead_other = after(lead_other, inverse0)
    corners, belows = jnp.where(even_row, lead_other, lead), jnp.where(even_row, lead, lead_other)
    fall = in_order(fall_parts, inverse0)
    fall_other = trade(fall, "row", 1)
    left1, lower1, inverse1, cross = run(
        third_kernel,
        (big, big, big, big),
        (corners, belows, inverse0),
        scratch=(square,),
        flops=10**10,
        name="k3",
    )
    rows_in, fall_other = in_order(rows_in, cross), after(fall_other, cross)
    col0, col1 = jnp.where(even_row, fall, fall_other), jnp.where(even_row, fall_other, fall)
    schur, panels = run(
        final_kernel,
        ((piece_rows, tile), (2, width, width)),
        (keep, piece, packed, rows_in, col0, col1, lower0, inverse0, lower1, inverse1, left1, cross),
        scratch=((2 * width, width), (2, width, width)),
        flops=10**9,
        name="kf",
    )
    return (
        schur.reshape(1, 1, 1, slab_rows, 1, 1, width),
        panels.reshape(2, 1, 1, width, width),
    )


def solution(mesh):
    return jax.shard_map(
        on_device,
        mesh=mesh,
        in_specs=(
            P("layer", None, "row", None, None, "col", None),
            P(None, "row", None, None, "col", None),
        ),
        out_specs=(
            P(None, "row", "layer", None, None, "col", None),
            P(None, None, "row", None, None),
        ),
        check_vma=False,
    )
```

```python
import functools

import jax
import jax.numpy as jnp
from jax import lax
from jax.experimental import pallas as pl
from jax.experimental.pallas import tpu as pltpu
from jax.sharding import PartitionSpec as P

F32 = jnp.float32
SUB = 8
NT = (((1,), (1,)), ((), ()))
NN = (((1,), (0,)), ((), ()))


def dot(a, b, dims=NN):
    return lax.dot_general(
        a, b, dims, precision=lax.Precision.HIGHEST, preferred_element_type=F32
    )


AXES = ("layer", "row", "col")


def position():
    return tuple(lax.axis_index(a).astype(jnp.int32) for a in AXES)


def split(x):
    high = x.astype(jnp.bfloat16)
    return high, (x - high.astype(F32)).astype(jnp.bfloat16)


def dot_split(a, b, dims=NN):
    part = lambda x, y: lax.dot_general(x, y, dims, preferred_element_type=F32)
    return part(a[0], b[0]) + (part(a[0], b[1]) + part(a[1], b[0]))


def lane_splat(x, lane):
    return jnp.broadcast_to(x[:, lane : lane + 1], x.shape)


def row_splat(x, row):
    return jnp.broadcast_to(x[row : row + 1, :], x.shape)


def recip(x):
    return pl.reciprocal(x, approx=True)


def total(terms):
    while len(terms) > 1:
        terms = [terms[i] + terms[i + 1] for i in range(0, len(terms), 2)]
    return terms[0]


def factor_rows(rows):
    groups = len(rows)
    sub = lax.broadcasted_iota(jnp.int32, rows[0].shape, 0)
    lane = lax.broadcasted_iota(jnp.int32, rows[0].shape, 1)
    here = [sub == j for j in range(SUB)]
    unit = [jnp.where(h, 1.0, 0.0).astype(F32) for h in here]
    held = list(rows)
    out = []
    cols = [lane_splat(held[0], k) for k in range(SUB)]
    for b in range(groups):
        y = held[b]
        last = b + 1 == groups
        if not last:
            near = held[b + 1]
            side = [lane_splat(near, b * SUB + k) for k in range(SUB)]
            ahead = [lane_splat(near, (b + 1) * SUB + k) for k in range(SUB)]
        below = {g: [lane_splat(held[g], b * SUB + k) for k in range(SUB)] for g in range(b + 2, groups)}
        done = jnp.zeros_like(y)
        for j in range(0, SUB, 2):
            c0, c1 = cols[j], cols[j + 1]
            p, q, s = row_splat(c0, j), row_splat(c1, j), row_splat(c1, j + 1)
            r = recip(p * s - q * q)
            m0, m1 = c0 - unit[j], c1 - unit[j + 1]
            if j + 2 < SUB:
                v0, v1 = s * c0 - q * c1, p * c1 - q * c0
            for k in range(j + 2, SUB):
                n0, n1 = row_splat(v0, k), row_splat(v1, k)
                cols[k] = cols[k] - (m0 * n0 + m1 * n1) * r
                if not last:
                    side[k] = side[k] - (side[j] * n0 + side[j + 1] * n1) * r
            y0, y1 = row_splat(y, j), row_splat(y, j + 1)
            w0, w1 = (s * y0 - q * y1) * r, (p * y1 - q * y0) * r
            if not last:
                s0, s1 = side[j], side[j + 1]
                v0, v1 = s * s0 - q * s1, p * s1 - q * s0
                final = j + 2 == SUB
                if not final:
                    v0, v1 = v0 * r, v1 * r
                for k in range(SUB):
                    step = s0 * row_splat(v0, k) + s1 * row_splat(v1, k)
                    ahead[k] = ahead[k] - (step * r if final else step)
                near = near - (s0 * w0 + s1 * w1)
            y = y - (m0 * w0 + m1 * w1)
            root0 = lax.rsqrt(p)
            ratio = q * root0 * root0
            root1 = lax.rsqrt(s - q * ratio)
            done = jnp.where(here[j], y0 * root0, done)
            done = jnp.where(here[j + 1], (y1 - ratio * y0) * root1, done)
        out.append(jnp.where(lane >= sub + b * SUB, done, 0.0))
        if last:
            break
        held[b + 1] = near
        cols = ahead
        if below:
            yk = [row_splat(y, k) for k in range(SUB)]
        for g, c in below.items():
            held[g] = held[g] - total([c[k] * yk[k] for k in range(SUB)])
    return out


def tile_rows(tile):
    return [tile[g * SUB : (g + 1) * SUB, :] for g in range(tile.shape[0] // SUB)]


def scales(tile):
    at_row = lax.broadcasted_iota(jnp.int32, tile.shape, 0)
    at_col = lax.broadcasted_iota(jnp.int32, tile.shape, 1)
    diagonal = jnp.sum(jnp.where(at_row == at_col, tile, 0.0), axis=0, keepdims=True)
    along = jnp.broadcast_to(lax.rsqrt(diagonal), tile.shape)
    return along, along.T


def factor(tile, along, down, turned_ref, inverse_ref, work):
    half = tile.shape[0] // 2
    at_row = lax.broadcasted_iota(jnp.int32, (half, 2 * half), 0)
    at_col = lax.broadcasted_iota(jnp.int32, (half, 2 * half), 1)
    a = tile * along * down
    one = jnp.where(at_row[:, :half] == at_col[:, :half], 1.0, 0.0).astype(F32)
    beside = jnp.where(at_row + half == at_col, 1.0, 0.0).astype(F32)
    work[:half, :half] = jnp.zeros((half, half), F32)
    work[:half, half:] = a[half:, :half]
    work[half:, :half] = a[half:, half:]
    work[half:, half:] = one
    first = jnp.concatenate(factor_rows(tile_rows(jnp.where(at_col < half, a[:half], beside))), axis=0)
    under = dot(work[:half, :], first, NT)
    work[half:, :half] -= dot(under, under, NT)
    second = jnp.concatenate(factor_rows(tile_rows(work[half:, :])), axis=0)
    inverse0, inverse1 = first[:, half:], second[:, half:]
    inverse_ref[:half, :half] = inverse0 * along[:half, :half]
    inverse_ref[:half, half:] = jnp.zeros((half, half), F32)
    inverse_ref[half:, :half] = -dot(inverse1, dot(under, inverse0)) * along[half:, :half]
    inverse_ref[half:, half:] = inverse1 * along[half:, half:]
    across, up = recip(along), recip(down)
    turned_ref[:half, :half] = first[:, :half] * across[:half, :half]
    turned_ref[:half, half:] = jnp.zeros((half, half), F32)
    turned_ref[half:, :half] = under * up[half:, :half]
    turned_ref[half:, half:] = second[:, :half] * across[half:, half:]


def turn_back(from_ref, to_ref, tile):
    width = from_ref.shape[0]
    at_row = lax.broadcasted_iota(jnp.int32, (tile, tile), 0)
    at_col = lax.broadcasted_iota(jnp.int32, (tile, tile), 1)
    same = at_row // (tile // 2) == at_col // (tile // 2)
    to_ref[...] = from_ref[...]
    for t in range(0, width, tile):
        at = slice(t, t + tile)
        held = from_ref[at, at]
        to_ref[at, at] = jnp.where(same, held.T, held)


def pack_kernel(source_ref, mine_ref, *refs):
    *send_refs, linear_ref, arrived = refs
    load = pltpu.make_async_copy(source_ref, linear_ref, arrived)
    load.start()
    layer, row, col = position()
    first = (row == 0) & (col == 0)
    height, tile = mine_ref.shape
    load.wait()
    piece = linear_ref.shape[0] // (len(send_refs) + 1)

    @pl.when(first)
    def _():
        at_row = lax.broadcasted_iota(jnp.int32, (tile, tile), 0)
        at_col = lax.broadcasted_iota(jnp.int32, (tile, tile), 1)
        corner = linear_ref[pl.ds(2 * tile + 1, tile, 2), :]
        mixed = jnp.where(at_row >= at_col, linear_ref[pl.ds(0, tile, 2), :], corner)
        below = linear_ref[pl.ds(2 * tile, tile, 2), :]
        diagonal = jnp.sum(jnp.where(at_row == at_col, corner, 0.0), axis=0, keepdims=True)
        for ref in (mine_ref, *send_refs):
            ref[:tile, :] = mixed
            ref[tile : 2 * tile, :] = below
            ref[2 * tile :, :] = jnp.broadcast_to(diagonal, (height - 2 * tile, tile))

    @pl.when(jnp.logical_not(first))
    def _():
        for k, ref in enumerate((mine_ref, *send_refs)):
            start = pl.multiple_of((layer ^ k) * piece, piece)
            ref[:piece, :] = linear_ref[pl.ds(start, piece), :]
            ref[piece:, :] = jnp.zeros((height - piece, tile), F32)


def unpack(pieces, to_ref):
    tile = pieces[0].shape[1]
    slab = pieces[0].shape[0] // 2
    for t, piece in enumerate(pieces):
        to_ref[t * slab : (t + 1) * slab, :tile] = piece[pl.ds(0, slab, 2), :]
        to_ref[t * slab : (t + 1) * slab, tile:] = piece[pl.ds(1, slab, 2), :]


def symmetric(lower, keep):
    part = jnp.where(keep, lower, 0.0)
    at = lax.broadcasted_iota(jnp.int32, lower.shape, 0) == lax.broadcasted_iota(jnp.int32, lower.shape, 1)
    return part + jnp.where(at, 0.0, part).T


def open_packed(packed_ref):
    tile = packed_ref.shape[1]
    at_row = lax.broadcasted_iota(jnp.int32, (tile, tile), 0)
    at_col = lax.broadcasted_iota(jnp.int32, (tile, tile), 1)
    mixed = packed_ref[:tile, :]
    tile0 = symmetric(mixed, at_row >= at_col)
    upper1 = jnp.where(at_row < at_col, mixed, 0.0)
    diagonal = jnp.broadcast_to(packed_ref[2 * tile : 2 * tile + 1, :], (tile, tile))
    tile1 = upper1 + upper1.T + jnp.where(at_row == at_col, diagonal, 0.0)
    return tile0, packed_ref[tile : 2 * tile, :], tile1


def first_kernel(packed_ref, lower_ref, inverse_ref, left_ref, rest_ref, along_ref, down_ref, work):
    tile0, below, tile1 = open_packed(packed_ref)
    along, down = scales(tile1)
    along_ref[...] = along
    down_ref[...] = down
    factor(tile0, *scales(tile0), lower_ref, inverse_ref, work)
    left = dot(below, inverse_ref[...], NT)
    left_ref[...] = left
    rest_ref[...] = tile1 - dot(left, left, NT)


def second_kernel(
    lower0_ref, inverse0_ref, left_ref, rest_ref, along_ref, down_ref, lower_ref, inverse_ref, work
):
    tile = rest_ref.shape[0]
    zero = jnp.zeros((tile, tile), F32)
    first, second = slice(0, tile), slice(tile, 2 * tile)
    lower_ref[first, first] = lower0_ref[...]
    lower_ref[first, second] = zero
    lower_ref[second, first] = left_ref[...]
    inverse_ref[first, first] = inverse0_ref[...]
    inverse_ref[first, second] = zero
    factor(
        rest_ref[...], along_ref[...], down_ref[...], lower_ref.at[second, second], inverse_ref.at[second, second], work
    )
    inverse_ref[second, first] = -dot(inverse_ref[second, second], dot(left_ref[...], inverse0_ref[...]))


def third_kernel(
    corners_ref, belows_ref, inverse0_ref, left_ref, lower_ref, inverse_ref, cross_ref, corner_ref, below_ref, work,
):
    tile = work.shape[0]
    first, second = slice(0, tile), slice(tile, 2 * tile)
    zero = jnp.zeros((tile, tile), F32)
    unpack([belows_ref.at[t] for t in range(belows_ref.shape[0])], below_ref)
    unpack([corners_ref.at[t] for t in range(corners_ref.shape[0])], corner_ref)
    scales0, scales1 = scales(corner_ref[first, first]), scales(corner_ref[second, second])
    top = dot(below_ref[first, :], inverse0_ref[...], NT)
    factor(
        corner_ref[first, first] - dot(top, top, NT),
        *scales0, lower_ref.at[first, first], inverse_ref.at[first, first], work,
    )
    bottom = dot(below_ref[second, :], inverse0_ref[...], NT)
    left_ref[first, :] = top
    left_ref[second, :] = bottom
    ahead = corner_ref[second, first] - dot(bottom, top, NT)
    rest = corner_ref[second, second] - dot(bottom, bottom, NT)
    under = dot(ahead, inverse_ref[first, first], NT)
    lower_ref[first, second] = zero
    lower_ref[second, first] = under
    inverse_ref[first, second] = zero
    factor(
        rest - dot(under, under, NT),
        *scales1, lower_ref.at[second, second], inverse_ref.at[second, second], work,
    )
    corner = dot_split(split(under), split(inverse_ref[first, first]))
    inverse_ref[second, first] = -dot_split(split(inverse_ref[second, second]), split(corner))
    cross = dot_split(split(left_ref[...]), split(inverse0_ref[...]))
    cross_ref[...] = -dot_split(split(inverse_ref[...]), split(cross))


def final_kernel(
    keep_ref, own_ref, packed_ref, rows_ref, col0_ref, col1_ref,
    lower0_ref, inverse0_ref, lower1_ref, inverse1_ref, left_ref, cross_ref,
    schur_ref, panels_ref, upper_ref, row_ref,
):
    layer, row, col = position()
    width = upper_ref.shape[1]
    tiles_per = keep_ref.shape[0]
    tile = width // tiles_per
    slabs = rows_ref.shape[0]
    slab_rows = width // slabs

    @pl.when(row == 0)
    def _():
        turn_back(lower0_ref, panels_ref.at[0], tile)
        panels_ref[1] = jnp.zeros((width, width), F32)

    @pl.when(row == 1)
    def _():
        panels_ref[0] = left_ref[...]
        turn_back(lower1_ref, panels_ref.at[1], tile)

    @pl.when(row > 1)
    def _():
        for k in range(2):
            unpack([rows_ref.at[t, k] for t in range(slabs)], row_ref.at[k])
        f0, f1 = split(row_ref[0]), split(row_ref[1])
        panels_ref[0] = dot_split(f0, split(inverse0_ref[...]), NT)
        panels_ref[1] = dot_split(f0, split(cross_ref[...]), NT) + dot_split(f1, split(inverse1_ref[...]), NT)

    @pl.when(col == 0)
    def _():
        upper_ref[...] = jnp.zeros(upper_ref.shape, F32)

    @pl.when((row == 0) & (col == 0))
    def _():
        tile0, below, tile1 = open_packed(packed_ref)
        row_ref[0, :tile, :tile] = tile0
        row_ref[0, tile:, :tile] = below
        row_ref[0, :tile, tile:] = below.T
        row_ref[0, tile:, tile:] = tile1

    @pl.when(col == 1)
    def _():
        upper_ref[:width, :] = left_ref[...].T
        upper_ref[width:, :] = jnp.zeros((width, width), F32)

    @pl.when(col > 1)
    def _():
        for k, ref in enumerate((col0_ref, col1_ref)):
            unpack([ref.at[t] for t in range(slabs)], row_ref.at[k])
        g0, g1 = split(row_ref[0]), split(row_ref[1])
        upper_ref[:width, :] = dot_split(split(inverse0_ref[...]), g0)
        upper_ref[width:, :] = dot_split(split(cross_ref[...]), g0) + dot_split(split(inverse1_ref[...]), g1)

    slab = pl.ds(pl.multiple_of(layer * slab_rows, slab_rows), slab_rows)

    @pl.when(col == 0)
    def _():
        row_ref[1, :slab_rows, :] = jnp.zeros((slab_rows, width), F32)

    @pl.when(col > 0)
    def _():
        first = dot_split(split(panels_ref[0, slab, :]), split(upper_ref[:width, :]))
        second = dot_split(split(panels_ref[1, slab, :]), split(upper_ref[width:, :]))
        row_ref[1, :slab_rows, :] = first + second

    product = row_ref[1, :slab_rows, :]
    at_row = (lax.broadcasted_iota(jnp.int32, (slab_rows, tile), 0) + layer * slab_rows) // tile
    for j in range(tiles_per):
        keep = jnp.zeros((slab_rows, tile), jnp.int32)
        for i in range(tiles_per):
            keep = jnp.where(at_row == i, jnp.broadcast_to(keep_ref[i : i + 1, j : j + 1], keep.shape), keep)
        own = own_ref[pl.ds(j, slab_rows, tiles_per), :]
        at = slice(j * tile, (j + 1) * tile)
        own = jnp.where((row == 0) & (col == 0), row_ref[0, slab, at], own)
        schur_ref[pl.ds(j, slab_rows, tiles_per), :] = own - jnp.where(keep > 0, product[:, at], 0.0)


def trade(x, axis, k):
    return lax.ppermute(x, axis, [(i, i ^ k) for i in range(lax.axis_size(axis))])


def ask_layers(x):
    return [x] + [trade(x, "layer", k) for k in range(1, lax.axis_size("layer"))]


def in_order(parts, *late):
    layer = lax.axis_index("layer").astype(jnp.int32)
    parts = parts[:1] + [after(part, *late) for part in parts[1:]]
    ordered = []
    for t in range(len(parts)):
        held = parts[0]
        for k in range(1, len(parts)):
            held = jnp.where(layer ^ t == k, parts[k], held)
        ordered.append(held)
    return jnp.stack(ordered)


def strides(count, least):
    step = 1
    while 2 * step < count:
        step *= 2
    out = []
    while step >= least:
        out.append(step)
        step //= 2
    return out


def after(x, *others):
    return lax.optimization_barrier((x,) + others)[0]


def run(kernel, outs, ins, scratch=(), flops=0, name=None, source=pltpu.VMEM):
    vmem = pl.BlockSpec(memory_space=pltpu.VMEM)
    return pl.pallas_call(
        kernel,
        out_shape=tuple(jax.ShapeDtypeStruct(s, F32) for s in outs),
        in_specs=[pl.BlockSpec(memory_space=source)] * len(ins),
        out_specs=tuple(vmem for _ in outs),
        scratch_shapes=[pltpu.VMEM(s, F32) if isinstance(s, tuple) else s for s in scratch],
        compiler_params=pltpu.CompilerParams(vmem_limit_bytes=24 * 1024 * 1024),
        cost_estimate=pl.CostEstimate(flops=flops, bytes_accessed=10**6, transcendentals=0),
        name=name,
    )(*ins)


def on_device(partials, pattern):
    layers, rows, cols = (lax.axis_size(a) for a in AXES)
    layer, row, col = position()
    width = partials.shape[3]
    tiles_per = pattern.shape[2]
    tile = width // tiles_per
    slab_rows = width // layers
    piece_rows = slab_rows * tiles_per
    height = 2 * tile + SUB
    even_row, even_col = row % 2 == 0, col % 2 == 0
    square, big = (tile, tile), (width, width)

    mine, *sends = run(
        pack_kernel,
        ((height, tile),) * layers,
        (pltpu.with_memory_space_constraint(partials.reshape(width * tiles_per, tile), pltpu.HBM),),
        scratch=((width * tiles_per, tile), pltpu.SemaphoreType.DMA),
        name="k0",
        source=pltpu.HBM,
    )
    front = total([mine] + [trade(x, "layer", k + 1) for k, x in enumerate(sends)])
    piece = front[:piece_rows]

    keep = (pattern.reshape(tiles_per, tiles_per) > 0) | (row < 2) | (col < 2)
    keep = keep.astype(jnp.int32)
    fall = after(piece, keep)
    for s in strides(rows, 2):
        fall_from, fall_got = fall, trade(fall, "row", s)
        if s > 2:
            fall = jnp.where(row % (2 * s) >= s, fall_got, fall_from)

    lead = front
    for s in strides(cols, 2):
        lead = jnp.where(col % (2 * s) >= s, trade(lead, "col", s), lead)
    fall_got = after(fall_got, lead)
    lead = after(lead, fall_got)
    got = trade(lead, "col", 1)
    fall_from, fall_got = after(fall_from, lead), after(fall_got, lead)
    fall = jnp.where(row % 4 >= 2, fall_got, fall_from)
    fall_parts = ask_layers(fall)
    low, high = jnp.where(even_col, lead, got), jnp.where(even_col, got, lead)
    panels_in = jnp.stack([low[:piece_rows], high[:piece_rows]])
    high = high[:piece_rows]

    high = after(high, low)

    for s in strides(rows, 2):
        low = jnp.where(row % (2 * s) >= s, trade(low, "row", s), low)
    for s in strides(rows, 2):
        high_from, high_got = high, trade(high, "row", s)
        if s > 2:
            high = jnp.where(row % (2 * s) >= s, high_got, high_from)
    high = jnp.where(row % 4 >= 2, after(high_got, low), high_from)
    got = trade(low, "row", 1)
    packed = jnp.where(even_row, low, got)
    lead_parts = ask_layers(jnp.where(even_row, got[:piece_rows], high))
    packed = after(packed, high)

    small_lower, small_inverse, left0, rest0, *scales0 = run(
        first_kernel,
        (square,) * 6,
        (packed,),
        scratch=(square,),
        flops=5 * 10**9,
        name="k1",
    )
    rows_in = ask_layers(after(panels_in, rest0))
    lead = in_order(lead_parts, rest0)
    lead_other = trade(lead, "row", 1)
    lower0, inverse0 = run(
        second_kernel,
        (big, big),
        (small_lower, small_inverse, left0, after(rest0, lead), *scales0),
        scratch=(square,),
        flops=5 * 10**9,
        name="k2",
    )
    lead_other = after(lead_other, inverse0)
    corners, belows = jnp.where(even_row, lead_other, lead), jnp.where(even_row, lead, lead_other)
    fall = in_order(fall_parts, inverse0)
    fall_other = trade(fall, "row", 1)
    left1, lower1, inverse1, cross = run(
        third_kernel,
        (big, big, big, big),
        (corners, belows, inverse0),
        scratch=(big, big, square),
        flops=10**10,
        name="k3",
    )
    rows_in, fall_other = in_order(rows_in, cross), after(fall_other, cross)
    col0, col1 = jnp.where(even_row, fall, fall_other), jnp.where(even_row, fall_other, fall)
    schur, panels = run(
        final_kernel,
        ((piece_rows, tile), (2, width, width)),
        (keep, piece, packed, rows_in, col0, col1, lower0, inverse0, lower1, inverse1, left1, cross),
        scratch=((2 * width, width), (2, width, width)),
        flops=10**9,
        name="kf",
    )
    return (
        schur.reshape(1, 1, 1, slab_rows, 1, 1, width),
        panels.reshape(2, 1, 1, width, width),
    )


def solution(mesh):
    return jax.shard_map(
        on_device,
        mesh=mesh,
        in_specs=(
            P("layer", None, "row", None, None, "col", None),
            P(None, "row", None, None, "col", None),
        ),
        out_specs=(
            P(None, "row", "layer", None, None, "col", None),
            P(None, None, "row", None, None),
        ),
        check_vma=False,
    )
```
